256 devices in a mesh: gx: 8 (over y, z_hi), gy: 4 (over x), gz: 8 (over z_lo, core).
Axes of the slice: x: 4, y: 4, z: 8 (z_hi: 2, z_lo: 4; z = z_hi * 4 + z_lo), core: 2. Of those that a mesh axis runs over, the one named last changes fastest.
Arguments:
- base_flow: float32 [3, 64, 128, 1024], P(None, 'gx', 'gy', 'gz'), may hold values from -4 to 4
- adjoint_velocity: float32 [3, 64, 128, 1024], P(None, 'gx', 'gy', 'gz'), may hold values from -3.6 to 3.6
- penalty: float32 [64, 128, 1024], P('gx', 'gy', 'gz'), may hold values from 4 to 64
Outputs:
- projected: float32 [3, 64, 128, 1024], P(None, 'gx', 'gy', 'gz')
- pressure: float32 [64, 128, 1024], P('gx', 'gy', 'gz')
The draws below stay inside these ranges and needn't reach their ends.
All inputs are finite; a program needn't handle non-finite values.
Results may differ from the reference program's by a relative error of at most 0.00013.
Values sent between devices are 32-bit elements; how exact they have to be, the bound alone decides.
A program may use at most 64 MiB of HBM per device.

```python
import math
import jax
import jax.numpy as jnp
import numpy as np
from jax import lax

ITERS = 3
XP = 64
YP = 128
ZP = 1024


def draw_adjoint_velocity(key, part):
    key = jax.random.fold_in(key, 11)
    extent_all = (3, XP, YP, ZP)
    rise_x = jnp.arange(XP, dtype=jnp.float32) / XP
    rise_y = jnp.arange(YP, dtype=jnp.float32) / YP
    rise_z = jnp.arange(ZP, dtype=jnp.float32) / ZP
    exponent = rise_x[:, None, None] + rise_y[None, :, None] + rise_z[None, None, :]
    envelope = jnp.exp(1.0986123 * exponent) / 9.0
    values = 0.3 * envelope * jnp.clip(jax.random.normal(key, extent_all, jnp.float32), -4.0, 4.0)
    return values


def block_levels(own_key, dims, cuts, least, top_value):
    def one(dim, blocks):
        draws = jax.random.uniform(jax.random.fold_in(jax.random.fold_in(own_key, 6), dim), (blocks,), jnp.float32, least / len(cuts), top_value / len(cuts))
        return jnp.repeat(jnp.exp(draws), dims[dim] // blocks).reshape((-1,) + (1,) * (len(dims) - dim - 1))

    level = one(*cuts[0])
    for cut in cuts[1:]:
        level = level * one(*cut)
    return level


def centred(own_key, shape, deviation, most, pieces=(), kind=jnp.bfloat16):
    drawn = jax.random.normal(own_key, shape, jnp.float32) * deviation
    if len(pieces) > 0:
        drawn = block_levels(own_key, shape, pieces, -0.22, 0.18) * drawn
    return jnp.clip(drawn, min=-most, max=most).astype(kind)


def setup_inputs(seed: int = 0) -> dict:
    keys = jax.random.split(jax.random.key(seed), 4)
    return {
        "base_flow": centred(keys[0], (3, XP, YP, ZP), 0.3, 4.0, ((1, 8), (2, 4), (3, 8)), jnp.float32),
        "adjoint_velocity": draw_adjoint_velocity(jax.random.fold_in(keys[3], 71), 0),
        "penalty": jnp.clip(jnp.exp(math.log(64.0) - 2.7725887 * jax.random.uniform(keys[2], (XP, YP, ZP), jnp.float32) ** block_levels(keys[2], (XP, YP, ZP), ((0, 8), (1, 4), (2, 8)), -0.2, 0.2)), 4.0, 64.0),
    }


def gll_tables():
    points = 8
    gll_nodes = np.array([-1.0, -0.8717401485096066, -0.5917001814331423, -0.2092992179024789, 0.2092992179024789, 0.5917001814331423, 0.8717401485096066, 1.0])
    previous = np.ones(points)
    current = np.array(gll_nodes)
    for degree in range(1, points - 1):
        previous, current = current, ((2 * degree + 1) * gll_nodes * current - degree * previous) / (degree + 1)
    at_nodes = current
    weights = 2.0 / (points * (points - 1) * at_nodes ** 2)
    derivative = np.zeros((points, points))
    for target in range(points):
        for source in range(points):
            if target != source:
                derivative[target, source] = at_nodes[target] / (at_nodes[source] * (gll_nodes[target] - gll_nodes[source]))
    derivative[0, 0] = -points * (points - 1) / 4.0
    derivative[points - 1, points - 1] = points * (points - 1) / 4.0
    return weights, derivative


def node_masks(extent, position, devices, periodic):
    local_pos = jnp.arange(extent)
    global_pos = position * extent + local_pos
    first_node = jnp.logical_and(local_pos % 8 == 0, jnp.logical_or(periodic, global_pos > 0))
    last_node = jnp.logical_and(local_pos % 8 == 7, jnp.logical_or(periodic, global_pos < devices * extent - 1))
    return first_node.astype(jnp.float32), last_node.astype(jnp.float32)


def apply_dim(values, small, which_dim):
    rotated = jnp.moveaxis(values, which_dim, -1)
    extent = rotated.shape
    blocked = rotated.reshape(extent[:-1] + (extent[-1] // 8, 8))
    result = jnp.einsum("abej,ij->abei", blocked, small, precision=lax.Precision.HIGHEST)
    return jnp.moveaxis(result.reshape(extent), -1, which_dim)


def assemble(values):
    for which_dim, periodic in ((1, False), (2, False), (3, True)):
        first_node, last_node = node_masks(values.shape[which_dim], 0, 1, periodic)
        view_shape = [1, 1, 1, 1]
        view_shape[which_dim] = values.shape[which_dim]
        values = values + first_node.reshape(view_shape) * jnp.roll(values, 1, axis=which_dim) + last_node.reshape(view_shape) * jnp.roll(values, -1, axis=which_dim)
    return values


def reference(base_flow, adjoint_velocity, penalty):
    weights, derivative = gll_tables()
    small = jnp.asarray(derivative, jnp.float32)
    small_t = jnp.asarray(derivative.T, jnp.float32)
    extents = penalty.shape
    vectors = [jnp.asarray(np.tile(weights, extents[which_dim] // 8), jnp.float32) for which_dim in range(3)]
    mass = vectors[0][:, None, None] * vectors[1][None, :, None] * vectors[2][None, None, :]
    counts = []
    for which_dim, periodic in ((0, False), (1, False), (2, True)):
        first_node, last_node = node_masks(extents[which_dim], 0, 1, periodic)
        counts.append(1.0 + first_node + last_node)
    mult = counts[0][:, None, None] * counts[1][None, :, None] * counts[2][None, None, :]
    inv_mult = 1.0 / mult
    mass_total = mass * mult
    advection = []
    for comp_i in range(3):
        term = jnp.zeros(extents, jnp.float32)
        for comp_j in range(3):
            term = term - base_flow[comp_j] * apply_dim(adjoint_velocity[comp_i], small, comp_j)
            term = term + adjoint_velocity[comp_j] * apply_dim(base_flow[comp_j], small, comp_i)
        advection.append(mass * term)
    advc = assemble(jnp.stack(advection)) / mass_total
    divergence = apply_dim(advc[0], small, 0) + apply_dim(advc[1], small, 1) + apply_dim(advc[2], small, 2)
    rhs = -assemble((mass * divergence)[None])[0]

    def operator(values):
        local = penalty * mass * values
        for which_dim in range(3):
            local = local + apply_dim(mass * apply_dim(values, small, which_dim), small_t, which_dim)
        return assemble(local[None])[0]

    pressure = jnp.zeros_like(rhs)
    residual = rhs
    direction = rhs
    norm_now = jnp.sum(residual * residual * inv_mult)
    for step in range(ITERS):
        image = operator(direction)
        alpha = norm_now / jnp.sum(direction * image * inv_mult)
        pressure = pressure + alpha * direction
        residual = residual - alpha * image
        if step + 1 < ITERS:
            norm_next = jnp.sum(residual * residual * inv_mult)
            direction = residual + (norm_next / norm_now) * direction
            norm_now = norm_next
    gradient = jnp.stack([mass * apply_dim(pressure, small, which_dim) for which_dim in range(3)])
    projected = advc - assemble(gradient) / mass_total
    return projected, pressure
```

```python
import functools

import jax
import jax.numpy as jnp
import numpy as np
from jax import lax
from jax.experimental import pallas as pl
from jax.experimental.pallas import tpu as pltpu
from jax.sharding import PartitionSpec as P

MESH = pl.DeviceIdType.MESH
F32 = jnp.float32
HI = lax.Precision.HIGHEST
N = 8
NX, NY, NZ = 8, 32, 128
ROWS = NX * NY
GX, GY, GZ = 8, 4, 8


def gll_tables():
    points = 8
    nodes = np.array(
        [
            -1.0,
            -0.8717401485096066,
            -0.5917001814331423,
            -0.2092992179024789,
            0.2092992179024789,
            0.5917001814331423,
            0.8717401485096066,
            1.0,
        ]
    )
    previous = np.ones(points)
    current = np.array(nodes)
    for degree in range(1, points - 1):
        previous, current = (
            current,
            ((2 * degree + 1) * nodes * current - degree * previous) / (degree + 1),
        )
    weights = 2.0 / (points * (points - 1) * current**2)
    derivative = np.zeros((points, points))
    for target in range(points):
        for source in range(points):
            if target != source:
                derivative[target, source] = current[target] / (
                    current[source] * (nodes[target] - nodes[source])
                )
    derivative[0, 0] = -points * (points - 1) / 4.0
    derivative[points - 1, points - 1] = points * (points - 1) / 4.0
    return weights, derivative


W, D = gll_tables()
L = (D.T * W) @ D / W[:, None]


def average(extent):
    m = np.eye(extent)
    for k in range(8, extent, 8):
        m[k - 1, k - 1] = m[k, k] = m[k - 1, k] = m[k, k - 1] = 0.5
    return m


def along(matrix, extent):
    return np.kron(np.eye(extent // 8), matrix)


def over_y(matrix):
    return np.kron(np.eye(NX), matrix)


def face_rows_y(matrix):
    rows = np.zeros((16, ROWS))
    full = along(matrix, NY)
    for x in range(NX):
        rows[x, x * NY : (x + 1) * NY] = full[0]
        rows[8 + x, x * NY : (x + 1) * NY] = full[NY - 1]
    return rows


def face_rows_z(matrix):
    rows = np.zeros((16, NZ))
    full = along(matrix, NZ)
    rows[0] = full[0]
    rows[8] = full[NZ - 1]
    return rows


def tables():
    ay, az = average(NY), average(NZ)
    y_first = over_y(along(D, NY))
    y_second = np.concatenate(
        [
            over_y(ay),
            over_y(ay @ along(D, NY)),
            face_rows_y(D),
            over_y(ay @ along(L, NY)),
            face_rows_y(L),
        ]
    )
    local = np.arange(8)
    edge = np.where((local == 0) | (local == 7), 2.0, 1.0)
    wyz = W[:, None] * np.tile(W, 16)[None, :]
    myz = edge[:, None] * np.tile(edge, 16)[None, :]
    picks = np.zeros((16, NZ))
    picks[0, 0] = 1.0
    picks[8, NZ - 1] = 1.0
    z_all = np.concatenate(
        [
            along(D, NZ).T,
            az.T,
            (az @ along(D, NZ)).T,
            (az @ along(L, NZ)).T,
            face_rows_z(D),
            face_rows_z(L),
            picks,
            wyz,
            wyz * myz,
            1.0 / myz,
        ]
    )
    return [np.asarray(t, np.float32) for t in (y_first, y_second, z_all)]


Y_AVG, Y_DA, Y_DF, Y_LA, Y_LF = 0, 256, 512, 528, 784
Z_D, Z_AVG, Z_DA, Z_LA, Z_DF, Z_LF, Z_PICK, Z_W, Z_WM, Z_IM = (
    0,
    128,
    256,
    384,
    512,
    528,
    544,
    560,
    568,
    576,
)


def dot(a, b):
    return lax.dot_general(
        a, b, (((1,), (0,)), ((), ())), precision=HI, preferred_element_type=F32
    )


def dot_nt(a, b):
    return lax.dot_general(
        a, b, (((1,), (1,)), ((), ())), precision=HI, preferred_element_type=F32
    )


def dot_tn(a, b):
    return lax.dot_general(
        a, b, (((0,), (0,)), ((), ())), precision=HI, preferred_element_type=F32
    )


def flat(value):
    return value.reshape(ROWS, NZ)


def cube(value):
    return value.reshape(NX, NY, NZ)


def line(matrix_row, tiles):
    total = None
    for coefficient, tile in zip(matrix_row, tiles):
        part = tile * float(np.float32(coefficient))
        total = part if total is None else total + part
    return total


def kernel(
    base,
    adj,
    pen,
    yfirst,
    ysecond,
    zall,
    projected,
    pressure,
    bs,
    us,
    ps,
    y1,
    y2,
    zt,
    raw,
    za,
    ya,
    adv,
    pav,
    vec,
    tt,
    grad,
    wm,
    fz1,
    rz1,
    fy1,
    ry1,
    rx1,
    rxp,
    fx,
    rx,
    fy,
    ry,
    fz,
    rz,
    gfx,
    grx,
    gfy,
    gry,
    gfz,
    grz,
    mom,
    red1,
    part,
    red2,
    load_sem,
    send_sem,
    recv_sem,
    red_send,
    red_recv,
    out_sem,
):
    px = lax.axis_index("gx")
    py = lax.axis_index("gy")
    pz = lax.axis_index("gz")

    def at_x(offset):
        return (lax.rem(px + offset + GX, GX), py, pz)

    def at_y(offset):
        return (px, lax.rem(py + offset + GY, GY), pz)

    def at_z(offset):
        return (px, py, lax.rem(pz + offset + GZ, GZ))

    row = px // 2
    half = lax.rem(px, 2)
    index1 = half * 8 + pz
    index2 = row * 4 + py

    def group1(k):
        i = lax.rem(index1 + k, 16)
        return (row * 2 + i // 8, py, lax.rem(i, 8))

    def group2(k):
        i = lax.rem(index2 + k, 16)
        return ((i // 4) * 2 + half, lax.rem(i, 4), pz)

    loads = [
        pltpu.make_async_copy(adj, us, load_sem.at[0]),
        pltpu.make_async_copy(base, bs, load_sem.at[1]),
        pltpu.make_async_copy(yfirst, y1, load_sem.at[2]),
        pltpu.make_async_copy(zall, zt, load_sem.at[3]),
        pltpu.make_async_copy(pen, ps, load_sem.at[4]),
        pltpu.make_async_copy(ysecond, y2, load_sem.at[5]),
    ]
    for copy in loads:
        copy.start()

    barrier = pltpu.get_barrier_semaphore()
    for k in range(1, 16):
        pl.semaphore_signal(barrier, inc=1, device_id=group1(k), device_id_type=MESH)
        pl.semaphore_signal(barrier, inc=1, device_id=group2(k), device_id_type=MESH)
    for k in (-1, 1):
        pl.semaphore_signal(barrier, inc=1, device_id=at_x(k), device_id_type=MESH)

    hx = (jnp.where(px > 0, 0.5, 0.0), jnp.where(px < GX - 1, 0.5, 0.0))
    hy = (jnp.where(py > 0, 0.5, 0.0), jnp.where(py < GY - 1, 0.5, 0.0))
    sub = lax.broadcasted_iota(jnp.int32, (8, NZ), 0)
    first = jnp.where(sub == 0, 1.0, 0.0)
    last = jnp.where(sub == 7, 1.0, 0.0)

    pending = []
    counter = [0]

    def send(src, dst, device):
        k = counter[0]
        counter[0] += 1
        copy = pltpu.make_async_remote_copy(
            src_ref=src,
            dst_ref=dst,
            send_sem=send_sem.at[k],
            recv_sem=recv_sem.at[k],
            device_id=device,
            device_id_type=MESH,
        )
        copy.start()
        pending.append(copy)
        return copy

    for copy in loads[:4]:
        copy.wait()

    def tiles(ref, yt):
        return [ref[x, pl.ds(8 * yt, 8), :] for x in range(NX)]

    dz_table = zt[pl.ds(Z_D, 128), :]
    for i in range(3):
        ui = us.at[i]
        dy = cube(dot(y1[...], flat(ui[...])))
        dz = cube(dot(flat(ui[...]), dz_table))
        raw[i] = -(bs[1] * dy + bs[2] * dz)
    for j in range(3):
        uj = bs.at[j]
        raw[1] += us[j] * cube(dot(y1[...], flat(uj[...])))
        raw[2] += us[j] * cube(dot(flat(uj[...]), dz_table))
    for yt in range(4):
        rows = pl.ds(8 * yt, 8)
        for i in range(3):
            src = tiles(us.at[i], yt)
            for x in range(NX):
                raw[i, x, rows, :] -= bs[0, x, rows, :] * line(D[x], src)
        for j in range(3):
            src = tiles(bs.at[j], yt)
            for x in range(NX):
                raw[0, x, rows, :] += us[j, x, rows, :] * line(D[x], src)
    loads[4].wait()
    raw[3] = ps[...]

    avg_z = zt[pl.ds(Z_AVG, 128), :]
    pick = zt[pl.ds(Z_PICK, 16), :]
    faces = None
    for i in range(4):
        own = dot_nt(pick, flat(raw[i]))
        if i == 0:
            faces = own
        else:
            faces = faces + pltpu.roll(own, i, 0)
    fz1[...] = faces
    pl.semaphore_wait(barrier, 32)
    copies = [
        send(fz1.at[pl.ds(0, 8)], rz1.at[pl.ds(8, 8)], at_z(-1)),
        send(fz1.at[pl.ds(8, 8)], rz1.at[pl.ds(0, 8)], at_z(1)),
    ]
    for i in range(4):
        za[i] = cube(dot(flat(raw[i]), avg_z))
    for copy in copies:
        copy.wait_recv()
    delta = 0.5 * (rz1[...] - fz1[...])
    for i in range(4):
        pick_i = pick if i == 0 else pltpu.roll(pick, i, 0)
        za[i] += cube(dot_tn(delta, pick_i))
    loads[5].wait()
    for i in range(4):
        for x in range(NX):
            fy1[0, i, pl.ds(x, 1), :] = za[i, x, pl.ds(0, 1), :]
            fy1[1, i, pl.ds(x, 1), :] = za[i, x, pl.ds(NY - 1, 1), :]
    copies = [
        send(fy1.at[0], ry1.at[1], at_y(-1)),
        send(fy1.at[1], ry1.at[0], at_y(1)),
    ]
    avg_y = y2[pl.ds(Y_AVG, 256), :]
    for i in range(4):
        ya[i] = cube(dot(avg_y, flat(za[i])))
    for copy in copies:
        copy.wait_recv()

    def add_y(target, low, high):
        for x in range(NX):
            target[x, pl.ds(0, 8), :] += first * low[x : x + 1, :]
            target[x, pl.ds(NY - 8, 8), :] += last * high[x : x + 1, :]

    for i in range(4):
        add_y(
            ya.at[i],
            hy[0] * (ry1[0, i] - fy1[0, i]),
            hy[1] * (ry1[1, i] - fy1[1, i]),
        )
    copies = [
        send(ya.at[pl.ds(0, 3), 0], rx1.at[1], at_x(-1)),
        send(ya.at[pl.ds(0, 3), NX - 1], rx1.at[0], at_x(1)),
    ]
    copies_p = [
        send(ya.at[3, 0], rxp.at[1], at_x(-1)),
        send(ya.at[3, NX - 1], rxp.at[0], at_x(1)),
    ]

    w_tile = zt[pl.ds(Z_W, 8), :]
    wm_tile = zt[pl.ds(Z_WM, 8), :]
    im_tile = zt[pl.ds(Z_IM, 8), :]
    fix_low = 1.0 - first * (0.5 - hy[0])
    fix_high = 1.0 - last * (0.5 - hy[1])
    inv_low = 1.0 + first * (1.0 - 2.0 * hy[0])
    inv_high = 1.0 + last * (1.0 - 2.0 * hy[1])
    wm_y = [wm_tile * fix_low, wm_tile, wm_tile, wm_tile * fix_high]
    im_y = [im_tile * inv_low, im_tile, im_tile, im_tile * inv_high]
    scale_x = [float(w) for w in W]
    mult_x = [1.0 + 2.0 * hx[0]] + [1.0] * 6 + [1.0 + 2.0 * hx[1]]
    inv_x = [1.0 - hx[0]] + [1.0] * 6 + [1.0 - hx[1]]
    for yt in range(4):
        for x in range(NX):
            wm[x, pl.ds(8 * yt, 8), :] = wm_y[yt] * (mult_x[x] * scale_x[x])

    for i in range(3):
        for x in range(1, NX - 1):
            adv[i, x] = ya[i, x]
    for copy in copies:
        copy.wait_recv()
    for i in range(3):
        adv[i, 0] = ya[i, 0] + hx[0] * (rx1[0, i] - ya[i, 0])
        adv[i, NX - 1] = ya[i, NX - 1] + hx[1] * (rx1[1, i] - ya[i, NX - 1])

    def local(vx, vy, vz, mx, ymat, zmat, with_mass):
        yz = cube(dot(y2[pl.ds(ymat, 256), :], flat(vy[...]))) + cube(
            dot(flat(vz[...]), zt[pl.ds(zmat, 128), :])
        )
        if with_mass:
            yz = yz + pav[...] * vx[...]
        tt[...] = yz
        for yt in range(4):
            src = tiles(vx, yt)
            for x in range(NX):
                tt[x, pl.ds(8 * yt, 8), :] += line(mx[x], src)

    def x_faces(source, mx, low, high):
        for yt in range(4):
            src = tiles(source, yt)
            low[pl.ds(8 * yt, 8), :] = line(mx[0], src)
            high[pl.ds(8 * yt, 8), :] = line(mx[NX - 1], src)

    def add_z(target, delta_z):
        target[...] += cube(dot_tn(delta_z, pick))

    def phase(k, vx, vy, vz, mx, ymat, yface, zmat, zface, with_mass, sign):
        x_faces(vx, mx, fx.at[k, 0], fx.at[k, 1])
        sx = [
            send(fx.at[k, 0], rx.at[k, 1], at_x(-1)),
            send(fx.at[k, 1], rx.at[k, 0], at_x(1)),
        ]
        fz[k] = dot_nt(zt[pl.ds(zface, 16), :], flat(vz[...]))
        sz = [
            send(fz.at[k, pl.ds(0, 8)], rz.at[k, pl.ds(8, 8)], at_z(-1)),
            send(fz.at[k, pl.ds(8, 8)], rz.at[k, pl.ds(0, 8)], at_z(1)),
        ]
        fy[k] = dot(y2[pl.ds(yface, 16), :], flat(vy[...]))
        sy = [
            send(fy.at[k, pl.ds(0, 8)], ry.at[k, pl.ds(8, 8)], at_y(-1)),
            send(fy.at[k, pl.ds(8, 8)], ry.at[k, pl.ds(0, 8)], at_y(1)),
        ]
        if with_mass and k == 1:
            finish_penalty()
        local(vx, vy, vz, mx, ymat, zmat, with_mass)
        for copy in sy:
            copy.wait_recv()
        add_y(
            tt,
            hy[0] * (ry[k, pl.ds(0, 8), :] - fy[k, pl.ds(0, 8), :]),
            hy[1] * (ry[k, pl.ds(8, 8), :] - fy[k, pl.ds(8, 8), :]),
        )
        for copy in sz:
            copy.wait_recv()
        add_z(tt, 0.5 * (rz[k] - fz[k]))
        out = vec.at[k]
        for x in range(1, NX - 1):
            out[x] = tt[x] * (sign * wm[x])
        for copy in sx:
            copy.wait_recv()
        out[0] = (tt[0] + hx[0] * (rx[k, 0] - fx[k, 0])) * (sign * wm[0])
        out[NX - 1] = (tt[NX - 1] + hx[1] * (rx[k, 1] - fx[k, 1])) * (sign * wm[NX - 1])

    def finish_penalty():
        for x in range(1, NX - 1):
            pav[x] = ya[3, x]
        for copy in copies_p:
            copy.wait_recv()
        pav[0] = ya[3, 0] + hx[0] * (rxp[0] - ya[3, 0])
        pav[NX - 1] = ya[3, NX - 1] + hx[1] * (rxp[1] - ya[3, NX - 1])

    phase(0, adv.at[0], adv.at[1], adv.at[2], D, Y_DA, Y_DF, Z_DA, Z_DF, False, -1.0)
    for k in (1, 2):
        v = vec.at[k - 1]
        phase(k, v, v, v, L, Y_LA, Y_LF, Z_LA, Z_LF, True, 1.0)

    def inner(a, b):
        total = None
        for yt in range(4):
            rows = pl.ds(8 * yt, 8)
            s = None
            for x in range(NX):
                p = a[x, rows, :] * b[x, rows, :]
                if x in (0, NX - 1):
                    p = p * inv_x[x]
                s = p if s is None else s + p
            s = s * im_y[yt]
            total = s if total is None else total + s
        return jnp.sum(total, axis=0, keepdims=True)

    v0, v1, v2 = vec.at[0], vec.at[1], vec.at[2]
    local(v2, v2, v2, L, Y_LA, Z_LA, True)
    total = None
    for yt in range(4):
        rows = pl.ds(8 * yt, 8)
        s = None
        for x in range(NX):
            p = v2[x, rows, :] * tt[x, rows, :] * scale_x[x]
            s = p if s is None else s + p
        total = s if total is None else total + s
    mom[pl.ds(5, 1), :] = jnp.sum(total * w_tile, axis=0, keepdims=True)
    mom[pl.ds(0, 1), :] = inner(v0, v0)
    mom[pl.ds(1, 1), :] = inner(v0, v1)
    mom[pl.ds(2, 1), :] = inner(v1, v1)
    mom[pl.ds(3, 1), :] = inner(v1, v2)
    mom[pl.ds(4, 1), :] = inner(v2, v2)
    mom[pl.ds(6, 2), :] = jnp.zeros((2, NZ), F32)

    def spread(source, slots, own, group, which):
        slots[own] = source[...]
        for k in range(1, 16):
            copy = pltpu.make_async_remote_copy(
                src_ref=source,
                dst_ref=slots.at[own],
                send_sem=red_send.at[which, k],
                recv_sem=red_recv.at[which],
                device_id=group(k),
                device_id_type=MESH,
            )
            copy.start()
            pending.append(copy)

    def gather(slots, which):
        view = slots.at[pl.ds(0, 15)]
        pltpu.make_async_copy(view, view, red_recv.at[which]).wait()
        total = slots[0]
        for k in range(1, 16):
            total = total + slots[k]
        return total

    spread(mom, red1, index1, group1, 0)

    zpick = zt[pl.ds(Z_DF, 16), :]
    for k in range(3):
        v = vec.at[k]
        x_faces(v, D, gfx.at[0, k], gfx.at[1, k])
        gfy[:, k] = dot(y2[pl.ds(Y_DF, 16), :], flat(v[...])).reshape(2, 8, NZ)
    faces = None
    for k in range(3):
        own = dot_nt(zpick, flat(vec[k]))
        faces = own if k == 0 else faces + pltpu.roll(own, k, 0)
    gfz[...] = faces
    gsend = [
        send(gfx.at[0], grx.at[1], at_x(-1)),
        send(gfx.at[1], grx.at[0], at_x(1)),
        send(gfz.at[pl.ds(0, 8)], grz.at[pl.ds(8, 8)], at_z(-1)),
        send(gfz.at[pl.ds(8, 8)], grz.at[pl.ds(0, 8)], at_z(1)),
        send(gfy.at[0], gry.at[1], at_y(-1)),
        send(gfy.at[1], gry.at[0], at_y(1)),
    ]
    part[...] = gather(red1, 0)
    spread(part, red2, index2, group2, 1)
    for k in range(3):
        v = vec.at[k]
        grad[k, 1] = cube(dot(y2[pl.ds(Y_DA, 256), :], flat(v[...])))
        grad[k, 2] = cube(dot(flat(v[...]), zt[pl.ds(Z_DA, 128), :]))
        for yt in range(4):
            src = tiles(v, yt)
            for x in range(NX):
                grad[k, 0, x, pl.ds(8 * yt, 8), :] = line(D[x], src)
    for copy in gsend:
        copy.wait_recv()
    delta_z = 0.5 * (grz[...] - gfz[...])
    for k in range(3):
        grad[k, 0, 0] += hx[0] * (grx[0, k] - gfx[0, k])
        grad[k, 0, NX - 1] += hx[1] * (grx[1, k] - gfx[1, k])
        add_y(
            grad.at[k, 1],
            hy[0] * (gry[0, k] - gfy[0, k]),
            hy[1] * (gry[1, k] - gfy[1, k]),
        )
        pick_k = pick if k == 0 else pltpu.roll(pick, k, 0)
        grad[k, 2] += cube(dot_tn(delta_z, pick_k))

    sums = jnp.sum(gather(red2, 1), axis=1, keepdims=True)
    m = [jnp.broadcast_to(sums[k : k + 1, :], (8, NZ)) for k in range(6)]
    s0, s1, s2 = lax.rsqrt(m[1]), lax.rsqrt(m[3]), lax.rsqrt(m[5])
    h01 = m[2] * s0 * s1
    h02 = m[3] * s0 * s2
    h12 = m[4] * s1 * s2
    h00, h11, h22 = m[1] * s0 * s0, m[3] * s1 * s1, m[5] * s2 * s2
    g0, g1, g2 = m[0] * s0, m[1] * s1, m[2] * s2
    l10 = h01 / h00
    l20 = h02 / h00
    d1 = h11 - l10 * h01
    e1 = h12 - l20 * h01
    l21 = e1 / d1
    d2 = h22 - l20 * h02 - l21 * e1
    y0 = g0
    y1_ = g1 - l10 * y0
    y2_ = g2 - l20 * y0 - l21 * y1_
    c2 = y2_ / d2
    c1 = y1_ / d1 - l21 * c2
    c0 = y0 / h00 - l10 * c1 - l20 * c2
    c0, c1, c2 = c0 * s0, c1 * s1, c2 * s2

    for yt in range(4):
        rows = pl.ds(8 * yt, 8)
        for x in range(NX):
            tt[x, rows, :] = (
                c0 * v0[x, rows, :] + c1 * v1[x, rows, :] + c2 * v2[x, rows, :]
            )
            for i in range(3):
                raw[i, x, rows, :] = adv[i, x, rows, :] - (
                    c0 * grad[0, i, x, rows, :]
                    + c1 * grad[1, i, x, rows, :]
                    + c2 * grad[2, i, x, rows, :]
                )
    outs = [
        pltpu.make_async_copy(raw.at[pl.ds(0, 3)], projected, out_sem.at[0]),
        pltpu.make_async_copy(tt, pressure, out_sem.at[1]),
    ]
    for copy in outs:
        copy.start()
    for copy in pending:
        copy.wait_send()
    for copy in outs:
        copy.wait()


def per_device(base_flow, adjoint_velocity, penalty):
    field = (NX, NY, NZ)
    v = lambda *shape: pltpu.VMEM(shape, F32)
    consts = [jnp.asarray(t) for t in tables()]
    any_spec = pl.BlockSpec(memory_space=pltpu.HBM)
    sends = 30
    return pl.pallas_call(
        kernel,
        out_shape=(
            jax.ShapeDtypeStruct((3,) + field, F32),
            jax.ShapeDtypeStruct(field, F32),
        ),
        in_specs=[any_spec] * 6,
        out_specs=(any_spec, any_spec),
        scratch_shapes=[
            v(3, *field),
            v(3, *field),
            v(*field),
            v(*consts[0].shape),
            v(*consts[1].shape),
            v(*consts[2].shape),
            v(4, *field),
            v(4, *field),
            v(4, *field),
            v(3, *field),
            v(*field),
            v(3, *field),
            v(*field),
            v(3, 3, *field),
            v(*field),
            v(16, ROWS),
            v(16, ROWS),
            v(2, 4, 8, NZ),
            v(2, 4, 8, NZ),
            v(2, 3, NY, NZ),
            v(2, NY, NZ),
            v(3, 2, NY, NZ),
            v(3, 2, NY, NZ),
            v(3, 16, NZ),
            v(3, 16, NZ),
            v(3, 16, ROWS),
            v(3, 16, ROWS),
            v(2, 3, NY, NZ),
            v(2, 3, NY, NZ),
            v(2, 3, 8, NZ),
            v(2, 3, 8, NZ),
            v(16, ROWS),
            v(16, ROWS),
            v(8, NZ),
            v(16, 8, NZ),
            v(8, NZ),
            v(16, 8, NZ),
            pltpu.SemaphoreType.DMA((6,)),
            pltpu.SemaphoreType.DMA((sends + 10,)),
            pltpu.SemaphoreType.DMA((sends + 10,)),
            pltpu.SemaphoreType.DMA((2, 16)),
            pltpu.SemaphoreType.DMA((2,)),
            pltpu.SemaphoreType.DMA((2,)),
        ],
        compiler_params=pltpu.CompilerParams(
            collective_id=0, has_side_effects=True, vmem_limit_bytes=63 * 1024 * 1024
        ),
        name="adjoint",
    )(base_flow, adjoint_velocity, penalty, *consts)


def solution(mesh):
    spec3 = P(None, "gx", "gy", "gz")
    spec1 = P("gx", "gy", "gz")
    return jax.shard_map(
        per_device,
        mesh=mesh,
        in_specs=(spec3, spec3, spec1),
        out_specs=(spec3, spec1),
        check_vma=False,
    )
```

```python
import functools

import jax
import jax.numpy as jnp
import ml_dtypes
import numpy as np
from jax import lax
from jax.experimental import pallas as pl
from jax.experimental.pallas import tpu as pltpu
from jax.sharding import PartitionSpec as P

MESH = pl.DeviceIdType.MESH
F32 = jnp.float32
HI = lax.Precision.HIGHEST
N = 8
NX, NY, NZ = 8, 32, 128
ROWS = NX * NY
GX, GY, GZ = 8, 4, 8
NEAR = [(-1, 0, 0), (1, 0, 0)] + [
    (0, dy, dz) for dy in (-1, 1, 0) for dz in (-1, 1, 0) if (dy, dz) != (0, 0)
]


def gll_tables():
    points = 8
    nodes = np.array(
        [
            -1.0,
            -0.8717401485096066,
            -0.5917001814331423,
            -0.2092992179024789,
            0.2092992179024789,
            0.5917001814331423,
            0.8717401485096066,
            1.0,
        ]
    )
    previous = np.ones(points)
    current = np.array(nodes)
    for degree in range(1, points - 1):
        previous, current = (
            current,
            ((2 * degree + 1) * nodes * current - degree * previous) / (degree + 1),
        )
    weights = 2.0 / (points * (points - 1) * current**2)
    derivative = np.zeros((points, points))
    for target in range(points):
        for source in range(points):
            if target != source:
                derivative[target, source] = current[target] / (
                    current[source] * (nodes[target] - nodes[source])
                )
    derivative[0, 0] = -points * (points - 1) / 4.0
    derivative[points - 1, points - 1] = points * (points - 1) / 4.0
    return weights, derivative


W, D = gll_tables()
L = (D.T * W) @ D / W[:, None]


def average(extent):
    m = np.eye(extent)
    for k in range(8, extent, 8):
        m[k - 1, k - 1] = m[k, k] = m[k - 1, k] = m[k, k - 1] = 0.5
    return m


def along(matrix, extent):
    return np.kron(np.eye(extent // 8), matrix)


def over_y(matrix):
    return np.kron(np.eye(NX), matrix)


def face_rows_y(matrix):
    rows = np.zeros((16, ROWS))
    full = along(matrix, NY)
    for x in range(NX):
        rows[x, x * NY : (x + 1) * NY] = full[0]
        rows[8 + x, x * NY : (x + 1) * NY] = full[NY - 1]
    return rows


def face_rows_z(matrix):
    rows = np.zeros((16, NZ))
    full = along(matrix, NZ)
    rows[0] = full[0]
    rows[8] = full[NZ - 1]
    return rows


def tables():
    ay, az = average(NY), average(NZ)
    y_first = over_y(along(D, NY))
    y_second = np.concatenate(
        [
            over_y(ay),
            over_y(ay @ along(D, NY)),
            face_rows_y(D),
            over_y(ay @ along(L, NY)),
            face_rows_y(L),
        ]
    )
    local = np.arange(8)
    edge = np.where((local == 0) | (local == 7), 2.0, 1.0)
    wyz = W[:, None] * np.tile(W, 16)[None, :]
    myz = edge[:, None] * np.tile(edge, 16)[None, :]
    picks = np.zeros((16, NZ))
    picks[0, 0] = 1.0
    picks[8, NZ - 1] = 1.0
    z_all = np.concatenate(
        [
            along(D, NZ).T,
            az.T,
            (az @ along(D, NZ)).T,
            (az @ along(L, NZ)).T,
            face_rows_z(D),
            face_rows_z(L),
            picks,
            wyz,
            wyz * myz,
            1.0 / myz,
        ]
    )
    bf16 = ml_dtypes.bfloat16

    def split(matrix):
        high = np.asarray(matrix, np.float32).astype(bf16)
        low = (matrix - high.astype(np.float64)).astype(np.float32).astype(bf16)
        return high, low

    y_first = np.concatenate(split(y_first), axis=0)
    high, low = split(along(D, NZ).T)
    z_first = np.concatenate(
        [
            np.concatenate([high, low], axis=1),
            np.concatenate([high, np.zeros_like(low)], axis=1),
        ],
        axis=0,
    )
    return [
        y_first,
        z_first,
        np.asarray(y_second, np.float32),
        np.asarray(z_all, np.float32),
    ]


Y_AVG, Y_DA, Y_DF, Y_LA, Y_LF = 0, 256, 512, 528, 784
Z_D, Z_AVG, Z_DA, Z_LA, Z_DF, Z_LF, Z_PICK, Z_W, Z_WM, Z_IM = (
    0,
    128,
    256,
    384,
    512,
    528,
    544,
    560,
    568,
    576,
)


def dot(a, b):
    return lax.dot_general(
        a, b, (((1,), (0,)), ((), ())), precision=HI, preferred_element_type=F32
    )


def dot_nt(a, b):
    return lax.dot_general(
        a, b, (((1,), (1,)), ((), ())), precision=HI, preferred_element_type=F32
    )


def dot_tn(a, b):
    return lax.dot_general(
        a, b, (((0,), (0,)), ((), ())), precision=HI, preferred_element_type=F32
    )


def flat(value):
    return value.reshape(ROWS, NZ)


def cube(value):
    return value.reshape(NX, NY, NZ)


def line(matrix_row, tiles):
    total = None
    for coefficient, tile in zip(matrix_row, tiles):
        part = tile * float(np.float32(coefficient))
        total = part if total is None else total + part
    return total


def kernel(
    base,
    adj,
    pen,
    yfirst,
    zfirst,
    ysecond,
    zall,
    adv_out,
    grad_out,
    vec_out,
    coef_out,
    bs,
    us,
    ps,
    y1,
    z1,
    y2,
    zt,
    raw,
    halo,
    adv,
    pav,
    vec,
    tt,
    grad,
    wm,
    fz1,
    rz1,
    fy1,
    ry1,
    xf,
    xq,
    rx1,
    rq1,
    rx2,
    hx1,
    rmix,
    fx,
    rx,
    fy,
    ry,
    fz,
    rz,
    gfx,
    grx,
    gfy,
    gry,
    gfz,
    grz,
    mom,
    red1,
    part,
    red2,
    coef,
    load_sem,
    send_sem,
    recv_sem,
    red_send,
    red_recv,
    out_sem,
):
    px = lax.axis_index("gx")
    py = lax.axis_index("gy")
    pz = lax.axis_index("gz")

    def at(dx, dy, dz):
        return (
            lax.rem(px + dx + GX, GX),
            lax.rem(py + dy + GY, GY),
            lax.rem(pz + dz + GZ, GZ),
        )

    def at_x(offset):
        return at(offset, 0, 0)

    def at_y(offset):
        return at(0, offset, 0)

    def at_z(offset):
        return at(0, 0, offset)

    row = px // 2
    half = lax.rem(px, 2)
    index1 = half * 8 + pz
    index2 = row * 4 + py

    def group1(k):
        i = lax.rem(index1 + k, 16)
        return (row * 2 + i // 8, py, lax.rem(i, 8))

    def group2(k):
        i = lax.rem(index2 + k, 16)
        return ((i // 4) * 2 + half, lax.rem(i, 4), pz)

    loads = [
        pltpu.make_async_copy(adj, us, load_sem.at[0]),
        pltpu.make_async_copy(base, bs, load_sem.at[1]),
        pltpu.make_async_copy(yfirst, y1, load_sem.at[2]),
        pltpu.make_async_copy(zfirst, z1, load_sem.at[3]),
        pltpu.make_async_copy(zall, zt, load_sem.at[4]),
        pltpu.make_async_copy(pen, ps, load_sem.at[5]),
        pltpu.make_async_copy(ysecond, y2, load_sem.at[6]),
    ]
    for copy in loads:
        copy.start()

    barrier = pltpu.get_barrier_semaphore()
    for dx, dy, dz in NEAR:
        pl.semaphore_signal(
            barrier, inc=1, device_id=at(dx, dy, dz), device_id_type=MESH
        )
    for k in range(1, 16):
        pl.semaphore_signal(barrier, inc=1, device_id=group1(k), device_id_type=MESH)
        pl.semaphore_signal(barrier, inc=1, device_id=group2(k), device_id_type=MESH)

    hx = (jnp.where(px > 0, 0.5, 0.0), jnp.where(px < GX - 1, 0.5, 0.0))
    hy = (jnp.where(py > 0, 0.5, 0.0), jnp.where(py < GY - 1, 0.5, 0.0))
    hx2 = (jnp.where(px > 1, 0.5, 0.0), jnp.where(px < GX - 2, 0.5, 0.0))
    sub = lax.broadcasted_iota(jnp.int32, (8, NZ), 0)
    first = jnp.where(sub == 0, 1.0, 0.0)
    last = jnp.where(sub == 7, 1.0, 0.0)

    pending = []
    counter = [0]

    def send(src, dst, device):
        k = counter[0]
        counter[0] += 1
        copy = pltpu.make_async_remote_copy(
            src_ref=src,
            dst_ref=dst,
            send_sem=send_sem.at[k],
            recv_sem=recv_sem.at[k],
            device_id=device,
            device_id_type=MESH,
        )
        copy.start()
        pending.append(copy)
        return copy

    for copy in loads[:4]:
        copy.wait()

    def tiles(ref, yt):
        return [ref[x, pl.ds(8 * yt, 8), :] for x in range(NX)]

    def bf16_dot(a, b):
        return lax.dot_general(
            a, b, (((1,), (0,)), ((), ())), preferred_element_type=F32
        )

    def first_yz(value, need_y, need_z):
        value = flat(value)
        high = value.astype(jnp.bfloat16)
        low = (value - high.astype(F32)).astype(jnp.bfloat16)
        both = jnp.concatenate([high, low], axis=1)
        dy = dz = None
        if need_y:
            out = bf16_dot(y1[...], both)
            dy = cube(out[:ROWS, :NZ] + out[:ROWS, NZ:] + out[ROWS:, :NZ])
        if need_z:
            out = bf16_dot(both, z1[...])
            dz = cube(out[:, :NZ] + out[:, NZ:])
        return dy, dz

    for i in range(3):
        dy, dz = first_yz(us[i], True, True)
        raw[i] = -(bs[1] * dy + bs[2] * dz)
    for j in range(3):
        dy, dz = first_yz(bs[j], True, True)
        raw[1] += us[j] * dy
        raw[2] += us[j] * dz
    for yt in range(4):
        rows = pl.ds(8 * yt, 8)
        for i in range(3):
            src = tiles(us.at[i], yt)
            for x in range(NX):
                raw[i, x, rows, :] -= bs[0, x, rows, :] * line(D[x], src)
        for j in range(3):
            src = tiles(bs.at[j], yt)
            for x in range(NX):
                raw[0, x, rows, :] += us[j, x, rows, :] * line(D[x], src)
    for copy in loads[4:6]:
        copy.wait()
    raw[3] = ps[...]
    pick = zt[pl.ds(Z_PICK, 16), :]
    faces = None
    for i in range(4):
        own = dot_nt(pick, flat(raw[i]))
        faces = own if i == 0 else faces + pltpu.roll(own, i, 0)
    fz1[...] = faces
    for i in range(4):
        for x in range(NX):
            for side, y in ((0, 0), (1, NY - 1)):
                fy1[side, i, pl.ds(x, 1), :] = raw[i, x, pl.ds(y, 1), :]
    pl.semaphore_wait(barrier, 30 + len(NEAR))
    near = []
    for dz in (-1, 1):
        for dy in (0, -1, 1):
            src = fz1.at[pl.ds(0 if dz < 0 else 8, 8)]
            dst = rz1.at[1 if dz < 0 else 0, 1 - dy]
            near.append(send(src, dst, at(0, dy, dz)))
    near += [
        send(fy1.at[0], ry1.at[1], at_y(-1)),
        send(fy1.at[1], ry1.at[0], at_y(1)),
    ]
    raw_x = [
        send(raw.at[pl.ds(0, 3), 0], rx1.at[1, pl.ds(0, 3)], at_x(-1)),
        send(raw.at[pl.ds(0, 3), NX - 1], rx1.at[0, pl.ds(0, 3)], at_x(1)),
    ]
    copies_p = [
        send(raw.at[3, 0], rx1.at[1, 3], at_x(-1)),
        send(raw.at[3, NX - 1], rx1.at[0, 3], at_x(1)),
    ]

    w_tile = zt[pl.ds(Z_W, 8), :]
    wm_tile = zt[pl.ds(Z_WM, 8), :]
    im_tile = zt[pl.ds(Z_IM, 8), :]
    fix_low = 1.0 - first * (0.5 - hy[0])
    fix_high = 1.0 - last * (0.5 - hy[1])
    inv_low = 1.0 + first * (1.0 - 2.0 * hy[0])
    inv_high = 1.0 + last * (1.0 - 2.0 * hy[1])
    wm_y = [wm_tile * fix_low, wm_tile, wm_tile, wm_tile * fix_high]
    im_y = [im_tile * inv_low, im_tile, im_tile, im_tile * inv_high]
    scale_x = [float(w) for w in W]
    mult_x = [1.0 + 2.0 * hx[0]] + [1.0] * 6 + [1.0 + 2.0 * hx[1]]
    inv_x = [1.0 - hx[0]] + [1.0] * 6 + [1.0 - hx[1]]
    for yt in range(4):
        for x in range(NX):
            wm[x, pl.ds(8 * yt, 8), :] = wm_y[yt] * (mult_x[x] * scale_x[x])

    lane = lax.broadcasted_iota(jnp.int32, (8, NZ), 1)
    begin = lax.rem(lane, 8) == 0
    end = lax.rem(lane, 8) == 7
    keep_z = jnp.where(begin | end, 0.5, 1.0)
    from_low = jnp.where(begin & (lane > 0), 0.5, 0.0)
    from_high = jnp.where(end & (lane < NZ - 1), 0.5, 0.0)
    low_y = [first * hy[0]] + [first * 0.5] * 3
    high_y = [last * 0.5] * 3 + [last * hy[1]]
    keep_y = [1.0 - low_y[t] - high_y[t] for t in range(4)]

    def mix_slab(src, low, high, edge, dst):
        for t in range(4):
            rows = pl.ds(8 * t, 8)
            down = low if t == 0 else src[pl.ds(8 * t - 1, 1), :]
            up = high if t == 3 else src[pl.ds(8 * t + 8, 1), :]
            value = src[rows, :] * keep_y[t] + down * low_y[t] + up * high_y[t]
            dst[rows, :] = (
                value * keep_z
                + pltpu.roll(value, 1, 1) * from_low
                + pltpu.roll(value, NZ - 1, 1) * from_high
                + edge[rows, :]
            )

    wide = lax.broadcasted_iota(jnp.int32, (8, ROWS), 1)
    y_of = lax.rem(wide, NY)
    x_of = wide // NY
    inner_begin = (lax.rem(wide, 8) == 0) & (y_of > 0)
    inner_end = (lax.rem(wide, 8) == 7) & (y_of < NY - 1)

    def y_mix(mid, down, up):
        partner = jnp.where(
            y_of == 0,
            pltpu.roll(down, ROWS - (NY - 1), 1),
            jnp.where(
                y_of == NY - 1,
                pltpu.roll(up, NY - 1, 1),
                jnp.where(
                    inner_begin, pltpu.roll(mid, 1, 1), pltpu.roll(mid, ROWS - 1, 1)
                ),
            ),
        )
        weight = jnp.where(
            y_of == 0,
            hy[0],
            jnp.where(
                y_of == NY - 1, hy[1], jnp.where(inner_begin | inner_end, 0.5, 0.0)
            ),
        )
        return mid + weight * (partner - mid)

    spots = jnp.concatenate(
        [
            jnp.where((sub == i) & (lane == 0), 0.5, 0.0)
            + jnp.where((sub == 4 + i) & (lane == NZ - 1), 0.5, 0.0)
            for i in range(4)
        ],
        axis=1,
    ).astype(F32)
    spots = jnp.concatenate([spots] * 3, axis=0).astype(jnp.bfloat16)

    def expand(values):
        parts, rest = [], values
        for _ in range(3):
            parts.append(rest.astype(jnp.bfloat16).astype(F32))
            rest = rest - parts[-1]
        split = jnp.concatenate(parts, axis=0).astype(jnp.bfloat16)
        return lax.dot_general(
            split, spots, (((0,), (0,)), ((), ())), preferred_element_type=F32
        )

    for copy in near:
        copy.wait_recv()
    edges = y_mix(rz1[0, 1], rz1[0, 0], rz1[0, 2]) + pltpu.roll(
        y_mix(rz1[1, 1], rz1[1, 0], rz1[1, 2]), 4, 0
    )
    wide_halo = expand(edges)
    for i in range(4):
        halo[i] = cube(wide_halo[:, NZ * i : NZ * (i + 1)])
    for side in (0, 1):
        for i in range(4):
            for end in (0, 1):
                xq[side, pl.ds(NY + 4 * end + i, 1), :] = ry1[
                    end, i, pl.ds(side * (NX - 1), 1), :
                ]
        xq[side, pl.ds(NY + 8, 8), :] = edges[:, NZ * side : NZ * (side + 1)]

    def mixed(i, x, dst):
        mix_slab(
            raw.at[i, x],
            ry1[0, i, pl.ds(x, 1), :],
            ry1[1, i, pl.ds(x, 1), :],
            halo.at[i, x],
            dst,
        )

    for side in (0, 1):
        mixed(0, side * (NX - 1), xf.at[side, 0])
    for x in range(1, NX - 1):
        mixed(0, x, adv.at[0, x])
    for yt in range(4):
        rows = pl.ds(8 * yt, 8)
        src = [xf[0, 0, rows, :]]
        src += [adv[0, x, rows, :] for x in range(1, NX - 1)]
        src += [xf[1, 0, rows, :]]
        ends = [src[0] * (1.0 - hx[0]), src[NX - 1] * (1.0 - hx[1])]
        xq[0, rows, :] = line(D[0], src[: NX - 1] + [ends[1]])
        xq[1, rows, :] = line(D[NX - 1], [ends[0]] + src[1:])
    sx = [
        send(xq.at[0], rq1.at[1], at_x(-1)),
        send(xq.at[1], rq1.at[0], at_x(1)),
        send(xf.at[0, 0], rx2.at[1, 0], at_x(-2)),
        send(xf.at[1, 0], rx2.at[0, 0], at_x(2)),
    ]
    for i in range(1, 3):
        for side in (0, 1):
            mixed(i, side * (NX - 1), xf.at[side, i])
        for x in range(1, NX - 1):
            mixed(i, x, adv.at[i, x])
    for side in (0, 1):
        mixed(3, side * (NX - 1), xf.at[side, 3])
    for x in range(1, NX - 1):
        mixed(3, x, pav.at[x])
    loads[6].wait()
    for copy in raw_x:
        copy.wait_recv()
    for copy in sx:
        copy.wait_recv()
    edges = jnp.where(lane < NZ // 2, rq1[1, pl.ds(NY + 8, 8), :], rq1[0, pl.ds(NY + 8, 8), :])
    wide_halo = expand(edges)
    for i in range(4):
        part_halo = wide_halo[:, NZ * i : NZ * (i + 1)]
        hx1[0, i] = part_halo[NZ - NY :, :]
        hx1[1, i] = part_halo[:NY, :]

    def neighbour_face(side, i):
        mix_slab(
            rx1.at[side, i],
            rq1[side, pl.ds(NY + i, 1), :],
            rq1[side, pl.ds(NY + 4 + i, 1), :],
            hx1.at[side, i],
            rmix.at[side, i],
        )

    for i in range(3):
        for side in (0, 1):
            neighbour_face(side, i)
            own = xf[side, i]
            adv[i, side * (NX - 1)] = own + hx[side] * (rmix[side, i] - own)
    for side in (0, 1):
        mine, other = side * (NX - 1), (1 - side) * (NX - 1)
        rx[0, side] = (
            rq1[side, pl.ds(0, NY), :]
            + (0.5 * float(D[other, other])) * (xf[side, 0] - rmix[side, 0])
            + (float(D[other, mine]) * hx2[side]) * rx2[side, 0]
        )
    def local(vx, vy, vz, mx, ymat, zmat, with_mass):
        yz = cube(dot(y2[pl.ds(ymat, 256), :], flat(vy[...]))) + cube(
            dot(flat(vz[...]), zt[pl.ds(zmat, 128), :])
        )
        if with_mass:
            yz = yz + pav[...] * vx[...]
        tt[...] = yz
        for yt in range(4):
            src = tiles(vx, yt)
            for x in range(NX):
                tt[x, pl.ds(8 * yt, 8), :] += line(mx[x], src)

    def x_faces(source, mx, low, high):
        for yt in range(4):
            src = tiles(source, yt)
            low[pl.ds(8 * yt, 8), :] = line(mx[0], src)
            high[pl.ds(8 * yt, 8), :] = line(mx[NX - 1], src)

    def add_y(target, low, high):
        for x in range(NX):
            target[x, pl.ds(0, 8), :] += first * low[x : x + 1, :]
            target[x, pl.ds(NY - 8, 8), :] += last * high[x : x + 1, :]

    def add_z(target, delta_z):
        target[...] += cube(dot_tn(delta_z, pick))

    gradient_copies = {}

    def gradient_faces(k):
        v = vec.at[k]
        x_faces(v, D, gfx.at[0, k], gfx.at[1, k])
        gfy[k] = dot(y2[pl.ds(Y_DF, 16), :], flat(v[...]))
        gfz[k] = dot_nt(zt[pl.ds(Z_DF, 16), :], flat(v[...]))
        low, high = pl.ds(0, 8), pl.ds(8, 8)
        gradient_copies[k] = [
            send(gfx.at[0, k], grx.at[1, k], at_x(-1)),
            send(gfx.at[1, k], grx.at[0, k], at_x(1)),
            send(gfz.at[k, low], grz.at[k, high], at_z(-1)),
            send(gfz.at[k, high], grz.at[k, low], at_z(1)),
            send(gfy.at[k, low], gry.at[k, high], at_y(-1)),
            send(gfy.at[k, high], gry.at[k, low], at_y(1)),
        ]

    def gradient_local(k):
        v = vec.at[k]
        grad[k, 1] = cube(dot(y2[pl.ds(Y_DA, 256), :], flat(v[...])))
        grad[k, 2] = cube(dot(flat(v[...]), zt[pl.ds(Z_DA, 128), :]))
        for yt in range(4):
            src = tiles(v, yt)
            for x in range(NX):
                grad[k, 0, x, pl.ds(8 * yt, 8), :] = line(D[x], src)

    def gradient_edges(k):
        for copy in gradient_copies[k]:
            copy.wait_recv()
        for side in (0, 1):
            grad[k, 0, side * (NX - 1)] += hx[side] * (grx[side, k] - gfx[side, k])
        add_y(
            grad.at[k, 1],
            hy[0] * (gry[k, pl.ds(0, 8), :] - gfy[k, pl.ds(0, 8), :]),
            hy[1] * (gry[k, pl.ds(8, 8), :] - gfy[k, pl.ds(8, 8), :]),
        )
        add_z(grad.at[k, 2], 0.5 * (grz[k] - gfz[k]))

    def phase(k, vx, vy, vz, mx, ymat, yface, zmat, zface, with_mass, sign):
        x_faces(vx, mx, fx.at[k, 0], fx.at[k, 1])
        sx = []
        if k > 0:
            sx = [
                send(fx.at[k, 0], rx.at[k, 1], at_x(-1)),
                send(fx.at[k, 1], rx.at[k, 0], at_x(1)),
            ]
        fz[k] = dot_nt(zt[pl.ds(zface, 16), :], flat(vz[...]))
        sz = [
            send(fz.at[k, pl.ds(0, 8)], rz.at[k, pl.ds(8, 8)], at_z(-1)),
            send(fz.at[k, pl.ds(8, 8)], rz.at[k, pl.ds(0, 8)], at_z(1)),
        ]
        fy[k] = dot(y2[pl.ds(yface, 16), :], flat(vy[...]))
        sy = [
            send(fy.at[k, pl.ds(0, 8)], ry.at[k, pl.ds(8, 8)], at_y(-1)),
            send(fy.at[k, pl.ds(8, 8)], ry.at[k, pl.ds(0, 8)], at_y(1)),
        ]
        if with_mass and k == 1:
            finish_penalty()
        local(vx, vy, vz, mx, ymat, zmat, with_mass)
        if k > 0:
            gradient_faces(k - 1)
        for copy in sy:
            copy.wait_recv()
        add_y(
            tt,
            hy[0] * (ry[k, pl.ds(0, 8), :] - fy[k, pl.ds(0, 8), :]),
            hy[1] * (ry[k, pl.ds(8, 8), :] - fy[k, pl.ds(8, 8), :]),
        )
        for copy in sz:
            copy.wait_recv()
        add_z(tt, 0.5 * (rz[k] - fz[k]))
        out = vec.at[k]
        for x in range(1, NX - 1):
            out[x] = tt[x] * (sign * wm[x])
        if k > 0:
            gradient_local(k - 1)
        for copy in sx:
            copy.wait_recv()
        out[0] = (tt[0] + hx[0] * (rx[k, 0] - fx[k, 0])) * (sign * wm[0])
        out[NX - 1] = (tt[NX - 1] + hx[1] * (rx[k, 1] - fx[k, 1])) * (sign * wm[NX - 1])

    def finish_penalty():
        for copy in copies_p:
            copy.wait_recv()
        for side in (0, 1):
            neighbour_face(side, 3)
            own = xf[side, 3]
            pav[side * (NX - 1)] = own + hx[side] * (rmix[side, 3] - own)

    phase(0, adv.at[0], adv.at[1], adv.at[2], D, Y_DA, Y_DF, Z_DA, Z_DF, False, -1.0)
    for k in (1, 2):
        v = vec.at[k - 1]
        phase(k, v, v, v, L, Y_LA, Y_LF, Z_LA, Z_LF, True, 1.0)

    def inner(a, b):
        total = None
        for yt in range(4):
            rows = pl.ds(8 * yt, 8)
            s = None
            for x in range(NX):
                p = a[x, rows, :] * b[x, rows, :]
                if x in (0, NX - 1):
                    p = p * inv_x[x]
                s = p if s is None else s + p
            s = s * im_y[yt]
            total = s if total is None else total + s
        return jnp.sum(total, axis=0, keepdims=True)

    v0, v1, v2 = vec.at[0], vec.at[1], vec.at[2]
    local(v2, v2, v2, L, Y_LA, Z_LA, True)
    total = None
    for yt in range(4):
        rows = pl.ds(8 * yt, 8)
        s = None
        for x in range(NX):
            p = v2[x, rows, :] * tt[x, rows, :] * scale_x[x]
            s = p if s is None else s + p
        total = s if total is None else total + s
    mom[pl.ds(5, 1), :] = jnp.sum(total * w_tile, axis=0, keepdims=True)
    mom[pl.ds(0, 1), :] = inner(v0, v0)
    mom[pl.ds(1, 1), :] = inner(v0, v1)
    mom[pl.ds(2, 1), :] = inner(v1, v1)
    mom[pl.ds(3, 1), :] = inner(v1, v2)
    mom[pl.ds(4, 1), :] = inner(v2, v2)
    mom[pl.ds(6, 2), :] = jnp.zeros((2, NZ), F32)

    def spread(source, slots, own, group, which):
        slots[own] = source[...]
        for k in range(1, 16):
            copy = pltpu.make_async_remote_copy(
                src_ref=source,
                dst_ref=slots.at[own],
                send_sem=red_send.at[which, k],
                recv_sem=red_recv.at[which],
                device_id=group(k),
                device_id_type=MESH,
            )
            copy.start()
            pending.append(copy)

    def gather(slots, which):
        view = slots.at[pl.ds(0, 15)]
        pltpu.make_async_copy(view, view, red_recv.at[which]).wait()
        total = slots[0]
        for k in range(1, 16):
            total = total + slots[k]
        return total

    spread(mom, red1, index1, group1, 0)

    gradient_faces(2)
    part[...] = gather(red1, 0)
    spread(part, red2, index2, group2, 1)
    gradient_local(2)
    for k in range(3):
        gradient_edges(k)

    outs = [
        pltpu.make_async_copy(adv, adv_out, out_sem.at[0]),
        pltpu.make_async_copy(grad, grad_out, out_sem.at[1]),
        pltpu.make_async_copy(vec, vec_out, out_sem.at[2]),
    ]
    for copy in outs:
        copy.start()
    sums = jnp.sum(gather(red2, 1), axis=1, keepdims=True)
    m = [jnp.broadcast_to(sums[k : k + 1, :], (8, NZ)) for k in range(6)]
    s0, s1, s2 = lax.rsqrt(m[1]), lax.rsqrt(m[3]), lax.rsqrt(m[5])
    h01 = m[2] * s0 * s1
    h02 = m[3] * s0 * s2
    h12 = m[4] * s1 * s2
    h00, h11, h22 = m[1] * s0 * s0, m[3] * s1 * s1, m[5] * s2 * s2
    g0, g1, g2 = m[0] * s0, m[1] * s1, m[2] * s2
    l10 = h01 / h00
    l20 = h02 / h00
    d1 = h11 - l10 * h01
    e1 = h12 - l20 * h01
    l21 = e1 / d1
    d2 = h22 - l20 * h02 - l21 * e1
    y0 = g0
    y1_ = g1 - l10 * y0
    y2_ = g2 - l20 * y0 - l21 * y1_
    c2 = y2_ / d2
    c1 = y1_ / d1 - l21 * c2
    c0 = y0 / h00 - l10 * c1 - l20 * c2
    c0, c1, c2 = c0 * s0, c1 * s1, c2 * s2

    coef[...] = jnp.where(sub == 0, c0, jnp.where(sub == 1, c1, c2))
    last_out = pltpu.make_async_copy(coef, coef_out, out_sem.at[3])
    last_out.start()
    for copy in pending:
        copy.wait_send()
    for copy in outs:
        copy.wait()
    last_out.wait()


PIECES = 4


def combine(
    adv_in,
    grad_in,
    vec_in,
    coef_in,
    projected,
    pressure,
    adv,
    grad,
    vec,
    coef,
    proj,
    pres,
    load_sem,
    coef_sem,
    out_sem,
):
    size = NX // PIECES
    coef_copy = pltpu.make_async_copy(coef_in, coef, coef_sem.at[0])
    coef_copy.start()
    loads, outs = [], []
    for k in range(PIECES):
        part = pl.ds(size * k, size)
        copies = [
            pltpu.make_async_copy(vec_in.at[:, part], vec.at[:, part], load_sem.at[k, 0]),
            pltpu.make_async_copy(adv_in.at[:, part], adv.at[:, part], load_sem.at[k, 1]),
            pltpu.make_async_copy(
                grad_in.at[:, :, part], grad.at[:, :, part], load_sem.at[k, 2]
            ),
        ]
        for copy in copies:
            copy.start()
        loads.append(copies)
    coef_copy.wait()
    c = [coef[pl.ds(k, 1), :] for k in range(3)]
    for k in range(PIECES):
        part = pl.ds(size * k, size)
        loads[k][0].wait()
        pres[part] = c[0] * vec[0, part] + c[1] * vec[1, part] + c[2] * vec[2, part]
        outs.append(pltpu.make_async_copy(pres.at[part], pressure.at[part], out_sem.at[k, 0]))
        outs[-1].start()
        for copy in loads[k][1:]:
            copy.wait()
        for i in range(3):
            proj[i, part] = adv[i, part] - (
                c[0] * grad[0, i, part] + c[1] * grad[1, i, part] + c[2] * grad[2, i, part]
            )
        outs.append(
            pltpu.make_async_copy(proj.at[:, part], projected.at[:, part], out_sem.at[k, 1])
        )
        outs[-1].start()
    for copy in outs:
        copy.wait()


def per_device(base_flow, adjoint_velocity, penalty):
    field = (NX, NY, NZ)
    v = lambda *shape: pltpu.VMEM(shape, F32)
    consts = [jnp.asarray(t) for t in tables()]
    any_spec = pl.BlockSpec(memory_space=pltpu.HBM)
    sends = 60
    adv, grad, vec, coef = pl.pallas_call(
        kernel,
        out_shape=(
            jax.ShapeDtypeStruct((3,) + field, F32),
            jax.ShapeDtypeStruct((3, 3) + field, F32),
            jax.ShapeDtypeStruct((3,) + field, F32),
            jax.ShapeDtypeStruct((8, NZ), F32),
        ),
        in_specs=[any_spec] * 7,
        out_specs=(any_spec,) * 4,
        scratch_shapes=[
            v(3, *field),
            v(3, *field),
            v(*field),
            pltpu.VMEM(consts[0].shape, jnp.bfloat16),
            pltpu.VMEM(consts[1].shape, jnp.bfloat16),
            v(*consts[2].shape),
            v(*consts[3].shape),
            v(4, *field),
            v(4, *field),
            v(3, *field),
            v(*field),
            v(3, *field),
            v(*field),
            v(3, 3, *field),
            v(*field),
            v(16, ROWS),
            v(2, 3, 8, ROWS),
            v(2, 4, 8, NZ),
            v(2, 4, 8, NZ),
            v(2, 4, NY, NZ),
            v(2, NY + 16, NZ),
            v(2, 4, NY, NZ),
            v(2, NY + 16, NZ),
            v(2, 2, NY, NZ),
            v(2, 4, NY, NZ),
            v(2, 4, NY, NZ),
            v(3, 2, NY, NZ),
            v(3, 2, NY, NZ),
            v(3, 16, NZ),
            v(3, 16, NZ),
            v(3, 16, ROWS),
            v(3, 16, ROWS),
            v(2, 3, NY, NZ),
            v(2, 3, NY, NZ),
            v(3, 16, NZ),
            v(3, 16, NZ),
            v(3, 16, ROWS),
            v(3, 16, ROWS),
            v(8, NZ),
            v(16, 8, NZ),
            v(8, NZ),
            v(16, 8, NZ),
            v(8, NZ),
            pltpu.SemaphoreType.DMA((7,)),
            pltpu.SemaphoreType.DMA((sends + 10,)),
            pltpu.SemaphoreType.DMA((sends + 10,)),
            pltpu.SemaphoreType.DMA((2, 16)),
            pltpu.SemaphoreType.DMA((2,)),
            pltpu.SemaphoreType.DMA((4,)),
        ],
        compiler_params=pltpu.CompilerParams(
            collective_id=0, has_side_effects=True, vmem_limit_bytes=63 * 1024 * 1024
        ),
        name="adjoint",
    )(base_flow, adjoint_velocity, penalty, *consts)
    return pl.pallas_call(
        combine,
        out_shape=(
            jax.ShapeDtypeStruct((3,) + field, F32),
            jax.ShapeDtypeStruct(field, F32),
        ),
        in_specs=[any_spec] * 4,
        out_specs=(any_spec,) * 2,
        scratch_shapes=[
            v(3, *field),
            v(3, 3, *field),
            v(3, *field),
            v(8, NZ),
            v(3, *field),
            v(*field),
            pltpu.SemaphoreType.DMA((PIECES, 3)),
            pltpu.SemaphoreType.DMA((1,)),
            pltpu.SemaphoreType.DMA((PIECES, 2)),
        ],
        compiler_params=pltpu.CompilerParams(vmem_limit_bytes=63 * 1024 * 1024),
        name="combine",
    )(adv, grad, vec, coef)


def solution(mesh):
    spec3 = P(None, "gx", "gy", "gz")
    spec1 = P("gx", "gy", "gz")
    return jax.shard_map(
        per_device,
        mesh=mesh,
        in_specs=(spec3, spec3, spec1),
        out_specs=(spec3, spec1),
        check_vma=False,
    )
```

```python
import functools

import jax
import jax.numpy as jnp
import ml_dtypes
import numpy as np
from jax import lax
from jax.experimental import pallas as pl
from jax.experimental.pallas import tpu as pltpu
from jax.sharding import PartitionSpec as P

MESH = pl.DeviceIdType.MESH
F32 = jnp.float32
N = 8
NX, NY, NZ = 8, 32, 128
ROWS = NX * NY
GX, GY, GZ = 8, 4, 8
NEAR = [(-1, 0, 0), (1, 0, 0)] + [
    (0, dy, dz) for dy in (-1, 1, 0) for dz in (-1, 1, 0) if (dy, dz) != (0, 0)
]


def gll_tables():
    points = 8
    nodes = np.array(
        [
            -1.0,
            -0.8717401485096066,
            -0.5917001814331423,
            -0.2092992179024789,
            0.2092992179024789,
            0.5917001814331423,
            0.8717401485096066,
            1.0,
        ]
    )
    previous = np.ones(points)
    current = np.array(nodes)
    for degree in range(1, points - 1):
        previous, current = (
            current,
            ((2 * degree + 1) * nodes * current - degree * previous) / (degree + 1),
        )
    weights = 2.0 / (points * (points - 1) * current**2)
    derivative = np.zeros((points, points))
    for target in range(points):
        for source in range(points):
            if target != source:
                derivative[target, source] = current[target] / (
                    current[source] * (nodes[target] - nodes[source])
                )
    derivative[0, 0] = -points * (points - 1) / 4.0
    derivative[points - 1, points - 1] = points * (points - 1) / 4.0
    return weights, derivative


W, D = gll_tables()
L = (D.T * W) @ D / W[:, None]


def average(extent):
    m = np.eye(extent)
    for k in range(8, extent, 8):
        m[k - 1, k - 1] = m[k, k] = m[k - 1, k] = m[k, k - 1] = 0.5
    return m


def along(matrix, extent):
    return np.kron(np.eye(extent // 8), matrix)


def face_rows_z(matrix):
    rows = np.zeros((16, NZ))
    full = along(matrix, NZ)
    rows[0] = full[0]
    rows[8] = full[NZ - 1]
    return rows


def split(matrix):
    parts, rest = [], np.asarray(matrix, np.float64)
    for _ in range(3):
        parts.append(rest.astype(np.float32).astype(ml_dtypes.bfloat16))
        rest = rest - parts[-1].astype(np.float64)
    return parts


def tables():
    az = average(NZ)
    blocks = []
    for matrix in (along(D, NZ), az @ along(D, NZ), az @ along(L, NZ)):
        high, mid, low = split(matrix.T)
        blocks.append(
            np.concatenate(
                [
                    np.concatenate([high, mid, high], axis=1),
                    np.concatenate([high, mid, low], axis=1),
                ],
                axis=0,
            )
        )
    z_blocks = np.stack(blocks)
    picks = np.zeros((16, NZ))
    picks[0, 0] = 1.0
    picks[8, NZ - 1] = 1.0
    z_faces = np.concatenate(
        split(face_rows_z(D))
        + split(face_rows_z(L))
        + [picks.astype(ml_dtypes.bfloat16)] * 3,
        axis=0,
    )
    local = np.arange(8)
    edge = np.where((local == 0) | (local == 7), 2.0, 1.0)
    wyz = W[:, None] * np.tile(W, 16)[None, :]
    myz = edge[:, None] * np.tile(edge, 16)[None, :]
    columns = [
        np.repeat(matrix[:, k : k + 1], NZ, axis=1)
        for matrix in (D, L)
        for k in range(8)
    ]
    small = np.concatenate([wyz, wyz * myz, 1.0 / myz] + columns, axis=0)
    return [z_blocks, z_faces, np.asarray(small, np.float32)]


Z_D, Z_DA, Z_LA = 0, 1, 2
F_D, F_L, F_PICK = 0, 48, 96
T_W, T_WM, T_IM, T_D, T_L = 0, 8, 16, 24, 88


def dot(a, b):
    return lax.dot_general(a, b, (((1,), (0,)), ((), ())), preferred_element_type=F32)


def dot_nt(a, b):
    return lax.dot_general(a, b, (((1,), (1,)), ((), ())), preferred_element_type=F32)


def dot_tn(a, b):
    return lax.dot_general(a, b, (((0,), (0,)), ((), ())), preferred_element_type=F32)


def split3(value):
    high = value.astype(jnp.bfloat16)
    rest = value - high.astype(F32)
    mid = rest.astype(jnp.bfloat16)
    return high, mid, (rest - mid.astype(F32)).astype(jnp.bfloat16)


def stack3(value):
    parts, rest = [], value
    for _ in range(3):
        parts.append(rest.astype(jnp.bfloat16).astype(F32))
        rest = rest - parts[-1]
    return jnp.concatenate(parts, axis=0).astype(jnp.bfloat16)


def flat(value):
    return value.reshape(ROWS, NZ)


def cube(value):
    return value.reshape(NX, NY, NZ)


def line(matrix_row, tiles):
    total = None
    for coefficient, tile in zip(matrix_row, tiles):
        part = tile * float(np.float32(coefficient))
        total = part if total is None else total + part
    return total


def kernel(
    base,
    adj,
    pen,
    zblocks,
    zfaces,
    small,
    adv_out,
    grad_out,
    vec_out,
    coef_out,
    bs,
    us,
    ps,
    zb,
    zf,
    zt,
    raw,
    halo,
    adv,
    pav,
    vec,
    tt,
    grad,
    wm,
    wyz,
    q2,
    rq2,
    fz1,
    rz1,
    fy1,
    ry1,
    xf,
    xq,
    rx1,
    rq1,
    rx2,
    hx1,
    rmix,
    fx,
    rx,
    fy,
    ry,
    fz,
    rz,
    gfx,
    grx,
    gfy,
    gry,
    gfz,
    grz,
    mom,
    red1,
    part,
    red2,
    coef,
    load_sem,
    send_sem,
    recv_sem,
    red_send,
    red_recv,
    out_sem,
):
    px = lax.axis_index("gx")
    py = lax.axis_index("gy")
    pz = lax.axis_index("gz")

    def at(dx, dy, dz):
        return (
            lax.rem(px + dx + GX, GX),
            lax.rem(py + dy + GY, GY),
            lax.rem(pz + dz + GZ, GZ),
        )

    def at_x(offset):
        return at(offset, 0, 0)

    def at_y(offset):
        return at(0, offset, 0)

    def at_z(offset):
        return at(0, 0, offset)

    row = px // 2
    half = lax.rem(px, 2)
    index1 = half * 8 + pz
    index2 = row * 4 + py

    def group1(k):
        i = lax.rem(index1 + k, 16)
        return (row * 2 + i // 8, py, lax.rem(i, 8))

    def group2(k):
        i = lax.rem(index2 + k, 16)
        return ((i // 4) * 2 + half, lax.rem(i, 4), pz)

    loads = [
        pltpu.make_async_copy(adj, us, load_sem.at[0]),
        pltpu.make_async_copy(base, bs, load_sem.at[1]),
        pltpu.make_async_copy(zblocks.at[0], zb.at[0], load_sem.at[2]),
        pltpu.make_async_copy(small, zt, load_sem.at[3]),
        pltpu.make_async_copy(zfaces, zf, load_sem.at[4]),
        pltpu.make_async_copy(pen, ps, load_sem.at[5]),
        pltpu.make_async_copy(
            zblocks.at[pl.ds(1, 2)], zb.at[pl.ds(1, 2)], load_sem.at[6]
        ),
    ]
    for copy in loads:
        copy.start()

    barrier = pltpu.get_barrier_semaphore()
    for dx, dy, dz in NEAR:
        pl.semaphore_signal(
            barrier, inc=1, device_id=at(dx, dy, dz), device_id_type=MESH
        )
    for k in range(1, 16):
        pl.semaphore_signal(barrier, inc=1, device_id=group1(k), device_id_type=MESH)
        pl.semaphore_signal(barrier, inc=1, device_id=group2(k), device_id_type=MESH)

    hx = (jnp.where(px > 0, 0.5, 0.0), jnp.where(px < GX - 1, 0.5, 0.0))
    hy = (jnp.where(py > 0, 0.5, 0.0), jnp.where(py < GY - 1, 0.5, 0.0))
    hx2 = (jnp.where(px > 1, 0.5, 0.0), jnp.where(px < GX - 2, 0.5, 0.0))
    sub = lax.broadcasted_iota(jnp.int32, (8, NZ), 0)
    first = jnp.where(sub == 0, 1.0, 0.0)
    last = jnp.where(sub == 7, 1.0, 0.0)

    pending = []
    counter = [0]

    def send(src, dst, device):
        k = counter[0]
        counter[0] += 1
        copy = pltpu.make_async_remote_copy(
            src_ref=src,
            dst_ref=dst,
            send_sem=send_sem.at[k],
            recv_sem=recv_sem.at[k],
            device_id=device,
            device_id_type=MESH,
        )
        copy.start()
        pending.append(copy)
        return copy

    for copy in loads[:4]:
        copy.wait()

    def y_rows(yt):
        return pl.ds(8 * yt, 8)

    def tiles(ref, yt):
        return [ref[x, y_rows(yt), :] for x in range(NX)]

    def loop(count, start=0):
        def run(body):
            for k in range(start, count):
                body(k)

        return run

    def columns(offset):
        return [zt[pl.ds(offset + 8 * k, 8), :] for k in range(8)]

    def y_line(ref, x, coefficients):
        result = []
        for t in range(4):
            total = None
            for k in range(8):
                part = coefficients[k] * ref[x, pl.ds(8 * t + k, 1), :]
                total = part if total is None else total + part
            result.append(total)
        return result

    def z_line(parts, block):
        high, mid, low = parts
        out = dot(
            jnp.concatenate([high, mid], axis=1), zb[block, :, pl.ds(0, 2 * NZ)]
        )
        rest = dot(
            jnp.concatenate([low, high], axis=1), zb[block, :, pl.ds(2 * NZ, NZ)]
        )
        return cube(out[:, :NZ] + (out[:, NZ:] + rest))

    d_columns = columns(T_D)
    for i in range(3):
        raw[i] = -bs[2] * z_line(split3(flat(us[i])), Z_D)
    for j in range(3):
        raw[2] += us[j] * z_line(split3(flat(bs[j])), Z_D)

    @loop(NX)
    def _(x):
        for i in range(3):
            for t, value in enumerate(y_line(us.at[i], x, d_columns)):
                rows = pl.ds(8 * t, 8)
                raw[i, x, rows, :] -= bs[1, x, rows, :] * value
        for j in range(3):
            for t, value in enumerate(y_line(bs.at[j], x, d_columns)):
                rows = pl.ds(8 * t, 8)
                raw[1, x, rows, :] += us[j, x, rows, :] * value

    @loop(4)
    def _(yt):
        rows = y_rows(yt)
        for i in range(3):
            src = tiles(us.at[i], yt)
            for x in range(NX):
                raw[i, x, rows, :] -= bs[0, x, rows, :] * line(D[x], src)
        for j in range(3):
            src = tiles(bs.at[j], yt)
            for x in range(NX):
                raw[0, x, rows, :] += us[j, x, rows, :] * line(D[x], src)

    for copy in loads[4:6]:
        copy.wait()
    raw[3] = ps[...]
    def z_faces(parts, offset):
        high, mid, low = parts
        table = zf[pl.ds(offset, 48), :]
        a, b = dot_nt(table, high), dot_nt(table[:32], mid)
        c = dot_nt(table[:16], low)
        return a[:16] + (a[16:32] + b[:16] + (a[32:] + b[16:] + c))

    def z_ends(parts):
        table = zf[pl.ds(F_PICK, 16), :]
        a, b, c = (dot_nt(table, part) for part in parts)
        return a + (b + c)

    faces = None
    for i in range(4):
        own = z_ends(split3(flat(raw[i])))
        faces = own if i == 0 else faces + pltpu.roll(own, i, 0)
    fz1[...] = faces
    for i in range(4):
        for x in range(NX):
            for side, y in ((0, 0), (1, NY - 1)):
                fy1[side, i, pl.ds(x, 1), :] = raw[i, x, pl.ds(y, 1), :]
    pl.semaphore_wait(barrier, 30 + len(NEAR))
    near = []
    for dz in (-1, 1):
        for dy in (0, -1, 1):
            src = fz1.at[pl.ds(0 if dz < 0 else 8, 8)]
            dst = rz1.at[1 if dz < 0 else 0, 1 - dy]
            near.append(send(src, dst, at(0, dy, dz)))
    near += [
        send(fy1.at[0], ry1.at[1], at_y(-1)),
        send(fy1.at[1], ry1.at[0], at_y(1)),
    ]
    raw_x = [
        send(raw.at[pl.ds(0, 3), 0], rx1.at[1, pl.ds(0, 3)], at_x(-1)),
        send(raw.at[pl.ds(0, 3), NX - 1], rx1.at[0, pl.ds(0, 3)], at_x(1)),
    ]
    copies_p = [
        send(raw.at[3, 0], rx1.at[1, 3], at_x(-1)),
        send(raw.at[3, NX - 1], rx1.at[0, 3], at_x(1)),
    ]

    w_tile = zt[pl.ds(T_W, 8), :]
    wm_tile = zt[pl.ds(T_WM, 8), :]
    im_tile = zt[pl.ds(T_IM, 8), :]
    fix_low = 1.0 - first * (0.5 - hy[0])
    fix_high = 1.0 - last * (0.5 - hy[1])
    inv_low = 1.0 + first * (1.0 - 2.0 * hy[0])
    inv_high = 1.0 + last * (1.0 - 2.0 * hy[1])
    wm_y = [wm_tile * fix_low, wm_tile, wm_tile, wm_tile * fix_high]
    im_y = [im_tile * inv_low, im_tile, im_tile, im_tile * inv_high]
    scale_x = [float(w) for w in W]
    mult_x = [1.0 + 2.0 * hx[0]] + [1.0] * 6 + [1.0 + 2.0 * hx[1]]
    inv_x = [1.0 - hx[0]] + [1.0] * 6 + [1.0 - hx[1]]
    for yt in range(4):
        for x in range(NX):
            wm[x, pl.ds(8 * yt, 8), :] = wm_y[yt] * (mult_x[x] * scale_x[x])
        wyz[pl.ds(8 * yt, 8), :] = wm_y[yt]

    lane = lax.broadcasted_iota(jnp.int32, (8, NZ), 1)
    begin = lax.rem(lane, 8) == 0
    end = lax.rem(lane, 8) == 7
    keep_z = jnp.where(begin | end, 0.5, 1.0)
    from_low = jnp.where(begin & (lane > 0), 0.5, 0.0)
    from_high = jnp.where(end & (lane < NZ - 1), 0.5, 0.0)
    low_y = [first * hy[0]] + [first * 0.5] * 3
    high_y = [last * 0.5] * 3 + [last * hy[1]]
    keep_y = [1.0 - low_y[t] - high_y[t] for t in range(4)]

    def mix_slab(src, low, high, edge, dst):
        for t in range(4):
            rows = pl.ds(8 * t, 8)
            down = low if t == 0 else src[pl.ds(8 * t - 1, 1), :]
            up = high if t == 3 else src[pl.ds(8 * t + 8, 1), :]
            value = src[rows, :] * keep_y[t] + down * low_y[t] + up * high_y[t]
            dst[rows, :] = (
                value * keep_z
                + pltpu.roll(value, 1, 1) * from_low
                + pltpu.roll(value, NZ - 1, 1) * from_high
                + edge[rows, :]
            )

    wide = lax.broadcasted_iota(jnp.int32, (8, ROWS), 1)
    y_of = lax.rem(wide, NY)
    x_of = wide // NY
    inner_begin = (lax.rem(wide, 8) == 0) & (y_of > 0)
    inner_end = (lax.rem(wide, 8) == 7) & (y_of < NY - 1)

    def y_mix(mid, down, up):
        partner = jnp.where(
            y_of == 0,
            pltpu.roll(down, ROWS - (NY - 1), 1),
            jnp.where(
                y_of == NY - 1,
                pltpu.roll(up, NY - 1, 1),
                jnp.where(
                    inner_begin, pltpu.roll(mid, 1, 1), pltpu.roll(mid, ROWS - 1, 1)
                ),
            ),
        )
        weight = jnp.where(
            y_of == 0,
            hy[0],
            jnp.where(
                y_of == NY - 1, hy[1], jnp.where(inner_begin | inner_end, 0.5, 0.0)
            ),
        )
        return mid + weight * (partner - mid)

    spots = jnp.concatenate(
        [
            jnp.where((sub == i) & (lane == 0), 0.5, 0.0)
            + jnp.where((sub == 4 + i) & (lane == NZ - 1), 0.5, 0.0)
            for i in range(4)
        ],
        axis=1,
    ).astype(F32)
    spots = jnp.concatenate([spots] * 3, axis=0).astype(jnp.bfloat16)

    def expand(values):
        return dot_tn(stack3(values), spots)

    for copy in near:
        copy.wait_recv()
    edges = y_mix(rz1[0, 1], rz1[0, 0], rz1[0, 2]) + pltpu.roll(
        y_mix(rz1[1, 1], rz1[1, 0], rz1[1, 2]), 4, 0
    )
    wide_halo = expand(edges)
    for i in range(4):
        halo[i] = cube(wide_halo[:, NZ * i : NZ * (i + 1)])
    for side in (0, 1):
        for i in range(4):
            for end in (0, 1):
                xq[side, pl.ds(NY + 4 * end + i, 1), :] = ry1[
                    end, i, pl.ds(side * (NX - 1), 1), :
                ]
        xq[side, pl.ds(NY + 8, 8), :] = edges[:, NZ * side : NZ * (side + 1)]

    def mixed(i, x, dst):
        mix_slab(
            raw.at[i, x],
            ry1[0, i, pl.ds(x, 1), :],
            ry1[1, i, pl.ds(x, 1), :],
            halo.at[i, x],
            dst,
        )

    for side in (0, 1):
        mixed(0, side * (NX - 1), xf.at[side, 0])
    @loop(NX - 1, 1)
    def _(x):
        mixed(0, x, adv.at[0, x])

    @loop(4)
    def _(yt):
        rows = y_rows(yt)
        src = [xf[0, 0, rows, :]]
        src += [adv[0, x, rows, :] for x in range(1, NX - 1)]
        src += [xf[1, 0, rows, :]]
        ends = [src[0] * (1.0 - hx[0]), src[NX - 1] * (1.0 - hx[1])]
        xq[0, rows, :] = line(D[0], src[: NX - 1] + [ends[1]])
        xq[1, rows, :] = line(D[NX - 1], [ends[0]] + src[1:])

    sx = [
        send(xq.at[0], rq1.at[1], at_x(-1)),
        send(xq.at[1], rq1.at[0], at_x(1)),
        send(xf.at[0, 0], rx2.at[1, 0], at_x(-2)),
        send(xf.at[1, 0], rx2.at[0, 0], at_x(2)),
    ]
    for i in range(1, 4):
        for side in (0, 1):
            mixed(i, side * (NX - 1), xf.at[side, i])

    @loop(NX - 1, 1)
    def _(x):
        for i in range(1, 3):
            mixed(i, x, adv.at[i, x])
        mixed(3, x, pav.at[x])

    loads[6].wait()
    for copy in raw_x:
        copy.wait_recv()
    for copy in sx:
        copy.wait_recv()
    edges = jnp.where(lane < NZ // 2, rq1[1, pl.ds(NY + 8, 8), :], rq1[0, pl.ds(NY + 8, 8), :])
    wide_halo = expand(edges)
    for i in range(4):
        part_halo = wide_halo[:, NZ * i : NZ * (i + 1)]
        hx1[0, i] = part_halo[NZ - NY :, :]
        hx1[1, i] = part_halo[:NY, :]

    def neighbour_face(side, i):
        mix_slab(
            rx1.at[side, i],
            rq1[side, pl.ds(NY + i, 1), :],
            rq1[side, pl.ds(NY + 4 + i, 1), :],
            hx1.at[side, i],
            rmix.at[side, i],
        )

    for i in range(3):
        for side in (0, 1):
            neighbour_face(side, i)
            own = xf[side, i]
            adv[i, side * (NX - 1)] = own + hx[side] * (rmix[side, i] - own)
    for side in (0, 1):
        mine, other = side * (NX - 1), (1 - side) * (NX - 1)
        rx[0, side] = (
            rq1[side, pl.ds(0, NY), :]
            + (0.5 * float(D[other, other])) * (xf[side, 0] - rmix[side, 0])
            + (float(D[other, mine]) * hx2[side]) * rx2[side, 0]
        )
    inner_low, inner_high = first * 0.5, last * 0.5
    keep_inner = [
        1.0 - (inner_low if t > 0 else 0.0) - (inner_high if t < 3 else 0.0)
        for t in range(4)
    ]

    def y_part(ref, offset, target, faces):
        coefficients = columns(offset)

        @loop(NX)
        def _(x):
            values = y_line(ref, x, coefficients)
            if faces is not None:
                faces[pl.ds(x, 1), :] = values[0][:1, :]
                faces[pl.ds(8 + x, 1), :] = values[3][7:, :]
            for t in range(4):
                value = values[t] * keep_inner[t]
                if t > 0:
                    value = value + pltpu.roll(values[t - 1], 1, 0) * inner_low
                if t < 3:
                    value = value + pltpu.roll(values[t + 1], 7, 0) * inner_high
                target[x, pl.ds(8 * t, 8), :] = value

    def x_part(ref, mx, target):
        @loop(4)
        def _(yt):
            src = tiles(ref, yt)
            for x in range(NX):
                target[x, y_rows(yt), :] += line(mx[x], src)

    def x_faces(source, mx, low, high):
        @loop(4)
        def _(yt):
            src = tiles(source, yt)
            low[y_rows(yt), :] = line(mx[0], src)
            high[y_rows(yt), :] = line(mx[NX - 1], src)

    def add_y(target, low, high):
        for x in range(NX):
            target[x, pl.ds(0, 8), :] += first * low[x : x + 1, :]
            target[x, pl.ds(NY - 8, 8), :] += last * high[x : x + 1, :]

    def add_z(target, delta_z):
        target[...] += cube(dot_tn(stack3(delta_z), zf[pl.ds(F_PICK, 48), :]))

    gradient_copies = {}

    def gradient(k):
        v = vec.at[k]
        parts = split3(flat(v[...]))
        gfz[k] = z_faces(parts, F_D)
        y_part(v, T_D, grad.at[k, 1], gfy.at[k])

        @loop(4)
        def _(yt):
            rows = y_rows(yt)
            src = tiles(v, yt)
            for x in range(NX):
                value = line(D[x], src)
                grad[k, 0, x, rows, :] = value
                if x in (0, NX - 1):
                    gfx[min(x, 1), k, rows, :] = value

        low, high = pl.ds(0, 8), pl.ds(8, 8)
        gradient_copies[k] = [
            send(gfx.at[0, k], grx.at[1, k], at_x(-1)),
            send(gfx.at[1, k], grx.at[0, k], at_x(1)),
            send(gfz.at[k, low], grz.at[k, high], at_z(-1)),
            send(gfz.at[k, high], grz.at[k, low], at_z(1)),
            send(gfy.at[k, low], gry.at[k, high], at_y(-1)),
            send(gfy.at[k, high], gry.at[k, low], at_y(1)),
        ]
        grad[k, 2] = z_line(parts, Z_DA)

    def gradient_edges(k):
        for copy in gradient_copies[k]:
            copy.wait_recv()
        for side in (0, 1):
            grad[k, 0, side * (NX - 1)] += hx[side] * (grx[side, k] - gfx[side, k])
        add_y(
            grad.at[k, 1],
            hy[0] * (gry[k, pl.ds(0, 8), :] - gfy[k, pl.ds(0, 8), :]),
            hy[1] * (gry[k, pl.ds(8, 8), :] - gfy[k, pl.ds(8, 8), :]),
        )
        add_z(grad.at[k, 2], 0.5 * (grz[k] - gfz[k]))

    far = []

    def phase(k, vx, vy, vz, mx, ycol, zmat, zface, with_mass, sign):
        x_faces(vx, mx, fx.at[k, 0], fx.at[k, 1])
        sx = []
        if k == 1:
            sx = [
                send(fx.at[k, 0], rx.at[k, 1], at_x(-1)),
                send(fx.at[k, 1], rx.at[k, 0], at_x(1)),
            ]
            far[:] = [
                send(fx.at[k, 0], rx2.at[1, 1], at_x(-2)),
                send(fx.at[k, 1], rx2.at[0, 1], at_x(2)),
            ]
        parts = split3(flat(vz[...]))
        fz[k] = z_faces(parts, zface)
        sz = [
            send(fz.at[k, pl.ds(0, 8)], rz.at[k, pl.ds(8, 8)], at_z(-1)),
            send(fz.at[k, pl.ds(8, 8)], rz.at[k, pl.ds(0, 8)], at_z(1)),
        ]
        y_part(vy, ycol, tt, fy.at[k])
        sy = [
            send(fy.at[k, pl.ds(0, 8)], ry.at[k, pl.ds(8, 8)], at_y(-1)),
            send(fy.at[k, pl.ds(8, 8)], ry.at[k, pl.ds(0, 8)], at_y(1)),
        ]
        if with_mass and k == 1:
            finish_penalty()
        rest = z_line(parts, zmat)
        if with_mass:
            rest = rest + pav[...] * vx[...]
        tt[...] += rest
        x_part(vx, mx, tt)
        if k > 1:
            gradient(k - 1)
        for copy in sy:
            copy.wait_recv()
        add_y(
            tt,
            hy[0] * (ry[k, pl.ds(0, 8), :] - fy[k, pl.ds(0, 8), :]),
            hy[1] * (ry[k, pl.ds(8, 8), :] - fy[k, pl.ds(8, 8), :]),
        )
        for copy in sz:
            copy.wait_recv()
        add_z(tt, 0.5 * (rz[k] - fz[k]))
        out = vec.at[k]
        for x in range(1, NX - 1):
            out[x] = tt[x] * (sign * wm[x])
        if k == 1:
            @loop(4)
            def _(yt):
                rows = y_rows(yt)
                src = [tt[0, rows, :] * wm[0, rows, :]]
                src += [out[x, rows, :] for x in range(1, NX - 1)]
                src += [tt[NX - 1, rows, :] * wm[NX - 1, rows, :]]
                weight = wyz[rows, :]
                below = fx[1, 0, rows, :] * weight * (2.0 * scale_x[0] * hx[0])
                above = fx[1, 1, rows, :] * weight * (2.0 * scale_x[-1] * hx[1])
                q2[0, rows, :] = line(L[0], src[:-1] + [src[-1] - above])
                q2[1, rows, :] = line(L[NX - 1], [src[0] - below] + src[1:])

            far[2:] = [
                send(q2.at[0], rq2.at[1], at_x(-1)),
                send(q2.at[1], rq2.at[0], at_x(1)),
            ]
            gradient(0)
        if k == 2:
            for copy in far:
                copy.wait_recv()
            for side in (0, 1):
                mine, other = side * (NX - 1), (1 - side) * (NX - 1)
                near_term = (scale_x[other] * float(L[other, other])) * (
                    fx[1, side] - rx[1, side]
                )
                far_term = (2.0 * scale_x[mine] * float(L[other, mine])) * hx2[side]
                rx[2, side] = rq2[side] + wyz[...] * (
                    near_term + far_term * rx2[side, 1]
                )
        for copy in sx:
            copy.wait_recv()
        out[0] = (tt[0] + hx[0] * (rx[k, 0] - fx[k, 0])) * (sign * wm[0])
        out[NX - 1] = (tt[NX - 1] + hx[1] * (rx[k, 1] - fx[k, 1])) * (sign * wm[NX - 1])

    def finish_penalty():
        for copy in copies_p:
            copy.wait_recv()
        for side in (0, 1):
            neighbour_face(side, 3)
            own = xf[side, 3]
            pav[side * (NX - 1)] = own + hx[side] * (rmix[side, 3] - own)

    phase(0, adv.at[0], adv.at[1], adv.at[2], D, T_D, Z_DA, F_D, False, -1.0)
    for k in (1, 2):
        v = vec.at[k - 1]
        phase(k, v, v, v, L, T_L, Z_LA, F_L, True, 1.0)

    def inner(a, b):
        total = None
        for yt in range(4):
            rows = pl.ds(8 * yt, 8)
            s = None
            for x in range(NX):
                p = a[x, rows, :] * b[x, rows, :]
                if x in (0, NX - 1):
                    p = p * inv_x[x]
                s = p if s is None else s + p
            s = s * im_y[yt]
            total = s if total is None else total + s
        return jnp.sum(total, axis=0, keepdims=True)

    v0, v1, v2 = vec.at[0], vec.at[1], vec.at[2]
    y_part(v2, T_L, tt, None)
    tt[...] += z_line(split3(flat(vec[2])), Z_LA) + pav[...] * v2[...]
    x_part(v2, L, tt)
    total = None
    for yt in range(4):
        rows = pl.ds(8 * yt, 8)
        s = None
        for x in range(NX):
            p = v2[x, rows, :] * tt[x, rows, :] * scale_x[x]
            s = p if s is None else s + p
        total = s if total is None else total + s
    mom[pl.ds(5, 1), :] = jnp.sum(total * w_tile, axis=0, keepdims=True)
    mom[pl.ds(0, 1), :] = inner(v0, v0)
    mom[pl.ds(1, 1), :] = inner(v0, v1)
    mom[pl.ds(2, 1), :] = inner(v1, v1)
    mom[pl.ds(3, 1), :] = inner(v1, v2)
    mom[pl.ds(4, 1), :] = inner(v2, v2)
    mom[pl.ds(6, 2), :] = jnp.zeros((2, NZ), F32)

    def spread(source, slots, own, group, which):
        slots[own] = source[...]
        for k in range(1, 16):
            copy = pltpu.make_async_remote_copy(
                src_ref=source,
                dst_ref=slots.at[own],
                send_sem=red_send.at[which, k],
                recv_sem=red_recv.at[which],
                device_id=group(k),
                device_id_type=MESH,
            )
            copy.start()
            pending.append(copy)

    def gather(slots, which):
        view = slots.at[pl.ds(0, 15)]
        pltpu.make_async_copy(view, view, red_recv.at[which]).wait()
        total = slots[0]
        for k in range(1, 16):
            total = total + slots[k]
        return total

    spread(mom, red1, index1, group1, 0)

    gradient(2)
    part[...] = gather(red1, 0)
    spread(part, red2, index2, group2, 1)
    for k in range(3):
        gradient_edges(k)

    outs = [
        pltpu.make_async_copy(adv, adv_out, out_sem.at[0]),
        pltpu.make_async_copy(grad, grad_out, out_sem.at[1]),
        pltpu.make_async_copy(vec, vec_out, out_sem.at[2]),
    ]
    for copy in outs:
        copy.start()
    sums = jnp.sum(gather(red2, 1), axis=1, keepdims=True)
    m = [jnp.broadcast_to(sums[k : k + 1, :], (8, NZ)) for k in range(6)]
    s0, s1, s2 = lax.rsqrt(m[1]), lax.rsqrt(m[3]), lax.rsqrt(m[5])
    h01 = m[2] * s0 * s1
    h02 = m[3] * s0 * s2
    h12 = m[4] * s1 * s2
    h00, h11, h22 = m[1] * s0 * s0, m[3] * s1 * s1, m[5] * s2 * s2
    g0, g1, g2 = m[0] * s0, m[1] * s1, m[2] * s2
    l10 = h01 / h00
    l20 = h02 / h00
    d1 = h11 - l10 * h01
    e1 = h12 - l20 * h01
    l21 = e1 / d1
    d2 = h22 - l20 * h02 - l21 * e1
    y0 = g0
    y1_ = g1 - l10 * y0
    y2_ = g2 - l20 * y0 - l21 * y1_
    c2 = y2_ / d2
    c1 = y1_ / d1 - l21 * c2
    c0 = y0 / h00 - l10 * c1 - l20 * c2
    c0, c1, c2 = c0 * s0, c1 * s1, c2 * s2

    coef[...] = jnp.where(sub == 0, c0, jnp.where(sub == 1, c1, c2))
    last_out = pltpu.make_async_copy(coef, coef_out, out_sem.at[3])
    last_out.start()
    for copy in pending:
        copy.wait_send()
    for copy in outs:
        copy.wait()
    last_out.wait()


PIECES = 4


def combine(
    adv_in,
    grad_in,
    vec_in,
    coef_in,
    projected,
    pressure,
    adv,
    grad,
    vec,
    coef,
    proj,
    pres,
    load_sem,
    coef_sem,
    out_sem,
):
    size = NX // PIECES
    coef_copy = pltpu.make_async_copy(coef_in, coef, coef_sem.at[0])
    coef_copy.start()
    loads, outs = [], []
    for k in range(PIECES):
        part = pl.ds(size * k, size)
        copies = [
            pltpu.make_async_copy(vec_in.at[:, part], vec.at[:, part], load_sem.at[k, 0]),
            pltpu.make_async_copy(adv_in.at[:, part], adv.at[:, part], load_sem.at[k, 1]),
            pltpu.make_async_copy(
                grad_in.at[:, :, part], grad.at[:, :, part], load_sem.at[k, 2]
            ),
        ]
        for copy in copies:
            copy.start()
        loads.append(copies)
    coef_copy.wait()
    c = [coef[pl.ds(k, 1), :] for k in range(3)]
    for k in range(PIECES):
        part = pl.ds(size * k, size)
        loads[k][0].wait()
        pres[part] = c[0] * vec[0, part] + c[1] * vec[1, part] + c[2] * vec[2, part]
        outs.append(pltpu.make_async_copy(pres.at[part], pressure.at[part], out_sem.at[k, 0]))
        outs[-1].start()
        for copy in loads[k][1:]:
            copy.wait()
        for i in range(3):
            proj[i, part] = adv[i, part] - (
                c[0] * grad[0, i, part] + c[1] * grad[1, i, part] + c[2] * grad[2, i, part]
            )
        outs.append(
            pltpu.make_async_copy(proj.at[:, part], projected.at[:, part], out_sem.at[k, 1])
        )
        outs[-1].start()
    for copy in outs:
        copy.wait()


def per_device(base_flow, adjoint_velocity, penalty):
    field = (NX, NY, NZ)
    v = lambda *shape: pltpu.VMEM(shape, F32)
    consts = [jnp.asarray(t) for t in tables()]
    any_spec = pl.BlockSpec(memory_space=pltpu.HBM)
    sends = 60
    adv, grad, vec, coef = pl.pallas_call(
        kernel,
        out_shape=(
            jax.ShapeDtypeStruct((3,) + field, F32),
            jax.ShapeDtypeStruct((3, 3) + field, F32),
            jax.ShapeDtypeStruct((3,) + field, F32),
            jax.ShapeDtypeStruct((8, NZ), F32),
        ),
        in_specs=[any_spec] * 6,
        out_specs=(any_spec,) * 4,
        scratch_shapes=[
            v(3, *field),
            v(3, *field),
            v(*field),
            pltpu.VMEM(consts[0].shape, jnp.bfloat16),
            pltpu.VMEM(consts[1].shape, jnp.bfloat16),
            v(*consts[2].shape),
            v(4, *field),
            v(4, *field),
            v(3, *field),
            v(*field),
            v(3, *field),
            v(*field),
            v(3, 3, *field),
            v(*field),
            v(NY, NZ),
            v(2, NY, NZ),
            v(2, NY, NZ),
            v(16, ROWS),
            v(2, 3, 8, ROWS),
            v(2, 4, 8, NZ),
            v(2, 4, 8, NZ),
            v(2, 4, NY, NZ),
            v(2, NY + 16, NZ),
            v(2, 4, NY, NZ),
            v(2, NY + 16, NZ),
            v(2, 2, NY, NZ),
            v(2, 4, NY, NZ),
            v(2, 4, NY, NZ),
            v(3, 2, NY, NZ),
            v(3, 2, NY, NZ),
            v(3, 16, NZ),
            v(3, 16, NZ),
            v(3, 16, ROWS),
            v(3, 16, ROWS),
            v(2, 3, NY, NZ),
            v(2, 3, NY, NZ),
            v(3, 16, NZ),
            v(3, 16, NZ),
            v(3, 16, ROWS),
            v(3, 16, ROWS),
            v(8, NZ),
            v(16, 8, NZ),
            v(8, NZ),
            v(16, 8, NZ),
            v(8, NZ),
            pltpu.SemaphoreType.DMA((7,)),
            pltpu.SemaphoreType.DMA((sends + 10,)),
            pltpu.SemaphoreType.DMA((sends + 10,)),
            pltpu.SemaphoreType.DMA((2, 16)),
            pltpu.SemaphoreType.DMA((2,)),
            pltpu.SemaphoreType.DMA((4,)),
        ],
        compiler_params=pltpu.CompilerParams(
            collective_id=0, has_side_effects=True, vmem_limit_bytes=63 * 1024 * 1024
        ),
        name="adjoint",
    )(base_flow, adjoint_velocity, penalty, *consts)
    return pl.pallas_call(
        combine,
        out_shape=(
            jax.ShapeDtypeStruct((3,) + field, F32),
            jax.ShapeDtypeStruct(field, F32),
        ),
        in_specs=[any_spec] * 4,
        out_specs=(any_spec,) * 2,
        scratch_shapes=[
            v(3, *field),
            v(3, 3, *field),
            v(3, *field),
            v(8, NZ),
            v(3, *field),
            v(*field),
            pltpu.SemaphoreType.DMA((PIECES, 3)),
            pltpu.SemaphoreType.DMA((1,)),
            pltpu.SemaphoreType.DMA((PIECES, 2)),
        ],
        compiler_params=pltpu.CompilerParams(vmem_limit_bytes=63 * 1024 * 1024),
        name="combine",
    )(adv, grad, vec, coef)


def solution(mesh):
    spec3 = P(None, "gx", "gy", "gz")
    spec1 = P("gx", "gy", "gz")
    return jax.shard_map(
        per_device,
        mesh=mesh,
        in_specs=(spec3, spec3, spec1),
        out_specs=(spec3, spec1),
        check_vma=False,
    )
```

```python
import functools

import jax
import jax.numpy as jnp
import ml_dtypes
import numpy as np
from jax import lax
from jax.experimental import pallas as pl
from jax.experimental.pallas import tpu as pltpu
from jax.sharding import PartitionSpec as P

MESH = pl.DeviceIdType.MESH
F32 = jnp.float32
N = 8
NX, NY, NZ = 8, 32, 128
ROWS = NX * NY
GX, GY, GZ = 8, 4, 8
PIECES = 4
NEAR = [(-1, 0, 0), (1, 0, 0)] + [
    (0, dy, dz) for dy in (-1, 1, 0) for dz in (-1, 1, 0) if (dy, dz) != (0, 0)
]


def gll_tables():
    points = 8
    nodes = np.array(
        [
            -1.0,
            -0.8717401485096066,
            -0.5917001814331423,
            -0.2092992179024789,
            0.2092992179024789,
            0.5917001814331423,
            0.8717401485096066,
            1.0,
        ]
    )
    previous = np.ones(points)
    current = np.array(nodes)
    for degree in range(1, points - 1):
        previous, current = (
            current,
            ((2 * degree + 1) * nodes * current - degree * previous) / (degree + 1),
        )
    weights = 2.0 / (points * (points - 1) * current**2)
    derivative = np.zeros((points, points))
    for target in range(points):
        for source in range(points):
            if target != source:
                derivative[target, source] = current[target] / (
                    current[source] * (nodes[target] - nodes[source])
                )
    derivative[0, 0] = -points * (points - 1) / 4.0
    derivative[points - 1, points - 1] = points * (points - 1) / 4.0
    return weights, derivative


W, D = gll_tables()
L = (D.T * W) @ D / W[:, None]


def average(extent):
    m = np.eye(extent)
    for k in range(8, extent, 8):
        m[k - 1, k - 1] = m[k, k] = m[k - 1, k] = m[k, k - 1] = 0.5
    return m


def along(matrix, extent):
    return np.kron(np.eye(extent // 8), matrix)


def face_rows_z(matrix):
    rows = np.zeros((16, NZ))
    full = along(matrix, NZ)
    rows[0] = full[0]
    rows[8] = full[NZ - 1]
    return rows


def split(matrix):
    parts, rest = [], np.asarray(matrix, np.float64)
    for _ in range(3):
        parts.append(rest.astype(np.float32).astype(ml_dtypes.bfloat16))
        rest = rest - parts[-1].astype(np.float64)
    return parts


def tables():
    az = average(NZ)
    blocks = []
    for matrix in (along(D, NZ), az @ along(D, NZ), az @ along(L, NZ)):
        high, mid, low = split(matrix.T)
        blocks.append(
            np.concatenate(
                [
                    np.concatenate([high, mid, high], axis=1),
                    np.concatenate([high, mid, low], axis=1),
                ],
                axis=0,
            )
        )
    z_blocks = np.stack(blocks)
    picks = np.zeros((16, NZ))
    picks[0, 0] = 1.0
    picks[8, NZ - 1] = 1.0
    z_faces = np.concatenate(
        split(face_rows_z(D))
        + split(face_rows_z(L))
        + [picks.astype(ml_dtypes.bfloat16)] * 3,
        axis=0,
    )
    local = np.arange(8)
    edge = np.where((local == 0) | (local == 7), 2.0, 1.0)
    wyz = W[:, None] * np.tile(W, 16)[None, :]
    myz = edge[:, None] * np.tile(edge, 16)[None, :]
    columns = [
        np.repeat(matrix[:, k : k + 1], NZ, axis=1)
        for matrix in (D, L)
        for k in range(8)
    ]
    small = np.concatenate([wyz, wyz * myz, 1.0 / myz] + columns, axis=0)
    return [z_blocks, z_faces, np.asarray(small, np.float32)]


Z_D, Z_DA, Z_LA = 0, 1, 2
F_D, F_L, F_PICK = 0, 48, 96
T_W, T_WM, T_IM, T_D, T_L = 0, 8, 16, 24, 88


def dot(a, b):
    return lax.dot_general(a, b, (((1,), (0,)), ((), ())), preferred_element_type=F32)


def dot_nt(a, b):
    return lax.dot_general(a, b, (((1,), (1,)), ((), ())), preferred_element_type=F32)


def dot_tn(a, b):
    return lax.dot_general(a, b, (((0,), (0,)), ((), ())), preferred_element_type=F32)


def split3(value):
    high = value.astype(jnp.bfloat16)
    rest = value - high.astype(F32)
    mid = rest.astype(jnp.bfloat16)
    return high, mid, (rest - mid.astype(F32)).astype(jnp.bfloat16)


def stack3(value):
    parts, rest = [], value
    for _ in range(3):
        parts.append(rest.astype(jnp.bfloat16).astype(F32))
        rest = rest - parts[-1]
    return jnp.concatenate(parts, axis=0).astype(jnp.bfloat16)


def flat(value):
    return value.reshape(ROWS, NZ)


def cube(value):
    return value.reshape(NX, NY, NZ)


def line(matrix_row, tiles):
    total = None
    for coefficient, tile in zip(matrix_row, tiles):
        part = tile * float(np.float32(coefficient))
        total = part if total is None else total + part
    return total


def kernel(
    base,
    adj,
    pen,
    zblocks,
    zfaces,
    small,
    projected,
    pressure,
    bs,
    us,
    ps,
    zb,
    zf,
    zt,
    raw,
    halo,
    adv,
    pav,
    vec,
    tt,
    grad,
    wm,
    wyz,
    q2,
    rq2,
    fz1,
    rz1,
    fy1,
    ry1,
    xf,
    xq,
    rx1,
    rq1,
    rx2,
    hx1,
    rmix,
    fx,
    rx,
    fy,
    ry,
    fz,
    rz,
    gfx,
    grx,
    gfy,
    gry,
    gfz,
    grz,
    mom,
    red1,
    part,
    red2,
    res,
    load_sem,
    send_sem,
    recv_sem,
    red_send,
    red_recv,
    out_sem,
):
    px = lax.axis_index("gx")
    py = lax.axis_index("gy")
    pz = lax.axis_index("gz")

    def at(dx, dy, dz):
        return (
            lax.rem(px + dx + GX, GX),
            lax.rem(py + dy + GY, GY),
            lax.rem(pz + dz + GZ, GZ),
        )

    def at_x(offset):
        return at(offset, 0, 0)

    def at_y(offset):
        return at(0, offset, 0)

    def at_z(offset):
        return at(0, 0, offset)

    row = px // 2
    half = lax.rem(px, 2)
    index1 = half * 8 + pz
    index2 = row * 4 + py

    def group1(k):
        i = lax.rem(index1 + k, 16)
        return (row * 2 + i // 8, py, lax.rem(i, 8))

    def group2(k):
        i = lax.rem(index2 + k, 16)
        return ((i // 4) * 2 + half, lax.rem(i, 4), pz)

    loads = [
        pltpu.make_async_copy(adj, us, load_sem.at[0]),
        pltpu.make_async_copy(base, bs, load_sem.at[1]),
        pltpu.make_async_copy(zblocks.at[0], zb.at[0], load_sem.at[2]),
        pltpu.make_async_copy(small, zt, load_sem.at[3]),
        pltpu.make_async_copy(zfaces, zf, load_sem.at[4]),
        pltpu.make_async_copy(pen, ps, load_sem.at[5]),
        pltpu.make_async_copy(
            zblocks.at[pl.ds(1, 2)], zb.at[pl.ds(1, 2)], load_sem.at[6]
        ),
    ]
    for copy in loads:
        copy.start()

    barrier = pltpu.get_barrier_semaphore()
    for dx, dy, dz in NEAR:
        pl.semaphore_signal(
            barrier, inc=1, device_id=at(dx, dy, dz), device_id_type=MESH
        )
    mates1 = [group1(k) for k in range(1, 16)]
    mates2 = [group2(k) for k in range(1, 16)]
    for mate in mates1 + mates2:
        pl.semaphore_signal(barrier, inc=1, device_id=mate, device_id_type=MESH)

    hx = (jnp.where(px > 0, 0.5, 0.0), jnp.where(px < GX - 1, 0.5, 0.0))
    hy = (jnp.where(py > 0, 0.5, 0.0), jnp.where(py < GY - 1, 0.5, 0.0))
    hx2 = (jnp.where(px > 1, 0.5, 0.0), jnp.where(px < GX - 2, 0.5, 0.0))
    sub = lax.broadcasted_iota(jnp.int32, (8, NZ), 0)
    first = jnp.where(sub == 0, 1.0, 0.0)
    last = jnp.where(sub == 7, 1.0, 0.0)

    pending = []
    counter = [0]

    def send(src, dst, device):
        k = counter[0]
        counter[0] += 1
        copy = pltpu.make_async_remote_copy(
            src_ref=src,
            dst_ref=dst,
            send_sem=send_sem.at[k],
            recv_sem=recv_sem.at[k],
            device_id=device,
            device_id_type=MESH,
        )
        copy.start()
        pending.append(copy)
        return copy

    for copy in loads[:4]:
        copy.wait()

    def y_rows(yt):
        return pl.ds(8 * yt, 8)

    def tiles(ref, yt):
        return [ref[x, y_rows(yt), :] for x in range(NX)]

    def loop(count, start=0):
        def run(body):
            for k in range(start, count):
                body(k)

        return run

    def columns(offset):
        return [zt[pl.ds(offset + 8 * k, 8), :] for k in range(8)]

    def y_line(ref, x, coefficients):
        result = []
        for t in range(4):
            total = None
            for k in range(8):
                part = coefficients[k] * ref[x, pl.ds(8 * t + k, 1), :]
                total = part if total is None else total + part
            result.append(total)
        return result

    def z_line(parts, block):
        high, mid, low = parts
        out = dot(
            jnp.concatenate([high, mid], axis=1), zb[block, :, pl.ds(0, 2 * NZ)]
        )
        rest = dot(
            jnp.concatenate([low, high], axis=1), zb[block, :, pl.ds(2 * NZ, NZ)]
        )
        return cube(out[:, :NZ] + (out[:, NZ:] + rest))

    d_columns = columns(T_D)
    for i in range(3):
        raw[i] = -bs[2] * z_line(split3(flat(us[i])), Z_D)
    for j in range(3):
        raw[2] += us[j] * z_line(split3(flat(bs[j])), Z_D)

    @loop(NX)
    def _(x):
        for i in range(3):
            for t, value in enumerate(y_line(us.at[i], x, d_columns)):
                rows = pl.ds(8 * t, 8)
                raw[i, x, rows, :] -= bs[1, x, rows, :] * value
        for j in range(3):
            for t, value in enumerate(y_line(bs.at[j], x, d_columns)):
                rows = pl.ds(8 * t, 8)
                raw[1, x, rows, :] += us[j, x, rows, :] * value

    @loop(4)
    def _(yt):
        rows = y_rows(yt)
        for i in range(3):
            src = tiles(us.at[i], yt)
            for x in range(NX):
                raw[i, x, rows, :] -= bs[0, x, rows, :] * line(D[x], src)
        for j in range(3):
            src = tiles(bs.at[j], yt)
            for x in range(NX):
                raw[0, x, rows, :] += us[j, x, rows, :] * line(D[x], src)

    for copy in loads[4:6]:
        copy.wait()
    raw[3] = ps[...]
    def z_faces(parts, offset):
        high, mid, low = parts
        table = zf[pl.ds(offset, 48), :]
        a, b = dot_nt(table, high), dot_nt(table[:32], mid)
        c = dot_nt(table[:16], low)
        return a[:16] + (a[16:32] + b[:16] + (a[32:] + b[16:] + c))

    def z_ends(parts):
        table = zf[pl.ds(F_PICK, 16), :]
        a, b, c = (dot_nt(table, part) for part in parts)
        return a + (b + c)

    faces = None
    for i in range(4):
        own = z_ends(split3(flat(raw[i])))
        faces = own if i == 0 else faces + pltpu.roll(own, i, 0)
    fz1[...] = faces
    for i in range(4):
        for x in range(NX):
            for side, y in ((0, 0), (1, NY - 1)):
                fy1[side, i, pl.ds(x, 1), :] = raw[i, x, pl.ds(y, 1), :]
    pl.semaphore_wait(barrier, 30 + len(NEAR))
    near = []
    for dz in (-1, 1):
        for dy in (0, -1, 1):
            src = fz1.at[pl.ds(0 if dz < 0 else 8, 4)]
            dst = rz1.at[1 if dz < 0 else 0, 1 - dy, pl.ds(0, 4)]
            near.append(send(src, dst, at(0, dy, dz)))
    near += [
        send(fy1.at[0], ry1.at[1], at_y(-1)),
        send(fy1.at[1], ry1.at[0], at_y(1)),
    ]
    raw_x = [
        send(raw.at[pl.ds(0, 3), 0], rx1.at[1, pl.ds(0, 3)], at_x(-1)),
        send(raw.at[pl.ds(0, 3), NX - 1], rx1.at[0, pl.ds(0, 3)], at_x(1)),
    ]
    w_tile = zt[pl.ds(T_W, 8), :]
    wm_tile = zt[pl.ds(T_WM, 8), :]
    im_tile = zt[pl.ds(T_IM, 8), :]
    fix_low = 1.0 - first * (0.5 - hy[0])
    fix_high = 1.0 - last * (0.5 - hy[1])
    inv_low = 1.0 + first * (1.0 - 2.0 * hy[0])
    inv_high = 1.0 + last * (1.0 - 2.0 * hy[1])
    wm_y = [wm_tile * fix_low, wm_tile, wm_tile, wm_tile * fix_high]
    im_y = [im_tile * inv_low, im_tile, im_tile, im_tile * inv_high]
    scale_x = [float(w) for w in W]
    mult_x = [1.0 + 2.0 * hx[0]] + [1.0] * 6 + [1.0 + 2.0 * hx[1]]
    inv_x = [1.0 - hx[0]] + [1.0] * 6 + [1.0 - hx[1]]
    for yt in range(4):
        for x in range(NX):
            wm[x, pl.ds(8 * yt, 8), :] = wm_y[yt] * (mult_x[x] * scale_x[x])
        wyz[pl.ds(8 * yt, 8), :] = wm_y[yt]

    lane = lax.broadcasted_iota(jnp.int32, (8, NZ), 1)
    begin = lax.rem(lane, 8) == 0
    end = lax.rem(lane, 8) == 7
    keep_z = jnp.where(begin | end, 0.5, 1.0)
    from_low = jnp.where(begin & (lane > 0), 0.5, 0.0)
    from_high = jnp.where(end & (lane < NZ - 1), 0.5, 0.0)
    low_y = [first * hy[0]] + [first * 0.5] * 3
    high_y = [last * 0.5] * 3 + [last * hy[1]]
    keep_y = [1.0 - low_y[t] - high_y[t] for t in range(4)]

    def mix_slab(src, low, high, edge, dst):
        for t in range(4):
            rows = pl.ds(8 * t, 8)
            down = low if t == 0 else src[pl.ds(8 * t - 1, 1), :]
            up = high if t == 3 else src[pl.ds(8 * t + 8, 1), :]
            value = src[rows, :] * keep_y[t] + down * low_y[t] + up * high_y[t]
            dst[rows, :] = (
                value * keep_z
                + pltpu.roll(value, 1, 1) * from_low
                + pltpu.roll(value, NZ - 1, 1) * from_high
                + edge[rows, :]
            )

    wide = lax.broadcasted_iota(jnp.int32, (8, ROWS), 1)
    y_of = lax.rem(wide, NY)
    x_of = wide // NY
    inner_begin = (lax.rem(wide, 8) == 0) & (y_of > 0)
    inner_end = (lax.rem(wide, 8) == 7) & (y_of < NY - 1)

    def y_mix(mid, down, up):
        partner = jnp.where(
            y_of == 0,
            pltpu.roll(down, ROWS - (NY - 1), 1),
            jnp.where(
                y_of == NY - 1,
                pltpu.roll(up, NY - 1, 1),
                jnp.where(
                    inner_begin, pltpu.roll(mid, 1, 1), pltpu.roll(mid, ROWS - 1, 1)
                ),
            ),
        )
        weight = jnp.where(
            y_of == 0,
            hy[0],
            jnp.where(
                y_of == NY - 1, hy[1], jnp.where(inner_begin | inner_end, 0.5, 0.0)
            ),
        )
        return mid + weight * (partner - mid)

    spots = jnp.concatenate(
        [
            jnp.where((sub == i) & (lane == 0), 0.5, 0.0)
            + jnp.where((sub == 4 + i) & (lane == NZ - 1), 0.5, 0.0)
            for i in range(4)
        ],
        axis=1,
    ).astype(F32)
    spots = jnp.concatenate([spots] * 3, axis=0).astype(jnp.bfloat16)

    def expand(values):
        return dot_tn(stack3(values), spots)

    for copy in near:
        copy.wait_recv()
    edges = jnp.where(
        lax.broadcasted_iota(jnp.int32, (8, ROWS), 0) < 4,
        y_mix(rz1[0, 1], rz1[0, 0], rz1[0, 2]),
        pltpu.roll(y_mix(rz1[1, 1], rz1[1, 0], rz1[1, 2]), 4, 0),
    )
    wide_halo = expand(edges)
    for i in range(4):
        halo[i] = cube(wide_halo[:, NZ * i : NZ * (i + 1)])
    for side in (0, 1):
        for i in range(4):
            for end in (0, 1):
                xq[side, pl.ds(NY + 4 * end + i, 1), :] = ry1[
                    end, i, pl.ds(side * (NX - 1), 1), :
                ]
        xq[side, pl.ds(NY + 8, 8), :] = edges[:, NZ * side : NZ * (side + 1)]

    def mixed(i, x, dst):
        mix_slab(
            raw.at[i, x],
            ry1[0, i, pl.ds(x, 1), :],
            ry1[1, i, pl.ds(x, 1), :],
            halo.at[i, x],
            dst,
        )

    for side in (0, 1):
        mixed(0, side * (NX - 1), xf.at[side, 0])
    @loop(NX - 1, 1)
    def _(x):
        mixed(0, x, adv.at[0, x])

    @loop(4)
    def _(yt):
        rows = y_rows(yt)
        src = [xf[0, 0, rows, :]]
        src += [adv[0, x, rows, :] for x in range(1, NX - 1)]
        src += [xf[1, 0, rows, :]]
        ends = [src[0] * (1.0 - hx[0]), src[NX - 1] * (1.0 - hx[1])]
        xq[0, rows, :] = line(D[0], src[: NX - 1] + [ends[1]])
        xq[1, rows, :] = line(D[NX - 1], [ends[0]] + src[1:])

    sx = [
        send(xq.at[0], rq1.at[1], at_x(-1)),
        send(xq.at[1], rq1.at[0], at_x(1)),
        send(xf.at[0, 0], rx2.at[1, 0], at_x(-2)),
        send(xf.at[1, 0], rx2.at[0, 0], at_x(2)),
    ]
    copies_p = [
        send(raw.at[3, 0], rx1.at[1, 3], at_x(-1)),
        send(raw.at[3, NX - 1], rx1.at[0, 3], at_x(1)),
    ]
    for i in range(1, 4):
        for side in (0, 1):
            mixed(i, side * (NX - 1), xf.at[side, i])

    @loop(NX - 1, 1)
    def _(x):
        for i in range(1, 3):
            mixed(i, x, adv.at[i, x])
        mixed(3, x, pav.at[x])

    loads[6].wait()
    for copy in raw_x:
        copy.wait_recv()
    for copy in sx:
        copy.wait_recv()
    edges = jnp.where(lane < NZ // 2, rq1[1, pl.ds(NY + 8, 8), :], rq1[0, pl.ds(NY + 8, 8), :])
    wide_halo = expand(edges)
    for i in range(4):
        part_halo = wide_halo[:, NZ * i : NZ * (i + 1)]
        hx1[0, i] = part_halo[NZ - NY :, :]
        hx1[1, i] = part_halo[:NY, :]

    def neighbour_face(side, i):
        mix_slab(
            rx1.at[side, i],
            rq1[side, pl.ds(NY + i, 1), :],
            rq1[side, pl.ds(NY + 4 + i, 1), :],
            hx1.at[side, i],
            rmix.at[side, i],
        )

    for i in range(3):
        for side in (0, 1):
            neighbour_face(side, i)
            own = xf[side, i]
            adv[i, side * (NX - 1)] = own + hx[side] * (rmix[side, i] - own)
    for side in (0, 1):
        mine, other = side * (NX - 1), (1 - side) * (NX - 1)
        rx[0, side] = (
            rq1[side, pl.ds(0, NY), :]
            + (0.5 * float(D[other, other])) * (xf[side, 0] - rmix[side, 0])
            + (float(D[other, mine]) * hx2[side]) * rx2[side, 0]
        )
    inner_low, inner_high = first * 0.5, last * 0.5
    keep_inner = [
        1.0 - (inner_low if t > 0 else 0.0) - (inner_high if t < 3 else 0.0)
        for t in range(4)
    ]

    def y_part(ref, offset, target, faces):
        coefficients = columns(offset)

        @loop(NX)
        def _(x):
            values = y_line(ref, x, coefficients)
            if faces is not None:
                faces[0, pl.ds(x, 1), :] = values[0][:1, :]
                faces[1, pl.ds(x, 1), :] = values[3][7:, :]
            for t in range(4):
                value = values[t] * keep_inner[t]
                if t > 0:
                    value = value + pltpu.roll(values[t - 1], 1, 0) * inner_low
                if t < 3:
                    value = value + pltpu.roll(values[t + 1], 7, 0) * inner_high
                target[x, pl.ds(8 * t, 8), :] = value

    def x_part(ref, mx, target):
        @loop(4)
        def _(yt):
            src = tiles(ref, yt)
            for x in range(NX):
                target[x, y_rows(yt), :] += line(mx[x], src)

    def x_faces(source, mx, low, high):
        @loop(4)
        def _(yt):
            src = tiles(source, yt)
            low[y_rows(yt), :] = line(mx[0], src)
            high[y_rows(yt), :] = line(mx[NX - 1], src)

    def add_y(target, low, high):
        for x in range(NX):
            target[x, pl.ds(0, 8), :] += first * low[x : x + 1, :]
            target[x, pl.ds(NY - 8, 8), :] += last * high[x : x + 1, :]

    def add_z(target, delta_z):
        target[...] += cube(dot_tn(stack3(delta_z), zf[pl.ds(F_PICK, 48), :]))

    def gradient(k):
        v = vec.at[k]
        parts = split3(flat(v[...]))
        ends = z_faces(parts, F_D)
        if k == 0:
            gfz[...] = ends
        else:
            gfz[...] += pltpu.roll(ends, k, 0)
        y_part(v, T_D, grad.at[k, 1], gfy.at[:, k])

        @loop(4)
        def _(yt):
            rows = y_rows(yt)
            src = tiles(v, yt)
            for x in range(NX):
                value = line(D[x], src)
                grad[k, 0, x, rows, :] = value
                if x in (0, NX - 1):
                    gfx[min(x, 1), k, rows, :] = value

        grad[k, 2] = z_line(parts, Z_DA)

    def gradient_edges():
        delta = grz[...] - gfz[...]
        wide_halo = expand(delta[:8] + pltpu.roll(delta[8:], 4, 0))
        for k in range(3):
            for side in (0, 1):
                grad[k, 0, side * (NX - 1)] += hx[side] * (grx[side, k] - gfx[side, k])
            add_y(
                grad.at[k, 1],
                hy[0] * (gry[0, k] - gfy[0, k]),
                hy[1] * (gry[1, k] - gfy[1, k]),
            )
            grad[k, 2] += cube(wide_halo[:, NZ * k : NZ * (k + 1)])

    def inner(a, b):
        total = None
        for yt in range(4):
            rows = pl.ds(8 * yt, 8)
            s = None
            for x in range(NX):
                p = a[x, rows, :] * b[x, rows, :]
                if x in (0, NX - 1):
                    p = p * inv_x[x]
                s = p if s is None else s + p
            s = s * im_y[yt]
            total = s if total is None else total + s
        return jnp.sum(total, axis=0, keepdims=True)

    end_rows = lax.rem(lax.broadcasted_iota(jnp.int32, (16, ROWS), 0), 8) == 0
    far = []

    def phase(k, vx, vy, vz, mx, ycol, zmat, zface, with_mass, sign):
        parts = split3(flat(vz[...]))
        fz[k] = z_faces(parts, zface)
        sz = [
            send(fz.at[k, pl.ds(0, 1)], rz.at[k, pl.ds(8, 1)], at_z(-1)),
            send(fz.at[k, pl.ds(8, 1)], rz.at[k, pl.ds(0, 1)], at_z(1)),
        ]
        x_faces(vx, mx, fx.at[k, 0], fx.at[k, 1])
        sx = []
        if k == 1:
            sx = [
                send(fx.at[k, 0], rx.at[k, 1], at_x(-1)),
                send(fx.at[k, 1], rx.at[k, 0], at_x(1)),
            ]
        y_part(vy, ycol, tt, fy.at[k])
        sy = [
            send(fy.at[k, 0], ry.at[k, 1], at_y(-1)),
            send(fy.at[k, 1], ry.at[k, 0], at_y(1)),
        ]
        if with_mass and k == 1:
            finish_penalty()
        if k == 1:
            far[:] = [
                send(fx.at[k, 0], rx2.at[1, 1], at_x(-2)),
                send(fx.at[k, 1], rx2.at[0, 1], at_x(2)),
            ]
        rest = z_line(parts, zmat)
        if with_mass:
            rest = rest + pav[...] * vx[...]
        tt[...] += rest
        x_part(vx, mx, tt)
        if k == 2:
            gradient(1)
            mom[pl.ds(0, 1), :] = inner(vec.at[0], vec.at[0])
            mom[pl.ds(1, 1), :] = inner(vec.at[0], vec.at[1])
            mom[pl.ds(2, 1), :] = inner(vec.at[1], vec.at[1])
            mom[pl.ds(6, 2), :] = jnp.zeros((2, NZ), F32)
        for copy in sy:
            copy.wait_recv()
        add_y(
            tt,
            hy[0] * (ry[k, 0] - fy[k, 0]),
            hy[1] * (ry[k, 1] - fy[k, 1]),
        )
        for copy in sz:
            copy.wait_recv()
        add_z(tt, jnp.where(end_rows, 0.5 * (rz[k] - fz[k]), 0.0))
        out = vec.at[k]
        for x in range(1, NX - 1):
            out[x] = tt[x] * (sign * wm[x])
        if k == 1:
            @loop(4)
            def _(yt):
                rows = y_rows(yt)
                src = [tt[0, rows, :] * wm[0, rows, :]]
                src += [out[x, rows, :] for x in range(1, NX - 1)]
                src += [tt[NX - 1, rows, :] * wm[NX - 1, rows, :]]
                weight = wyz[rows, :]
                below = fx[1, 0, rows, :] * weight * (2.0 * scale_x[0] * hx[0])
                above = fx[1, 1, rows, :] * weight * (2.0 * scale_x[-1] * hx[1])
                q2[0, rows, :] = line(L[0], src[:-1] + [src[-1] - above])
                q2[1, rows, :] = line(L[NX - 1], [src[0] - below] + src[1:])

            far[2:] = [
                send(q2.at[0], rq2.at[1], at_x(-1)),
                send(q2.at[1], rq2.at[0], at_x(1)),
            ]
            gradient(0)
        if k == 2:
            for copy in far:
                copy.wait_recv()
            for side in (0, 1):
                mine, other = side * (NX - 1), (1 - side) * (NX - 1)
                near_term = (scale_x[other] * float(L[other, other])) * (
                    fx[1, side] - rx[1, side]
                )
                far_term = (2.0 * scale_x[mine] * float(L[other, mine])) * hx2[side]
                rx[2, side] = rq2[side] + wyz[...] * (
                    near_term + far_term * rx2[side, 1]
                )
        for copy in sx:
            copy.wait_recv()
        out[0] = (tt[0] + hx[0] * (rx[k, 0] - fx[k, 0])) * (sign * wm[0])
        out[NX - 1] = (tt[NX - 1] + hx[1] * (rx[k, 1] - fx[k, 1])) * (sign * wm[NX - 1])

    def finish_penalty():
        for copy in copies_p:
            copy.wait_recv()
        for side in (0, 1):
            neighbour_face(side, 3)
            own = xf[side, 3]
            pav[side * (NX - 1)] = own + hx[side] * (rmix[side, 3] - own)

    phase(0, adv.at[0], adv.at[1], adv.at[2], D, T_D, Z_DA, F_D, False, -1.0)
    for k in (1, 2):
        v = vec.at[k - 1]
        phase(k, v, v, v, L, T_L, Z_LA, F_L, True, 1.0)

    v0, v1, v2 = vec.at[0], vec.at[1], vec.at[2]
    y_part(v2, T_L, tt, None)
    tt[...] += z_line(split3(flat(vec[2])), Z_LA) + pav[...] * v2[...]
    x_part(v2, L, tt)
    total = None
    for yt in range(4):
        rows = pl.ds(8 * yt, 8)
        s = None
        for x in range(NX):
            p = v2[x, rows, :] * tt[x, rows, :] * scale_x[x]
            s = p if s is None else s + p
        total = s if total is None else total + s
    mom[pl.ds(5, 1), :] = jnp.sum(total * w_tile, axis=0, keepdims=True)
    mom[pl.ds(3, 1), :] = inner(v1, v2)
    mom[pl.ds(4, 1), :] = inner(v2, v2)

    def spread(source, slots, own, mates, which):
        slots[own] = source[...]
        for mate in mates:
            pltpu.make_async_remote_copy(
                src_ref=source,
                dst_ref=slots.at[own],
                send_sem=red_send.at[which],
                recv_sem=red_recv.at[which],
                device_id=mate,
                device_id_type=MESH,
            ).start()

    def wait_all(slots, semaphore):
        view = slots.at[pl.ds(0, 15)]
        pltpu.make_async_copy(view, view, semaphore).wait()

    def gather(slots, which):
        wait_all(slots, red_recv.at[which])
        total = slots[0]
        for k in range(1, 16):
            total = total + slots[k]
        return total

    spread(mom, red1, index2, mates2, 0)

    gradient(2)
    gradient_copies = [
        send(gfx.at[0], grx.at[1], at_x(-1)),
        send(gfx.at[1], grx.at[0], at_x(1)),
        send(gfz.at[pl.ds(0, 8)], grz.at[pl.ds(8, 8)], at_z(-1)),
        send(gfz.at[pl.ds(8, 8)], grz.at[pl.ds(0, 8)], at_z(1)),
        send(gfy.at[0], gry.at[1], at_y(-1)),
        send(gfy.at[1], gry.at[0], at_y(1)),
    ]
    part[...] = gather(red1, 0)
    spread(part, red2, index1, mates1, 1)
    for copy in gradient_copies:
        copy.wait_recv()
    gradient_edges()

    for copy in pending:
        copy.wait_send()
    wait_all(red1, red_send.at[0])
    sums = jnp.sum(gather(red2, 1), axis=1, keepdims=True)
    m = [jnp.broadcast_to(sums[k : k + 1, :], (8, NZ)) for k in range(6)]
    s0, s1, s2 = lax.rsqrt(m[1]), lax.rsqrt(m[3]), lax.rsqrt(m[5])
    h01 = m[2] * s0 * s1
    h02 = m[3] * s0 * s2
    h12 = m[4] * s1 * s2
    h00, h11, h22 = m[1] * s0 * s0, m[3] * s1 * s1, m[5] * s2 * s2
    g0, g1, g2 = m[0] * s0, m[1] * s1, m[2] * s2
    l10 = h01 / h00
    l20 = h02 / h00
    d1 = h11 - l10 * h01
    e1 = h12 - l20 * h01
    l21 = e1 / d1
    d2 = h22 - l20 * h02 - l21 * e1
    y0 = g0
    y1_ = g1 - l10 * y0
    y2_ = g2 - l20 * y0 - l21 * y1_
    c2 = y2_ / d2
    c1 = y1_ / d1 - l21 * c2
    c0 = y0 / h00 - l10 * c1 - l20 * c2
    c0, c1, c2 = c0 * s0, c1 * s1, c2 * s2

    c0, c1, c2 = c0[:1], c1[:1], c2[:1]
    outs = []
    for k in range(PIECES):
        slabs = pl.ds(k * (NX // PIECES), NX // PIECES)
        tt[slabs] = c0 * v0[slabs] + c1 * v1[slabs] + c2 * v2[slabs]
        outs.append(
            pltpu.make_async_copy(tt.at[slabs], pressure.at[slabs], out_sem.at[k, 0])
        )
        outs[-1].start()
        for i in range(3):
            res[i, slabs] = adv[i, slabs] - (
                c0 * grad[0, i, slabs] + c1 * grad[1, i, slabs] + c2 * grad[2, i, slabs]
            )
        outs.append(
            pltpu.make_async_copy(
                res.at[:, slabs], projected.at[:, slabs], out_sem.at[k, 1]
            )
        )
        outs[-1].start()
    wait_all(red2, red_send.at[1])
    for copy in outs:
        copy.wait()


def hand_on(projected_in, pressure_in, projected, pressure, proj, pres, load_sem, sem):
    loads, outs = [], []
    for k in range(PIECES):
        slabs = pl.ds(k * (NX // PIECES), NX // PIECES)
        for i, (source, held, target) in enumerate(
            [
                (projected_in.at[:, slabs], proj.at[:, slabs], projected.at[:, slabs]),
                (pressure_in.at[slabs], pres.at[slabs], pressure.at[slabs]),
            ]
        ):
            loads.append(pltpu.make_async_copy(source, held, load_sem.at[k, i]))
            outs.append(pltpu.make_async_copy(held, target, sem.at[k, i]))
    for copy in loads:
        copy.start()
    for load, out in zip(loads, outs):
        load.wait()
        out.start()
    for copy in outs:
        copy.wait()


def per_device(base_flow, adjoint_velocity, penalty):
    field = (NX, NY, NZ)
    v = lambda *shape: pltpu.VMEM(shape, F32)
    consts = [jnp.asarray(t) for t in tables()]
    any_spec = pl.BlockSpec(memory_space=pltpu.HBM)
    sends = 60
    shapes = (
        jax.ShapeDtypeStruct((3,) + field, F32),
        jax.ShapeDtypeStruct(field, F32),
    )
    results = pl.pallas_call(
        kernel,
        out_shape=shapes,
        in_specs=[any_spec] * 6,
        out_specs=(any_spec,) * 2,
        scratch_shapes=[
            v(3, *field),
            v(3, *field),
            v(*field),
            pltpu.VMEM(consts[0].shape, jnp.bfloat16),
            pltpu.VMEM(consts[1].shape, jnp.bfloat16),
            v(*consts[2].shape),
            v(4, *field),
            v(4, *field),
            v(3, *field),
            v(*field),
            v(3, *field),
            v(*field),
            v(3, 3, *field),
            v(*field),
            v(NY, NZ),
            v(2, NY, NZ),
            v(2, NY, NZ),
            v(16, ROWS),
            v(2, 3, 8, ROWS),
            v(2, 4, 8, NZ),
            v(2, 4, 8, NZ),
            v(2, 4, NY, NZ),
            v(2, NY + 16, NZ),
            v(2, 4, NY, NZ),
            v(2, NY + 16, NZ),
            v(2, 2, NY, NZ),
            v(2, 4, NY, NZ),
            v(2, 4, NY, NZ),
            v(3, 2, NY, NZ),
            v(3, 2, NY, NZ),
            v(3, 2, 8, NZ),
            v(3, 2, 8, NZ),
            v(3, 16, ROWS),
            v(3, 16, ROWS),
            v(2, 3, NY, NZ),
            v(2, 3, NY, NZ),
            v(2, 3, 8, NZ),
            v(2, 3, 8, NZ),
            v(16, ROWS),
            v(16, ROWS),
            v(8, NZ),
            v(16, 8, NZ),
            v(8, NZ),
            v(16, 8, NZ),
            v(3, *field),
            pltpu.SemaphoreType.DMA((7,)),
            pltpu.SemaphoreType.DMA((sends + 10,)),
            pltpu.SemaphoreType.DMA((sends + 10,)),
            pltpu.SemaphoreType.DMA((2,)),
            pltpu.SemaphoreType.DMA((2,)),
            pltpu.SemaphoreType.DMA((PIECES, 2)),
        ],
        compiler_params=pltpu.CompilerParams(
            collective_id=0, has_side_effects=True, vmem_limit_bytes=63 * 1024 * 1024
        ),
        name="adjoint",
    )(base_flow, adjoint_velocity, penalty, *consts)
    return pl.pallas_call(
        hand_on,
        out_shape=shapes,
        in_specs=[any_spec] * 2,
        out_specs=(any_spec,) * 2,
        scratch_shapes=[
            v(3, *field),
            v(*field),
            pltpu.SemaphoreType.DMA((PIECES, 2)),
            pltpu.SemaphoreType.DMA((PIECES, 2)),
        ],
        compiler_params=pltpu.CompilerParams(vmem_limit_bytes=63 * 1024 * 1024),
        name="hand_on",
    )(*results)


def solution(mesh):
    spec3 = P(None, "gx", "gy", "gz")
    spec1 = P("gx", "gy", "gz")
    return jax.shard_map(
        per_device,
        mesh=mesh,
        in_specs=(spec3, spec3, spec1),
        out_specs=(spec3, spec1),
        check_vma=False,
    )
```

```python
import functools

import jax
import jax.numpy as jnp
import ml_dtypes
import numpy as np
from jax import lax
from jax.experimental import pallas as pl
from jax.experimental.pallas import tpu as pltpu
from jax.sharding import PartitionSpec as P

MESH = pl.DeviceIdType.MESH
F32 = jnp.float32
N = 8
NX, NY, NZ = 8, 32, 128
ROWS = NX * NY
GX, GY, GZ = 8, 4, 8
PIECES = 4
NEAR = [(-1, 0, 0), (1, 0, 0)] + [
    (0, dy, dz) for dy in (-1, 1, 0) for dz in (-1, 1, 0) if (dy, dz) != (0, 0)
]


def gll_tables():
    points = 8
    nodes = np.array(
        [
            -1.0,
            -0.8717401485096066,
            -0.5917001814331423,
            -0.2092992179024789,
            0.2092992179024789,
            0.5917001814331423,
            0.8717401485096066,
            1.0,
        ]
    )
    previous = np.ones(points)
    current = np.array(nodes)
    for degree in range(1, points - 1):
        previous, current = (
            current,
            ((2 * degree + 1) * nodes * current - degree * previous) / (degree + 1),
        )
    weights = 2.0 / (points * (points - 1) * current**2)
    derivative = np.zeros((points, points))
    for target in range(points):
        for source in range(points):
            if target != source:
                derivative[target, source] = current[target] / (
                    current[source] * (nodes[target] - nodes[source])
                )
    derivative[0, 0] = -points * (points - 1) / 4.0
    derivative[points - 1, points - 1] = points * (points - 1) / 4.0
    return weights, derivative


W, D = gll_tables()
L = (D.T * W) @ D / W[:, None]


def average(extent):
    m = np.eye(extent)
    for k in range(8, extent, 8):
        m[k - 1, k - 1] = m[k, k] = m[k - 1, k] = m[k, k - 1] = 0.5
    return m


def along(matrix, extent):
    return np.kron(np.eye(extent // 8), matrix)


def face_rows_z(matrix):
    rows = np.zeros((16, NZ))
    full = along(matrix, NZ)
    rows[0] = full[0]
    rows[8] = full[NZ - 1]
    return rows


def split(matrix):
    parts, rest = [], np.asarray(matrix, np.float64)
    for _ in range(3):
        parts.append(rest.astype(np.float32).astype(ml_dtypes.bfloat16))
        rest = rest - parts[-1].astype(np.float64)
    return parts


def tables():
    az = average(NZ)
    blocks = []
    for matrix in (along(D, NZ), az @ along(D, NZ), az @ along(L, NZ)):
        high, mid, low = split(matrix.T)
        blocks.append(
            np.concatenate(
                [
                    np.concatenate([high, mid, high], axis=1),
                    np.concatenate([high, mid, low], axis=1),
                ],
                axis=0,
            )
        )
    z_blocks = np.stack(blocks)
    picks = np.zeros((16, NZ))
    picks[0, 0] = 1.0
    picks[8, NZ - 1] = 1.0
    z_faces = np.concatenate(
        split(face_rows_z(D))
        + split(face_rows_z(L))
        + [picks.astype(ml_dtypes.bfloat16)] * 3,
        axis=0,
    )
    local = np.arange(8)
    edge = np.where((local == 0) | (local == 7), 2.0, 1.0)
    wyz = W[:, None] * np.tile(W, 16)[None, :]
    myz = edge[:, None] * np.tile(edge, 16)[None, :]
    columns = [
        np.repeat(matrix[:, k : k + 1], NZ, axis=1)
        for matrix in (D, L)
        for k in range(8)
    ]
    small = np.concatenate([wyz, wyz * myz, 1.0 / myz] + columns, axis=0)
    return [z_blocks, z_faces, np.asarray(small, np.float32)]


Z_D, Z_DA, Z_LA = 0, 1, 2
F_D, F_L, F_PICK = 0, 48, 96
T_W, T_WM, T_IM, T_D, T_L = 0, 8, 16, 24, 88


def dot(a, b):
    return lax.dot_general(a, b, (((1,), (0,)), ((), ())), preferred_element_type=F32)


def dot_nt(a, b):
    return lax.dot_general(a, b, (((1,), (1,)), ((), ())), preferred_element_type=F32)


def dot_tn(a, b):
    return lax.dot_general(a, b, (((0,), (0,)), ((), ())), preferred_element_type=F32)


def split3(value):
    high = value.astype(jnp.bfloat16)
    rest = value - high.astype(F32)
    mid = rest.astype(jnp.bfloat16)
    return high, mid, (rest - mid.astype(F32)).astype(jnp.bfloat16)


def stack3(value):
    parts, rest = [], value
    for _ in range(3):
        parts.append(rest.astype(jnp.bfloat16).astype(F32))
        rest = rest - parts[-1]
    return jnp.concatenate(parts, axis=0).astype(jnp.bfloat16)


def flat(value):
    return value.reshape(ROWS, NZ)


def cube(value):
    return value.reshape(NX, NY, NZ)


def line(matrix_row, tiles):
    total = None
    for coefficient, tile in zip(matrix_row, tiles):
        part = tile * float(np.float32(coefficient))
        total = part if total is None else total + part
    return total


def kernel(
    base,
    adj,
    pen,
    zblocks,
    zfaces,
    small,
    projected,
    pressure,
    bs,
    us,
    ps,
    zb,
    zf,
    zt,
    raw,
    halo,
    adv,
    pav,
    vec,
    tt,
    grad,
    wm,
    wyz,
    q2,
    rq2,
    fz1,
    rz1,
    fy1,
    ry1,
    xf,
    xq,
    rx1,
    rq1,
    rx2,
    hx1,
    rmix,
    fx,
    rx,
    fy,
    ry,
    fz,
    rz,
    gfx,
    grx,
    gfy,
    gry,
    gfz,
    grz,
    mom,
    red1,
    part,
    red2,
    res,
    load_sem,
    send_sem,
    recv_sem,
    red_send,
    red_recv,
    out_sem,
):
    px = lax.axis_index("gx")
    py = lax.axis_index("gy")
    pz = lax.axis_index("gz")

    def at(dx, dy, dz):
        return (
            lax.rem(px + dx + GX, GX),
            lax.rem(py + dy + GY, GY),
            lax.rem(pz + dz + GZ, GZ),
        )

    def at_x(offset):
        return at(offset, 0, 0)

    def at_y(offset):
        return at(0, offset, 0)

    def at_z(offset):
        return at(0, 0, offset)

    row = px // 2
    half = lax.rem(px, 2)
    index1 = half * 8 + pz
    index2 = row * 4 + py

    def group1(k):
        i = lax.rem(index1 + k, 16)
        return (row * 2 + i // 8, py, lax.rem(i, 8))

    def group2(k):
        i = lax.rem(index2 + k, 16)
        return ((i // 4) * 2 + half, lax.rem(i, 4), pz)

    loads = [
        pltpu.make_async_copy(adj, us, load_sem.at[0]),
        pltpu.make_async_copy(base, bs, load_sem.at[1]),
        pltpu.make_async_copy(zblocks.at[0], zb.at[0], load_sem.at[2]),
        pltpu.make_async_copy(small, zt, load_sem.at[3]),
        pltpu.make_async_copy(zfaces, zf, load_sem.at[4]),
        pltpu.make_async_copy(pen, ps, load_sem.at[5]),
        pltpu.make_async_copy(
            zblocks.at[pl.ds(1, 2)], zb.at[pl.ds(1, 2)], load_sem.at[6]
        ),
    ]
    for copy in loads:
        copy.start()

    barrier = pltpu.get_barrier_semaphore()
    for dx, dy, dz in NEAR:
        pl.semaphore_signal(
            barrier, inc=1, device_id=at(dx, dy, dz), device_id_type=MESH
        )
    mates1 = [group1(k) for k in range(1, 16)]
    mates2 = [group2(k) for k in range(1, 16)]
    for mate in mates1 + mates2:
        pl.semaphore_signal(barrier, inc=1, device_id=mate, device_id_type=MESH)

    hx = (jnp.where(px > 0, 0.5, 0.0), jnp.where(px < GX - 1, 0.5, 0.0))
    hy = (jnp.where(py > 0, 0.5, 0.0), jnp.where(py < GY - 1, 0.5, 0.0))
    hx2 = (jnp.where(px > 1, 0.5, 0.0), jnp.where(px < GX - 2, 0.5, 0.0))
    sub = lax.broadcasted_iota(jnp.int32, (8, NZ), 0)
    first = jnp.where(sub == 0, 1.0, 0.0)
    last = jnp.where(sub == 7, 1.0, 0.0)

    pending = []
    counter = [0]

    def send(src, dst, device):
        k = counter[0]
        counter[0] += 1
        copy = pltpu.make_async_remote_copy(
            src_ref=src,
            dst_ref=dst,
            send_sem=send_sem.at[k],
            recv_sem=recv_sem.at[k],
            device_id=device,
            device_id_type=MESH,
        )
        copy.start()
        pending.append(copy)
        return copy

    for copy in loads[:4]:
        copy.wait()

    def y_rows(yt):
        return pl.ds(8 * yt, 8)

    def tiles(ref, yt):
        return [ref[x, y_rows(yt), :] for x in range(NX)]

    def loop(count, start=0):
        def run(body):
            for k in range(start, count):
                body(k)

        return run

    def columns(offset):
        return [zt[pl.ds(offset + 8 * k, 8), :] for k in range(8)]

    def y_line(ref, x, coefficients):
        result = []
        for t in range(4):
            total = None
            for k in range(8):
                part = coefficients[k] * ref[x, pl.ds(8 * t + k, 1), :]
                total = part if total is None else total + part
            result.append(total)
        return result

    def z_line(parts, block):
        high, mid, low = parts
        out = dot(
            jnp.concatenate([high, mid], axis=1), zb[block, :, pl.ds(0, 2 * NZ)]
        )
        rest = dot(
            jnp.concatenate([low, high], axis=1), zb[block, :, pl.ds(2 * NZ, NZ)]
        )
        return cube(out[:, :NZ] + (out[:, NZ:] + rest))

    d_columns = columns(T_D)
    for i in range(3):
        raw[i] = -bs[2] * z_line(split3(flat(us[i])), Z_D)
    for j in range(3):
        raw[2] += us[j] * z_line(split3(flat(bs[j])), Z_D)

    @loop(NX)
    def _(x):
        for i in range(3):
            for t, value in enumerate(y_line(us.at[i], x, d_columns)):
                rows = pl.ds(8 * t, 8)
                raw[i, x, rows, :] -= bs[1, x, rows, :] * value
        for j in range(3):
            for t, value in enumerate(y_line(bs.at[j], x, d_columns)):
                rows = pl.ds(8 * t, 8)
                raw[1, x, rows, :] += us[j, x, rows, :] * value

    @loop(4)
    def _(yt):
        rows = y_rows(yt)
        for i in range(3):
            src = tiles(us.at[i], yt)
            for x in range(NX):
                raw[i, x, rows, :] -= bs[0, x, rows, :] * line(D[x], src)
        for j in range(3):
            src = tiles(bs.at[j], yt)
            for x in range(NX):
                raw[0, x, rows, :] += us[j, x, rows, :] * line(D[x], src)

    for copy in loads[4:6]:
        copy.wait()
    raw[3] = ps[...]
    def z_faces(parts, offset):
        high, mid, low = parts
        table = zf[pl.ds(offset, 48), :]
        a, b = dot_nt(table, high), dot_nt(table[:32], mid)
        c = dot_nt(table[:16], low)
        return a[:16] + (a[16:32] + b[:16] + (a[32:] + b[16:] + c))

    def z_ends(parts):
        table = zf[pl.ds(F_PICK, 16), :]
        a, b, c = (dot_nt(table, part) for part in parts)
        return a + (b + c)

    faces = None
    for i in range(4):
        own = z_ends(split3(flat(raw[i])))
        faces = own if i == 0 else faces + pltpu.roll(own, i, 0)
    fz1[...] = faces
    for i in range(4):
        for x in range(NX):
            for side, y in ((0, 0), (1, NY - 1)):
                fy1[side, i, pl.ds(x, 1), :] = raw[i, x, pl.ds(y, 1), :]
    pl.semaphore_wait(barrier, 30 + len(NEAR))
    near = []
    for dz in (-1, 1):
        for dy in (0, -1, 1):
            src = fz1.at[pl.ds(0 if dz < 0 else 8, 4)]
            dst = rz1.at[1 if dz < 0 else 0, 1 - dy, pl.ds(0, 4)]
            near.append(send(src, dst, at(0, dy, dz)))
    near += [
        send(fy1.at[0], ry1.at[1], at_y(-1)),
        send(fy1.at[1], ry1.at[0], at_y(1)),
    ]
    raw_x = [
        send(raw.at[pl.ds(0, 3), 0], rx1.at[1, pl.ds(0, 3)], at_x(-1)),
        send(raw.at[pl.ds(0, 3), NX - 1], rx1.at[0, pl.ds(0, 3)], at_x(1)),
    ]
    w_tile = zt[pl.ds(T_W, 8), :]
    wm_tile = zt[pl.ds(T_WM, 8), :]
    im_tile = zt[pl.ds(T_IM, 8), :]
    fix_low = 1.0 - first * (0.5 - hy[0])
    fix_high = 1.0 - last * (0.5 - hy[1])
    inv_low = 1.0 + first * (1.0 - 2.0 * hy[0])
    inv_high = 1.0 + last * (1.0 - 2.0 * hy[1])
    wm_y = [wm_tile * fix_low, wm_tile, wm_tile, wm_tile * fix_high]
    im_y = [im_tile * inv_low, im_tile, im_tile, im_tile * inv_high]
    scale_x = [float(w) for w in W]
    mult_x = [1.0 + 2.0 * hx[0]] + [1.0] * 6 + [1.0 + 2.0 * hx[1]]
    inv_x = [1.0 - hx[0]] + [1.0] * 6 + [1.0 - hx[1]]
    for yt in range(4):
        for x in range(NX):
            wm[x, pl.ds(8 * yt, 8), :] = wm_y[yt] * (mult_x[x] * scale_x[x])
        wyz[pl.ds(8 * yt, 8), :] = wm_y[yt]

    lane = lax.broadcasted_iota(jnp.int32, (8, NZ), 1)
    begin = lax.rem(lane, 8) == 0
    end = lax.rem(lane, 8) == 7
    keep_z = jnp.where(begin | end, 0.5, 1.0)
    from_low = jnp.where(begin & (lane > 0), 0.5, 0.0)
    from_high = jnp.where(end & (lane < NZ - 1), 0.5, 0.0)
    low_y = [first * hy[0]] + [first * 0.5] * 3
    high_y = [last * 0.5] * 3 + [last * hy[1]]
    keep_y = [1.0 - low_y[t] - high_y[t] for t in range(4)]

    def mix_slab(src, low, high, edge, dst):
        for t in range(4):
            rows = pl.ds(8 * t, 8)
            down = low if t == 0 else src[pl.ds(8 * t - 1, 1), :]
            up = high if t == 3 else src[pl.ds(8 * t + 8, 1), :]
            value = src[rows, :] * keep_y[t] + down * low_y[t] + up * high_y[t]
            dst[rows, :] = (
                value * keep_z
                + pltpu.roll(value, 1, 1) * from_low
                + pltpu.roll(value, NZ - 1, 1) * from_high
                + edge[rows, :]
            )

    wide = lax.broadcasted_iota(jnp.int32, (8, ROWS), 1)
    y_of = lax.rem(wide, NY)
    x_of = wide // NY
    inner_begin = (lax.rem(wide, 8) == 0) & (y_of > 0)
    inner_end = (lax.rem(wide, 8) == 7) & (y_of < NY - 1)

    def y_mix(mid, down, up):
        partner = jnp.where(
            y_of == 0,
            pltpu.roll(down, ROWS - (NY - 1), 1),
            jnp.where(
                y_of == NY - 1,
                pltpu.roll(up, NY - 1, 1),
                jnp.where(
                    inner_begin, pltpu.roll(mid, 1, 1), pltpu.roll(mid, ROWS - 1, 1)
                ),
            ),
        )
        weight = jnp.where(
            y_of == 0,
            hy[0],
            jnp.where(
                y_of == NY - 1, hy[1], jnp.where(inner_begin | inner_end, 0.5, 0.0)
            ),
        )
        return mid + weight * (partner - mid)

    spots = jnp.concatenate(
        [
            jnp.where((sub == i) & (lane == 0), 0.5, 0.0)
            + jnp.where((sub == 4 + i) & (lane == NZ - 1), 0.5, 0.0)
            for i in range(4)
        ],
        axis=1,
    ).astype(F32)
    spots = jnp.concatenate([spots] * 3, axis=0).astype(jnp.bfloat16)

    def expand(values):
        return dot_tn(stack3(values), spots)

    for copy in near:
        copy.wait_recv()
    edges = jnp.where(
        lax.broadcasted_iota(jnp.int32, (8, ROWS), 0) < 4,
        y_mix(rz1[0, 1], rz1[0, 0], rz1[0, 2]),
        pltpu.roll(y_mix(rz1[1, 1], rz1[1, 0], rz1[1, 2]), 4, 0),
    )
    wide_halo = expand(edges)
    for i in range(4):
        halo[i] = cube(wide_halo[:, NZ * i : NZ * (i + 1)])
    for side in (0, 1):
        for i in range(4):
            for end in (0, 1):
                xq[side, pl.ds(NY + 4 * end + i, 1), :] = ry1[
                    end, i, pl.ds(side * (NX - 1), 1), :
                ]
        xq[side, pl.ds(NY + 8, 8), :] = edges[:, NZ * side : NZ * (side + 1)]

    def mixed(i, x, dst):
        mix_slab(
            raw.at[i, x],
            ry1[0, i, pl.ds(x, 1), :],
            ry1[1, i, pl.ds(x, 1), :],
            halo.at[i, x],
            dst,
        )

    for side in (0, 1):
        mixed(0, side * (NX - 1), xf.at[side, 0])
    @loop(NX - 1, 1)
    def _(x):
        mixed(0, x, adv.at[0, x])

    @loop(4)
    def _(yt):
        rows = y_rows(yt)
        src = [xf[0, 0, rows, :]]
        src += [adv[0, x, rows, :] for x in range(1, NX - 1)]
        src += [xf[1, 0, rows, :]]
        ends = [src[0] * (1.0 - hx[0]), src[NX - 1] * (1.0 - hx[1])]
        xq[0, rows, :] = line(D[0], src[: NX - 1] + [ends[1]])
        xq[1, rows, :] = line(D[NX - 1], [ends[0]] + src[1:])

    sx = [
        send(xq.at[0], rq1.at[1], at_x(-1)),
        send(xq.at[1], rq1.at[0], at_x(1)),
        send(xf.at[0, 0], rx2.at[1, 0], at_x(-2)),
        send(xf.at[1, 0], rx2.at[0, 0], at_x(2)),
    ]
    copies_p = [
        send(raw.at[3, 0], rx1.at[1, 3], at_x(-1)),
        send(raw.at[3, NX - 1], rx1.at[0, 3], at_x(1)),
    ]
    for i in range(1, 4):
        for side in (0, 1):
            mixed(i, side * (NX - 1), xf.at[side, i])

    @loop(NX - 1, 1)
    def _(x):
        for i in range(1, 3):
            mixed(i, x, adv.at[i, x])
        mixed(3, x, pav.at[x])

    loads[6].wait()
    for copy in raw_x:
        copy.wait_recv()
    for copy in sx:
        copy.wait_recv()
    edges = jnp.where(lane < NZ // 2, rq1[1, pl.ds(NY + 8, 8), :], rq1[0, pl.ds(NY + 8, 8), :])
    wide_halo = expand(edges)
    for i in range(4):
        part_halo = wide_halo[:, NZ * i : NZ * (i + 1)]
        hx1[0, i] = part_halo[NZ - NY :, :]
        hx1[1, i] = part_halo[:NY, :]

    def neighbour_face(side, i):
        mix_slab(
            rx1.at[side, i],
            rq1[side, pl.ds(NY + i, 1), :],
            rq1[side, pl.ds(NY + 4 + i, 1), :],
            hx1.at[side, i],
            rmix.at[side, i],
        )

    for i in range(3):
        for side in (0, 1):
            neighbour_face(side, i)
            own = xf[side, i]
            adv[i, side * (NX - 1)] = own + hx[side] * (rmix[side, i] - own)
    for side in (0, 1):
        mine, other = side * (NX - 1), (1 - side) * (NX - 1)
        rx[0, side] = (
            rq1[side, pl.ds(0, NY), :]
            + (0.5 * float(D[other, other])) * (xf[side, 0] - rmix[side, 0])
            + (float(D[other, mine]) * hx2[side]) * rx2[side, 0]
        )
    inner_low, inner_high = first * 0.5, last * 0.5
    keep_inner = [
        1.0 - (inner_low if t > 0 else 0.0) - (inner_high if t < 3 else 0.0)
        for t in range(4)
    ]

    def y_part(ref, offset, target, faces):
        coefficients = columns(offset)

        @loop(NX)
        def _(x):
            values = y_line(ref, x, coefficients)
            if faces is not None:
                faces[0, pl.ds(x, 1), :] = values[0][:1, :]
                faces[1, pl.ds(x, 1), :] = values[3][7:, :]
            for t in range(4):
                value = values[t] * keep_inner[t]
                if t > 0:
                    value = value + pltpu.roll(values[t - 1], 1, 0) * inner_low
                if t < 3:
                    value = value + pltpu.roll(values[t + 1], 7, 0) * inner_high
                target[x, pl.ds(8 * t, 8), :] = value

    def x_part(ref, mx, target):
        @loop(4)
        def _(yt):
            src = tiles(ref, yt)
            for x in range(NX):
                target[x, y_rows(yt), :] += line(mx[x], src)

    def x_faces(source, mx, low, high):
        @loop(4)
        def _(yt):
            src = tiles(source, yt)
            low[y_rows(yt), :] = line(mx[0], src)
            high[y_rows(yt), :] = line(mx[NX - 1], src)

    def add_y(target, low, high):
        for x in range(NX):
            target[x, pl.ds(0, 8), :] += first * low[x : x + 1, :]
            target[x, pl.ds(NY - 8, 8), :] += last * high[x : x + 1, :]

    def add_z(target, delta_z):
        target[...] += cube(dot_tn(stack3(delta_z), zf[pl.ds(F_PICK, 48), :]))

    def gradient(k):
        v = vec.at[k]
        parts = split3(flat(v[...]))
        ends = z_faces(parts, F_D)
        if k == 0:
            gfz[...] = ends
        else:
            gfz[...] += pltpu.roll(ends, k, 0)
        y_part(v, T_D, grad.at[k, 1], gfy.at[:, k])

        @loop(4)
        def _(yt):
            rows = y_rows(yt)
            src = tiles(v, yt)
            for x in range(NX):
                value = line(D[x], src)
                grad[k, 0, x, rows, :] = value
                if x in (0, NX - 1):
                    gfx[min(x, 1), k, rows, :] = value

        grad[k, 2] = z_line(parts, Z_DA)

    def gradient_edges():
        delta = grz[...] - gfz[...]
        wide_halo = expand(delta[:8] + pltpu.roll(delta[8:], 4, 0))
        for k in range(3):
            for side in (0, 1):
                grad[k, 0, side * (NX - 1)] += hx[side] * (grx[side, k] - gfx[side, k])
            add_y(
                grad.at[k, 1],
                hy[0] * (gry[0, k] - gfy[0, k]),
                hy[1] * (gry[1, k] - gfy[1, k]),
            )
            grad[k, 2] += cube(wide_halo[:, NZ * k : NZ * (k + 1)])

    def inner(a, b):
        total = None
        for yt in range(4):
            rows = pl.ds(8 * yt, 8)
            s = None
            for x in range(NX):
                p = a[x, rows, :] * b[x, rows, :]
                if x in (0, NX - 1):
                    p = p * inv_x[x]
                s = p if s is None else s + p
            s = s * im_y[yt]
            total = s if total is None else total + s
        return jnp.sum(total, axis=0, keepdims=True)

    end_rows = lax.rem(lax.broadcasted_iota(jnp.int32, (16, ROWS), 0), 8) == 0
    far = []

    def phase(k, vx, vy, vz, mx, ycol, zmat, zface, with_mass, sign):
        parts = split3(flat(vz[...]))
        fz[k] = z_faces(parts, zface)
        sz = [
            send(fz.at[k, pl.ds(0, 1)], rz.at[k, pl.ds(8, 1)], at_z(-1)),
            send(fz.at[k, pl.ds(8, 1)], rz.at[k, pl.ds(0, 1)], at_z(1)),
        ]
        x_faces(vx, mx, fx.at[k, 0], fx.at[k, 1])
        sx = []
        if k == 1:
            sx = [
                send(fx.at[k, 0], rx.at[k, 1], at_x(-1)),
                send(fx.at[k, 1], rx.at[k, 0], at_x(1)),
            ]
        y_part(vy, ycol, tt, fy.at[k])
        sy = [
            send(fy.at[k, 0], ry.at[k, 1], at_y(-1)),
            send(fy.at[k, 1], ry.at[k, 0], at_y(1)),
        ]
        if with_mass and k == 1:
            finish_penalty()
        if k == 1:
            far[:] = [
                send(fx.at[k, 0], rx2.at[1, 1], at_x(-2)),
                send(fx.at[k, 1], rx2.at[0, 1], at_x(2)),
            ]
        rest = z_line(parts, zmat)
        if with_mass:
            rest = rest + pav[...] * vx[...]
        tt[...] += rest
        x_part(vx, mx, tt)
        if k == 2:
            gradient(1)
            mom[pl.ds(0, 1), :] = inner(vec.at[0], vec.at[0])
            mom[pl.ds(1, 1), :] = inner(vec.at[0], vec.at[1])
            mom[pl.ds(2, 1), :] = inner(vec.at[1], vec.at[1])
            mom[pl.ds(6, 2), :] = jnp.zeros((2, NZ), F32)
        for copy in sy:
            copy.wait_recv()
        add_y(
            tt,
            hy[0] * (ry[k, 0] - fy[k, 0]),
            hy[1] * (ry[k, 1] - fy[k, 1]),
        )
        for copy in sz:
            copy.wait_recv()
        add_z(tt, jnp.where(end_rows, 0.5 * (rz[k] - fz[k]), 0.0))
        out = vec.at[k]
        for x in range(1, NX - 1):
            out[x] = tt[x] * (sign * wm[x])
        if k == 1:
            @loop(4)
            def _(yt):
                rows = y_rows(yt)
                src = [tt[0, rows, :] * wm[0, rows, :]]
                src += [out[x, rows, :] for x in range(1, NX - 1)]
                src += [tt[NX - 1, rows, :] * wm[NX - 1, rows, :]]
                weight = wyz[rows, :]
                below = fx[1, 0, rows, :] * weight * (2.0 * scale_x[0] * hx[0])
                above = fx[1, 1, rows, :] * weight * (2.0 * scale_x[-1] * hx[1])
                q2[0, rows, :] = line(L[0], src[:-1] + [src[-1] - above])
                q2[1, rows, :] = line(L[NX - 1], [src[0] - below] + src[1:])

            far[2:] = [
                send(q2.at[0], rq2.at[1], at_x(-1)),
                send(q2.at[1], rq2.at[0], at_x(1)),
            ]
            gradient(0)
        if k == 2:
            for copy in far:
                copy.wait_recv()
            for side in (0, 1):
                mine, other = side * (NX - 1), (1 - side) * (NX - 1)
                near_term = (scale_x[other] * float(L[other, other])) * (
                    fx[1, side] - rx[1, side]
                )
                far_term = (2.0 * scale_x[mine] * float(L[other, mine])) * hx2[side]
                rx[2, side] = rq2[side] + wyz[...] * (
                    near_term + far_term * rx2[side, 1]
                )
        for copy in sx:
            copy.wait_recv()
        out[0] = (tt[0] + hx[0] * (rx[k, 0] - fx[k, 0])) * (sign * wm[0])
        out[NX - 1] = (tt[NX - 1] + hx[1] * (rx[k, 1] - fx[k, 1])) * (sign * wm[NX - 1])

    def finish_penalty():
        for copy in copies_p:
            copy.wait_recv()
        for side in (0, 1):
            neighbour_face(side, 3)
            own = xf[side, 3]
            pav[side * (NX - 1)] = own + hx[side] * (rmix[side, 3] - own)

    phase(0, adv.at[0], adv.at[1], adv.at[2], D, T_D, Z_DA, F_D, False, -1.0)
    for k in (1, 2):
        v = vec.at[k - 1]
        phase(k, v, v, v, L, T_L, Z_LA, F_L, True, 1.0)

    v0, v1, v2 = vec.at[0], vec.at[1], vec.at[2]
    y_part(v2, T_L, tt, None)
    tt[...] += z_line(split3(flat(vec[2])), Z_LA) + pav[...] * v2[...]
    x_part(v2, L, tt)
    total = None
    for yt in range(4):
        rows = pl.ds(8 * yt, 8)
        s = None
        for x in range(NX):
            p = v2[x, rows, :] * tt[x, rows, :] * scale_x[x]
            s = p if s is None else s + p
        total = s if total is None else total + s
    mom[pl.ds(5, 1), :] = jnp.sum(total * w_tile, axis=0, keepdims=True)
    mom[pl.ds(3, 1), :] = inner(v1, v2)
    mom[pl.ds(4, 1), :] = inner(v2, v2)

    def spread(source, slots, own, mates, which):
        slots[own] = source[...]
        for mate in mates:
            pltpu.make_async_remote_copy(
                src_ref=source,
                dst_ref=slots.at[own],
                send_sem=red_send.at[which],
                recv_sem=red_recv.at[which],
                device_id=mate,
                device_id_type=MESH,
            ).start()

    def wait_all(slots, semaphore):
        view = slots.at[pl.ds(0, 15)]
        pltpu.make_async_copy(view, view, semaphore).wait()

    def gather(slots, which):
        wait_all(slots, red_recv.at[which])
        total = slots[0]
        for k in range(1, 16):
            total = total + slots[k]
        return total

    spread(mom, red1, index2, mates2, 0)

    gradient(2)
    gradient_copies = [
        send(gfx.at[0], grx.at[1], at_x(-1)),
        send(gfx.at[1], grx.at[0], at_x(1)),
        send(gfz.at[pl.ds(0, 8)], grz.at[pl.ds(8, 8)], at_z(-1)),
        send(gfz.at[pl.ds(8, 8)], grz.at[pl.ds(0, 8)], at_z(1)),
        send(gfy.at[0], gry.at[1], at_y(-1)),
        send(gfy.at[1], gry.at[0], at_y(1)),
    ]
    part[...] = gather(red1, 0)
    spread(part, red2, index1, mates1, 1)
    for copy in gradient_copies:
        copy.wait_recv()
    gradient_edges()

    for copy in pending:
        copy.wait_send()
    wait_all(red1, red_send.at[0])
    sums = jnp.sum(gather(red2, 1), axis=1, keepdims=True)
    m = [jnp.broadcast_to(sums[k : k + 1, :], (8, NZ)) for k in range(6)]
    s0, s1, s2 = lax.rsqrt(m[1]), lax.rsqrt(m[3]), lax.rsqrt(m[5])
    h01 = m[2] * s0 * s1
    h02 = m[3] * s0 * s2
    h12 = m[4] * s1 * s2
    h00, h11, h22 = m[1] * s0 * s0, m[3] * s1 * s1, m[5] * s2 * s2
    g0, g1, g2 = m[0] * s0, m[1] * s1, m[2] * s2
    l10 = h01 / h00
    l20 = h02 / h00
    d1 = h11 - l10 * h01
    d1 = jnp.where(d1 > 1e-6, d1, 1e30)
    e1 = h12 - l20 * h01
    l21 = e1 / d1
    d2 = h22 - l20 * h02 - l21 * e1
    d2 = jnp.where(d2 > 1e-6, d2, 1e30)
    y0 = g0
    y1_ = g1 - l10 * y0
    y2_ = g2 - l20 * y0 - l21 * y1_
    c2 = y2_ / d2
    c1 = y1_ / d1 - l21 * c2
    c0 = y0 / h00 - l10 * c1 - l20 * c2
    c0, c1, c2 = c0 * s0, c1 * s1, c2 * s2

    c0, c1, c2 = c0[:1], c1[:1], c2[:1]
    outs = []
    for k in range(PIECES):
        slabs = pl.ds(k * (NX // PIECES), NX // PIECES)
        tt[slabs] = c0 * v0[slabs] + c1 * v1[slabs] + c2 * v2[slabs]
        outs.append(
            pltpu.make_async_copy(tt.at[slabs], pressure.at[slabs], out_sem.at[k, 0])
        )
        outs[-1].start()
        for i in range(3):
            res[i, slabs] = adv[i, slabs] - (
                c0 * grad[0, i, slabs] + c1 * grad[1, i, slabs] + c2 * grad[2, i, slabs]
            )
        outs.append(
            pltpu.make_async_copy(
                res.at[:, slabs], projected.at[:, slabs], out_sem.at[k, 1]
            )
        )
        outs[-1].start()
    wait_all(red2, red_send.at[1])
    for copy in outs:
        copy.wait()


def hand_on(projected_in, pressure_in, projected, pressure, proj, pres, load_sem, sem):
    loads, outs = [], []
    for k in range(PIECES):
        slabs = pl.ds(k * (NX // PIECES), NX // PIECES)
        for i, (source, held, target) in enumerate(
            [
                (projected_in.at[:, slabs], proj.at[:, slabs], projected.at[:, slabs]),
                (pressure_in.at[slabs], pres.at[slabs], pressure.at[slabs]),
            ]
        ):
            loads.append(pltpu.make_async_copy(source, held, load_sem.at[k, i]))
            outs.append(pltpu.make_async_copy(held, target, sem.at[k, i]))
    for copy in loads:
        copy.start()
    for load, out in zip(loads, outs):
        load.wait()
        out.start()
    for copy in outs:
        copy.wait()


def per_device(base_flow, adjoint_velocity, penalty):
    field = (NX, NY, NZ)
    v = lambda *shape: pltpu.VMEM(shape, F32)
    consts = [jnp.asarray(t) for t in tables()]
    any_spec = pl.BlockSpec(memory_space=pltpu.HBM)
    sends = 60
    shapes = (
        jax.ShapeDtypeStruct((3,) + field, F32),
        jax.ShapeDtypeStruct(field, F32),
    )
    results = pl.pallas_call(
        kernel,
        out_shape=shapes,
        in_specs=[any_spec] * 6,
        out_specs=(any_spec,) * 2,
        scratch_shapes=[
            v(3, *field),
            v(3, *field),
            v(*field),
            pltpu.VMEM(consts[0].shape, jnp.bfloat16),
            pltpu.VMEM(consts[1].shape, jnp.bfloat16),
            v(*consts[2].shape),
            v(4, *field),
            v(4, *field),
            v(3, *field),
            v(*field),
            v(3, *field),
            v(*field),
            v(3, 3, *field),
            v(*field),
            v(NY, NZ),
            v(2, NY, NZ),
            v(2, NY, NZ),
            v(16, ROWS),
            v(2, 3, 8, ROWS),
            v(2, 4, 8, NZ),
            v(2, 4, 8, NZ),
            v(2, 4, NY, NZ),
            v(2, NY + 16, NZ),
            v(2, 4, NY, NZ),
            v(2, NY + 16, NZ),
            v(2, 2, NY, NZ),
            v(2, 4, NY, NZ),
            v(2, 4, NY, NZ),
            v(3, 2, NY, NZ),
            v(3, 2, NY, NZ),
            v(3, 2, 8, NZ),
            v(3, 2, 8, NZ),
            v(3, 16, ROWS),
            v(3, 16, ROWS),
            v(2, 3, NY, NZ),
            v(2, 3, NY, NZ),
            v(2, 3, 8, NZ),
            v(2, 3, 8, NZ),
            v(16, ROWS),
            v(16, ROWS),
            v(8, NZ),
            v(16, 8, NZ),
            v(8, NZ),
            v(16, 8, NZ),
            v(3, *field),
            pltpu.SemaphoreType.DMA((7,)),
            pltpu.SemaphoreType.DMA((sends + 10,)),
            pltpu.SemaphoreType.DMA((sends + 10,)),
            pltpu.SemaphoreType.DMA((2,)),
            pltpu.SemaphoreType.DMA((2,)),
            pltpu.SemaphoreType.DMA((PIECES, 2)),
        ],
        compiler_params=pltpu.CompilerParams(
            collective_id=0, has_side_effects=True, vmem_limit_bytes=63 * 1024 * 1024
        ),
        name="adjoint",
    )(base_flow, adjoint_velocity, penalty, *consts)
    return pl.pallas_call(
        hand_on,
        out_shape=shapes,
        in_specs=[any_spec] * 2,
        out_specs=(any_spec,) * 2,
        scratch_shapes=[
            v(3, *field),
            v(*field),
            pltpu.SemaphoreType.DMA((PIECES, 2)),
            pltpu.SemaphoreType.DMA((PIECES, 2)),
        ],
        compiler_params=pltpu.CompilerParams(vmem_limit_bytes=63 * 1024 * 1024),
        name="hand_on",
    )(*results)


def solution(mesh):
    spec3 = P(None, "gx", "gy", "gz")
    spec1 = P("gx", "gy", "gz")
    return jax.shard_map(
        per_device,
        mesh=mesh,
        in_specs=(spec3, spec3, spec1),
        out_specs=(spec3, spec1),
        check_vma=False,
    )
```

```python
import functools

import jax
import jax.numpy as jnp
import ml_dtypes
import numpy as np
from jax import lax
from jax.experimental import pallas as pl
from jax.experimental.pallas import tpu as pltpu
from jax.sharding import PartitionSpec as P

MESH = pl.DeviceIdType.MESH
F32 = jnp.float32
N = 8
NX, NY, NZ = 8, 32, 128
ROWS = NX * NY
GX, GY, GZ = 8, 4, 8
PIECES = 2
NEAR = [(-1, 0, 0), (1, 0, 0)] + [
    (0, dy, dz) for dy in (-1, 1, 0) for dz in (-1, 1, 0) if (dy, dz) != (0, 0)
]


def gll_tables():
    points = 8
    nodes = np.array(
        [
            -1.0,
            -0.8717401485096066,
            -0.5917001814331423,
            -0.2092992179024789,
            0.2092992179024789,
            0.5917001814331423,
            0.8717401485096066,
            1.0,
        ]
    )
    previous = np.ones(points)
    current = np.array(nodes)
    for degree in range(1, points - 1):
        previous, current = (
            current,
            ((2 * degree + 1) * nodes * current - degree * previous) / (degree + 1),
        )
    weights = 2.0 / (points * (points - 1) * current**2)
    derivative = np.zeros((points, points))
    for target in range(points):
        for source in range(points):
            if target != source:
                derivative[target, source] = current[target] / (
                    current[source] * (nodes[target] - nodes[source])
                )
    derivative[0, 0] = -points * (points - 1) / 4.0
    derivative[points - 1, points - 1] = points * (points - 1) / 4.0
    return weights, derivative


W, D = gll_tables()
L = (D.T * W) @ D / W[:, None]


def average(extent):
    m = np.eye(extent)
    for k in range(8, extent, 8):
        m[k - 1, k - 1] = m[k, k] = m[k - 1, k] = m[k, k - 1] = 0.5
    return m


def along(matrix, extent):
    return np.kron(np.eye(extent // 8), matrix)


def face_rows_z(matrix):
    rows = np.zeros((16, NZ))
    full = along(matrix, NZ)
    rows[0] = full[0]
    rows[8] = full[NZ - 1]
    return rows


def split(matrix):
    parts, rest = [], np.asarray(matrix, np.float64)
    for _ in range(3):
        parts.append(rest.astype(np.float32).astype(ml_dtypes.bfloat16))
        rest = rest - parts[-1].astype(np.float64)
    return parts


def tables():
    az = average(NZ)
    blocks = []
    for matrix in (along(D, NZ), az @ along(D, NZ), az @ along(L, NZ)):
        high, mid, low = split(matrix.T)
        blocks.append(
            np.concatenate(
                [
                    np.concatenate([high, mid, high], axis=1),
                    np.concatenate([high, mid, low], axis=1),
                ],
                axis=0,
            )
        )
    z_blocks = np.stack(blocks)
    picks = np.zeros((16, NZ))
    picks[0, 0] = 1.0
    picks[8, NZ - 1] = 1.0
    z_faces = np.concatenate(
        split(face_rows_z(D))
        + split(face_rows_z(L))
        + [picks.astype(ml_dtypes.bfloat16)] * 3,
        axis=0,
    )
    local = np.arange(8)
    edge = np.where((local == 0) | (local == 7), 2.0, 1.0)
    wyz = W[:, None] * np.tile(W, 16)[None, :]
    myz = edge[:, None] * np.tile(edge, 16)[None, :]
    columns = [
        np.repeat(matrix[:, k : k + 1], NZ, axis=1)
        for matrix in (D, L)
        for k in range(8)
    ]
    small = np.concatenate([wyz, wyz * myz, 1.0 / myz] + columns, axis=0)
    return [z_blocks, z_faces, np.asarray(small, np.float32)]


Z_D, Z_DA, Z_LA = 0, 1, 2
F_D, F_L, F_PICK = 0, 48, 96
T_W, T_WM, T_IM, T_D, T_L = 0, 8, 16, 24, 88


def dot(a, b):
    return lax.dot_general(a, b, (((1,), (0,)), ((), ())), preferred_element_type=F32)


def dot_nt(a, b):
    return lax.dot_general(a, b, (((1,), (1,)), ((), ())), preferred_element_type=F32)


def dot_tn(a, b):
    return lax.dot_general(a, b, (((0,), (0,)), ((), ())), preferred_element_type=F32)


def split3(value):
    high = value.astype(jnp.bfloat16)
    rest = value - high.astype(F32)
    mid = rest.astype(jnp.bfloat16)
    return high, mid, (rest - mid.astype(F32)).astype(jnp.bfloat16)


def stack3(value):
    parts, rest = [], value
    for _ in range(3):
        parts.append(rest.astype(jnp.bfloat16).astype(F32))
        rest = rest - parts[-1]
    return jnp.concatenate(parts, axis=0).astype(jnp.bfloat16)


def flat(value):
    return value.reshape(ROWS, NZ)


def cube(value):
    return value.reshape(NX, NY, NZ)


def line(matrix_row, tiles):
    total = None
    for coefficient, tile in zip(matrix_row, tiles):
        part = tile * float(np.float32(coefficient))
        total = part if total is None else total + part
    return total


def kernel(
    base,
    adj,
    pen,
    zblocks,
    zfaces,
    small,
    projected,
    pressure,
    bs,
    us,
    ps,
    zb,
    zf,
    zt,
    raw,
    halo,
    adv,
    pav,
    vec,
    tt,
    grad,
    wm,
    wyz,
    q2,
    rq2,
    fz1,
    rz1,
    fy1,
    ry1,
    xf,
    xq,
    rx1,
    rq1,
    rx2,
    hx1,
    rmix,
    fx,
    rx,
    fy,
    ry,
    fz,
    rz,
    gfx,
    grx,
    gfy,
    gry,
    gfz,
    grz,
    mom,
    red1,
    part,
    red2,
    res,
    load_sem,
    send_sem,
    recv_sem,
    red_send,
    red_recv,
    out_sem,
):
    px = lax.axis_index("gx")
    py = lax.axis_index("gy")
    pz = lax.axis_index("gz")

    def at(dx, dy, dz):
        return (
            lax.rem(px + dx + GX, GX),
            lax.rem(py + dy + GY, GY),
            lax.rem(pz + dz + GZ, GZ),
        )

    def at_x(offset):
        return at(offset, 0, 0)

    def at_y(offset):
        return at(0, offset, 0)

    def at_z(offset):
        return at(0, 0, offset)

    row = px // 2
    half = lax.rem(px, 2)
    index1 = half * 8 + pz
    index2 = row * 4 + py

    def group1(k):
        i = lax.rem(index1 + k, 16)
        return (row * 2 + i // 8, py, lax.rem(i, 8))

    def group2(k):
        i = lax.rem(index2 + k, 16)
        return ((i // 4) * 2 + half, lax.rem(i, 4), pz)

    loads = [
        pltpu.make_async_copy(adj, us, load_sem.at[0]),
        pltpu.make_async_copy(base, bs, load_sem.at[1]),
        pltpu.make_async_copy(zblocks.at[0], zb.at[0], load_sem.at[2]),
        pltpu.make_async_copy(small, zt, load_sem.at[3]),
        pltpu.make_async_copy(zfaces, zf, load_sem.at[4]),
        pltpu.make_async_copy(pen, ps, load_sem.at[5]),
        pltpu.make_async_copy(
            zblocks.at[pl.ds(1, 2)], zb.at[pl.ds(1, 2)], load_sem.at[6]
        ),
    ]
    for copy in loads:
        copy.start()

    barrier = pltpu.get_barrier_semaphore()
    for dx, dy, dz in NEAR:
        pl.semaphore_signal(
            barrier, inc=1, device_id=at(dx, dy, dz), device_id_type=MESH
        )
    mates1 = [group1(k) for k in range(1, 16)]
    mates2 = [group2(k) for k in range(1, 16)]
    for mate in mates1 + mates2:
        pl.semaphore_signal(barrier, inc=1, device_id=mate, device_id_type=MESH)

    hx = (jnp.where(px > 0, 0.5, 0.0), jnp.where(px < GX - 1, 0.5, 0.0))
    hy = (jnp.where(py > 0, 0.5, 0.0), jnp.where(py < GY - 1, 0.5, 0.0))
    hx2 = (jnp.where(px > 1, 0.5, 0.0), jnp.where(px < GX - 2, 0.5, 0.0))
    sub = lax.broadcasted_iota(jnp.int32, (8, NZ), 0)
    first = jnp.where(sub == 0, 1.0, 0.0)
    last = jnp.where(sub == 7, 1.0, 0.0)

    pending = []
    counter = [0]

    def send(src, dst, device):
        k = counter[0]
        counter[0] += 1
        copy = pltpu.make_async_remote_copy(
            src_ref=src,
            dst_ref=dst,
            send_sem=send_sem.at[k],
            recv_sem=recv_sem.at[k],
            device_id=device,
            device_id_type=MESH,
        )
        copy.start()
        pending.append(copy)
        return copy

    for copy in loads[:4]:
        copy.wait()

    def y_rows(yt):
        return pl.ds(8 * yt, 8)

    def tiles(ref, yt):
        return [ref[x, y_rows(yt), :] for x in range(NX)]

    def loop(count, start=0):
        def run(body):
            for k in range(start, count):
                body(k)

        return run

    def columns(offset):
        return [zt[pl.ds(offset + 8 * k, 8), :] for k in range(8)]

    def y_line(ref, x, coefficients):
        result = []
        for t in range(4):
            total = None
            for k in range(8):
                part = coefficients[k] * ref[x, pl.ds(8 * t + k, 1), :]
                total = part if total is None else total + part
            result.append(total)
        return result

    def z_line(parts, block):
        high, mid, low = parts
        out = dot(
            jnp.concatenate([high, mid], axis=1), zb[block, :, pl.ds(0, 2 * NZ)]
        )
        rest = dot(
            jnp.concatenate([low, high], axis=1), zb[block, :, pl.ds(2 * NZ, NZ)]
        )
        return cube(out[:, :NZ] + (out[:, NZ:] + rest))

    d_columns = columns(T_D)
    for i in range(3):
        raw[i] = -bs[2] * z_line(split3(flat(us[i])), Z_D)
    for j in range(3):
        raw[2] += us[j] * z_line(split3(flat(bs[j])), Z_D)

    @loop(NX)
    def _(x):
        for i in range(3):
            for t, value in enumerate(y_line(us.at[i], x, d_columns)):
                rows = pl.ds(8 * t, 8)
                raw[i, x, rows, :] -= bs[1, x, rows, :] * value
        for j in range(3):
            for t, value in enumerate(y_line(bs.at[j], x, d_columns)):
                rows = pl.ds(8 * t, 8)
                raw[1, x, rows, :] += us[j, x, rows, :] * value

    @loop(4)
    def _(yt):
        rows = y_rows(yt)
        for i in range(3):
            src = tiles(us.at[i], yt)
            for x in range(NX):
                raw[i, x, rows, :] -= bs[0, x, rows, :] * line(D[x], src)
        for j in range(3):
            src = tiles(bs.at[j], yt)
            for x in range(NX):
                raw[0, x, rows, :] += us[j, x, rows, :] * line(D[x], src)

    for copy in loads[4:6]:
        copy.wait()
    raw[3] = ps[...]
    def z_faces(parts, offset):
        high, mid, low = parts
        table = zf[pl.ds(offset, 48), :]
        a, b = dot_nt(table, high), dot_nt(table[:32], mid)
        c = dot_nt(table[:16], low)
        return a[:16] + (a[16:32] + b[:16] + (a[32:] + b[16:] + c))

    def z_ends(parts):
        table = zf[pl.ds(F_PICK, 16), :]
        a, b, c = (dot_nt(table, part) for part in parts)
        return a + (b + c)

    faces = None
    for i in range(4):
        own = z_ends(split3(flat(raw[i])))
        faces = own if i == 0 else faces + pltpu.roll(own, i, 0)
    fz1[...] = faces
    for i in range(4):
        for x in range(NX):
            for side, y in ((0, 0), (1, NY - 1)):
                fy1[side, i, pl.ds(x, 1), :] = raw[i, x, pl.ds(y, 1), :]
    pl.semaphore_wait(barrier, 30 + len(NEAR))
    near = []
    for dz in (-1, 1):
        for dy in (0, -1, 1):
            src = fz1.at[pl.ds(0 if dz < 0 else 8, 4)]
            dst = rz1.at[1 if dz < 0 else 0, 1 - dy, pl.ds(0, 4)]
            near.append(send(src, dst, at(0, dy, dz)))
    near += [
        send(fy1.at[0], ry1.at[1], at_y(-1)),
        send(fy1.at[1], ry1.at[0], at_y(1)),
    ]
    raw_x = [
        send(raw.at[pl.ds(0, 3), 0], rx1.at[1, pl.ds(0, 3)], at_x(-1)),
        send(raw.at[pl.ds(0, 3), NX - 1], rx1.at[0, pl.ds(0, 3)], at_x(1)),
    ]
    w_tile = zt[pl.ds(T_W, 8), :]
    wm_tile = zt[pl.ds(T_WM, 8), :]
    im_tile = zt[pl.ds(T_IM, 8), :]
    fix_low = 1.0 - first * (0.5 - hy[0])
    fix_high = 1.0 - last * (0.5 - hy[1])
    inv_low = 1.0 + first * (1.0 - 2.0 * hy[0])
    inv_high = 1.0 + last * (1.0 - 2.0 * hy[1])
    wm_y = [wm_tile * fix_low, wm_tile, wm_tile, wm_tile * fix_high]
    im_y = [im_tile * inv_low, im_tile, im_tile, im_tile * inv_high]
    scale_x = [float(w) for w in W]
    mult_x = [1.0 + 2.0 * hx[0]] + [1.0] * 6 + [1.0 + 2.0 * hx[1]]
    inv_x = [1.0 - hx[0]] + [1.0] * 6 + [1.0 - hx[1]]
    for yt in range(4):
        for x in range(NX):
            wm[x, pl.ds(8 * yt, 8), :] = wm_y[yt] * (mult_x[x] * scale_x[x])
        wyz[pl.ds(8 * yt, 8), :] = wm_y[yt]

    lane = lax.broadcasted_iota(jnp.int32, (8, NZ), 1)
    begin = lax.rem(lane, 8) == 0
    end = lax.rem(lane, 8) == 7
    keep_z = jnp.where(begin | end, 0.5, 1.0)
    from_low = jnp.where(begin & (lane > 0), 0.5, 0.0)
    from_high = jnp.where(end & (lane < NZ - 1), 0.5, 0.0)
    low_y = [first * hy[0]] + [first * 0.5] * 3
    high_y = [last * 0.5] * 3 + [last * hy[1]]
    keep_y = [1.0 - low_y[t] - high_y[t] for t in range(4)]

    def mix_slab(src, low, high, edge, dst):
        for t in range(4):
            rows = pl.ds(8 * t, 8)
            down = low if t == 0 else src[pl.ds(8 * t - 1, 1), :]
            up = high if t == 3 else src[pl.ds(8 * t + 8, 1), :]
            value = src[rows, :] * keep_y[t] + down * low_y[t] + up * high_y[t]
            dst[rows, :] = (
                value * keep_z
                + pltpu.roll(value, 1, 1) * from_low
                + pltpu.roll(value, NZ - 1, 1) * from_high
                + edge[rows, :]
            )

    wide = lax.broadcasted_iota(jnp.int32, (8, ROWS), 1)
    y_of = lax.rem(wide, NY)
    x_of = wide // NY
    inner_begin = (lax.rem(wide, 8) == 0) & (y_of > 0)
    inner_end = (lax.rem(wide, 8) == 7) & (y_of < NY - 1)

    def y_mix(mid, down, up):
        partner = jnp.where(
            y_of == 0,
            pltpu.roll(down, ROWS - (NY - 1), 1),
            jnp.where(
                y_of == NY - 1,
                pltpu.roll(up, NY - 1, 1),
                jnp.where(
                    inner_begin, pltpu.roll(mid, 1, 1), pltpu.roll(mid, ROWS - 1, 1)
                ),
            ),
        )
        weight = jnp.where(
            y_of == 0,
            hy[0],
            jnp.where(
                y_of == NY - 1, hy[1], jnp.where(inner_begin | inner_end, 0.5, 0.0)
            ),
        )
        return mid + weight * (partner - mid)

    spots = jnp.concatenate(
        [
            jnp.where((sub == i) & (lane == 0), 0.5, 0.0)
            + jnp.where((sub == 4 + i) & (lane == NZ - 1), 0.5, 0.0)
            for i in range(4)
        ],
        axis=1,
    ).astype(F32)
    spots = jnp.concatenate([spots] * 3, axis=0).astype(jnp.bfloat16)

    def expand(values):
        return dot_tn(stack3(values), spots)

    for copy in near:
        copy.wait_recv()
    edges = jnp.where(
        lax.broadcasted_iota(jnp.int32, (8, ROWS), 0) < 4,
        y_mix(rz1[0, 1], rz1[0, 0], rz1[0, 2]),
        pltpu.roll(y_mix(rz1[1, 1], rz1[1, 0], rz1[1, 2]), 4, 0),
    )
    wide_halo = expand(edges)
    for i in range(4):
        halo[i] = cube(wide_halo[:, NZ * i : NZ * (i + 1)])
    for side in (0, 1):
        for i in range(4):
            for end in (0, 1):
                xq[side, pl.ds(NY + 4 * end + i, 1), :] = ry1[
                    end, i, pl.ds(side * (NX - 1), 1), :
                ]
        xq[side, pl.ds(NY + 8, 8), :] = edges[:, NZ * side : NZ * (side + 1)]

    def mixed(i, x, dst):
        mix_slab(
            raw.at[i, x],
            ry1[0, i, pl.ds(x, 1), :],
            ry1[1, i, pl.ds(x, 1), :],
            halo.at[i, x],
            dst,
        )

    for side in (0, 1):
        mixed(0, side * (NX - 1), xf.at[side, 0])
    @loop(NX - 1, 1)
    def _(x):
        mixed(0, x, adv.at[0, x])

    @loop(4)
    def _(yt):
        rows = y_rows(yt)
        src = [xf[0, 0, rows, :]]
        src += [adv[0, x, rows, :] for x in range(1, NX - 1)]
        src += [xf[1, 0, rows, :]]
        ends = [src[0] * (1.0 - hx[0]), src[NX - 1] * (1.0 - hx[1])]
        xq[0, rows, :] = line(D[0], src[: NX - 1] + [ends[1]])
        xq[1, rows, :] = line(D[NX - 1], [ends[0]] + src[1:])

    sx = [
        send(xq.at[0], rq1.at[1], at_x(-1)),
        send(xq.at[1], rq1.at[0], at_x(1)),
        send(xf.at[0, 0], rx2.at[1, 0], at_x(-2)),
        send(xf.at[1, 0], rx2.at[0, 0], at_x(2)),
    ]
    copies_p = [
        send(raw.at[3, 0], rx1.at[1, 3], at_x(-1)),
        send(raw.at[3, NX - 1], rx1.at[0, 3], at_x(1)),
    ]
    for i in range(1, 4):
        for side in (0, 1):
            mixed(i, side * (NX - 1), xf.at[side, i])

    @loop(NX - 1, 1)
    def _(x):
        for i in range(1, 3):
            mixed(i, x, adv.at[i, x])
        mixed(3, x, pav.at[x])

    loads[6].wait()
    for copy in raw_x:
        copy.wait_recv()
    for copy in sx:
        copy.wait_recv()
    edges = jnp.where(lane < NZ // 2, rq1[1, pl.ds(NY + 8, 8), :], rq1[0, pl.ds(NY + 8, 8), :])
    wide_halo = expand(edges)
    for i in range(4):
        part_halo = wide_halo[:, NZ * i : NZ * (i + 1)]
        hx1[0, i] = part_halo[NZ - NY :, :]
        hx1[1, i] = part_halo[:NY, :]

    def neighbour_face(side, i):
        mix_slab(
            rx1.at[side, i],
            rq1[side, pl.ds(NY + i, 1), :],
            rq1[side, pl.ds(NY + 4 + i, 1), :],
            hx1.at[side, i],
            rmix.at[side, i],
        )

    for i in range(3):
        for side in (0, 1):
            neighbour_face(side, i)
            own = xf[side, i]
            adv[i, side * (NX - 1)] = own + hx[side] * (rmix[side, i] - own)
    for side in (0, 1):
        mine, other = side * (NX - 1), (1 - side) * (NX - 1)
        rx[0, side] = (
            rq1[side, pl.ds(0, NY), :]
            + (0.5 * float(D[other, other])) * (xf[side, 0] - rmix[side, 0])
            + (float(D[other, mine]) * hx2[side]) * rx2[side, 0]
        )
    inner_low, inner_high = first * 0.5, last * 0.5
    keep_inner = [
        1.0 - (inner_low if t > 0 else 0.0) - (inner_high if t < 3 else 0.0)
        for t in range(4)
    ]

    def y_part(ref, offset, target, faces):
        coefficients = columns(offset)

        @loop(NX)
        def _(x):
            values = y_line(ref, x, coefficients)
            if faces is not None:
                faces[0, pl.ds(x, 1), :] = values[0][:1, :]
                faces[1, pl.ds(x, 1), :] = values[3][7:, :]
            for t in range(4):
                value = values[t] * keep_inner[t]
                if t > 0:
                    value = value + pltpu.roll(values[t - 1], 1, 0) * inner_low
                if t < 3:
                    value = value + pltpu.roll(values[t + 1], 7, 0) * inner_high
                target[x, pl.ds(8 * t, 8), :] = value

    def x_part(ref, mx, target):
        @loop(4)
        def _(yt):
            src = tiles(ref, yt)
            for x in range(NX):
                target[x, y_rows(yt), :] += line(mx[x], src)

    def x_faces(source, mx, low, high):
        @loop(4)
        def _(yt):
            src = tiles(source, yt)
            low[y_rows(yt), :] = line(mx[0], src)
            high[y_rows(yt), :] = line(mx[NX - 1], src)

    def add_y(target, low, high):
        for x in range(NX):
            target[x, pl.ds(0, 8), :] += first * low[x : x + 1, :]
            target[x, pl.ds(NY - 8, 8), :] += last * high[x : x + 1, :]

    def add_z(target, delta_z):
        target[...] += cube(dot_tn(stack3(delta_z), zf[pl.ds(F_PICK, 48), :]))

    def gradient(k):
        v = vec.at[k]
        parts = split3(flat(v[...]))
        ends = z_faces(parts, F_D)
        if k == 0:
            gfz[...] = ends
        else:
            gfz[...] += pltpu.roll(ends, k, 0)
        y_part(v, T_D, grad.at[k, 1], gfy.at[:, k])

        @loop(4)
        def _(yt):
            rows = y_rows(yt)
            src = tiles(v, yt)
            for x in range(NX):
                value = line(D[x], src)
                grad[k, 0, x, rows, :] = value
                if x in (0, NX - 1):
                    gfx[min(x, 1), k, rows, :] = value

        grad[k, 2] = z_line(parts, Z_DA)

    def gradient_edges():
        delta = grz[...] - gfz[...]
        wide_halo = expand(delta[:8] + pltpu.roll(delta[8:], 4, 0))
        for k in range(3):
            for side in (0, 1):
                grad[k, 0, side * (NX - 1)] += hx[side] * (grx[side, k] - gfx[side, k])
            add_y(
                grad.at[k, 1],
                hy[0] * (gry[0, k] - gfy[0, k]),
                hy[1] * (gry[1, k] - gfy[1, k]),
            )
            grad[k, 2] += cube(wide_halo[:, NZ * k : NZ * (k + 1)])

    def inner(a, b):
        total = None
        for yt in range(4):
            rows = pl.ds(8 * yt, 8)
            s = None
            for x in range(NX):
                p = a[x, rows, :] * b[x, rows, :]
                if x in (0, NX - 1):
                    p = p * inv_x[x]
                s = p if s is None else s + p
            s = s * im_y[yt]
            total = s if total is None else total + s
        return jnp.sum(total, axis=0, keepdims=True)

    end_rows = lax.rem(lax.broadcasted_iota(jnp.int32, (16, ROWS), 0), 8) == 0
    far = []

    def phase(k, vx, vy, vz, mx, ycol, zmat, zface, with_mass, sign):
        parts = split3(flat(vz[...]))
        fz[k] = z_faces(parts, zface)
        sz = [
            send(fz.at[k, pl.ds(0, 1)], rz.at[k, pl.ds(8, 1)], at_z(-1)),
            send(fz.at[k, pl.ds(8, 1)], rz.at[k, pl.ds(0, 1)], at_z(1)),
        ]
        x_faces(vx, mx, fx.at[k, 0], fx.at[k, 1])
        sx = []
        if k == 1:
            sx = [
                send(fx.at[k, 0], rx.at[k, 1], at_x(-1)),
                send(fx.at[k, 1], rx.at[k, 0], at_x(1)),
            ]
        y_part(vy, ycol, tt, fy.at[k])
        sy = [
            send(fy.at[k, 0], ry.at[k, 1], at_y(-1)),
            send(fy.at[k, 1], ry.at[k, 0], at_y(1)),
        ]
        if k == 1:
            far[:] = [
                send(fx.at[k, 0], rx2.at[1, 1], at_x(-2)),
                send(fx.at[k, 1], rx2.at[0, 1], at_x(2)),
            ]
        rest = z_line(parts, zmat)
        if with_mass and k == 1:
            finish_penalty()
        if with_mass:
            rest = rest + pav[...] * vx[...]
        tt[...] += rest
        x_part(vx, mx, tt)
        if k == 2:
            gradient(1)
            mom[pl.ds(0, 1), :] = inner(vec.at[0], vec.at[0])
            mom[pl.ds(1, 1), :] = inner(vec.at[0], vec.at[1])
            mom[pl.ds(2, 1), :] = inner(vec.at[1], vec.at[1])
            mom[pl.ds(6, 2), :] = jnp.zeros((2, NZ), F32)
        for copy in sy:
            copy.wait_recv()
        add_y(
            tt,
            hy[0] * (ry[k, 0] - fy[k, 0]),
            hy[1] * (ry[k, 1] - fy[k, 1]),
        )
        for copy in sz:
            copy.wait_recv()
        add_z(tt, jnp.where(end_rows, 0.5 * (rz[k] - fz[k]), 0.0))
        out = vec.at[k]
        for x in range(1, NX - 1):
            out[x] = tt[x] * (sign * wm[x])
        if k == 1:
            @loop(4)
            def _(yt):
                rows = y_rows(yt)
                src = [tt[0, rows, :] * wm[0, rows, :]]
                src += [out[x, rows, :] for x in range(1, NX - 1)]
                src += [tt[NX - 1, rows, :] * wm[NX - 1, rows, :]]
                weight = wyz[rows, :]
                below = fx[1, 0, rows, :] * weight * (2.0 * scale_x[0] * hx[0])
                above = fx[1, 1, rows, :] * weight * (2.0 * scale_x[-1] * hx[1])
                q2[0, rows, :] = line(L[0], src[:-1] + [src[-1] - above])
                q2[1, rows, :] = line(L[NX - 1], [src[0] - below] + src[1:])

            far[2:] = [
                send(q2.at[0], rq2.at[1], at_x(-1)),
                send(q2.at[1], rq2.at[0], at_x(1)),
            ]
            gradient(0)
        if k == 2:
            for copy in far:
                copy.wait_recv()
            for side in (0, 1):
                mine, other = side * (NX - 1), (1 - side) * (NX - 1)
                near_term = (scale_x[other] * float(L[other, other])) * (
                    fx[1, side] - rx[1, side]
                )
                far_term = (2.0 * scale_x[mine] * float(L[other, mine])) * hx2[side]
                rx[2, side] = rq2[side] + wyz[...] * (
                    near_term + far_term * rx2[side, 1]
                )
        for copy in sx:
            copy.wait_recv()
        out[0] = (tt[0] + hx[0] * (rx[k, 0] - fx[k, 0])) * (sign * wm[0])
        out[NX - 1] = (tt[NX - 1] + hx[1] * (rx[k, 1] - fx[k, 1])) * (sign * wm[NX - 1])

    def finish_penalty():
        for copy in copies_p:
            copy.wait_recv()
        for side in (0, 1):
            neighbour_face(side, 3)
            own = xf[side, 3]
            pav[side * (NX - 1)] = own + hx[side] * (rmix[side, 3] - own)

    phase(0, adv.at[0], adv.at[1], adv.at[2], D, T_D, Z_DA, F_D, False, -1.0)
    for k in (1, 2):
        v = vec.at[k - 1]
        phase(k, v, v, v, L, T_L, Z_LA, F_L, True, 1.0)

    v0, v1, v2 = vec.at[0], vec.at[1], vec.at[2]
    y_part(v2, T_L, tt, None)
    tt[...] += z_line(split3(flat(vec[2])), Z_LA) + pav[...] * v2[...]
    x_part(v2, L, tt)
    total = None
    for yt in range(4):
        rows = pl.ds(8 * yt, 8)
        s = None
        for x in range(NX):
            p = v2[x, rows, :] * tt[x, rows, :] * scale_x[x]
            s = p if s is None else s + p
        total = s if total is None else total + s
    mom[pl.ds(5, 1), :] = jnp.sum(total * w_tile, axis=0, keepdims=True)
    mom[pl.ds(3, 1), :] = inner(v1, v2)
    mom[pl.ds(4, 1), :] = inner(v2, v2)

    def spread(source, slots, own, mates, which):
        slots[own] = source[...]
        for mate in mates:
            pltpu.make_async_remote_copy(
                src_ref=source,
                dst_ref=slots.at[own],
                send_sem=red_send.at[which],
                recv_sem=red_recv.at[which],
                device_id=mate,
                device_id_type=MESH,
            ).start()

    def wait_all(slots, semaphore):
        view = slots.at[pl.ds(0, 15)]
        pltpu.make_async_copy(view, view, semaphore).wait()

    def gather(slots, which):
        wait_all(slots, red_recv.at[which])
        total = slots[0]
        for k in range(1, 16):
            total = total + slots[k]
        return total

    spread(mom, red1, index2, mates2, 0)

    gradient(2)
    gradient_copies = [
        send(gfx.at[0], grx.at[1], at_x(-1)),
        send(gfx.at[1], grx.at[0], at_x(1)),
        send(gfz.at[pl.ds(0, 8)], grz.at[pl.ds(8, 8)], at_z(-1)),
        send(gfz.at[pl.ds(8, 8)], grz.at[pl.ds(0, 8)], at_z(1)),
        send(gfy.at[0], gry.at[1], at_y(-1)),
        send(gfy.at[1], gry.at[0], at_y(1)),
    ]
    part[...] = gather(red1, 0)
    spread(part, red2, index1, mates1, 1)
    for copy in gradient_copies:
        copy.wait_recv()
    gradient_edges()

    for copy in pending:
        copy.wait_send()
    wait_all(red1, red_send.at[0])
    sums = jnp.sum(gather(red2, 1), axis=1, keepdims=True)
    m = [jnp.broadcast_to(sums[k : k + 1, :], (8, NZ)) for k in range(6)]
    s0, s1, s2 = lax.rsqrt(m[1]), lax.rsqrt(m[3]), lax.rsqrt(m[5])
    h01 = m[2] * s0 * s1
    h02 = m[3] * s0 * s2
    h12 = m[4] * s1 * s2
    h00, h11, h22 = m[1] * s0 * s0, m[3] * s1 * s1, m[5] * s2 * s2
    g0, g1, g2 = m[0] * s0, m[1] * s1, m[2] * s2
    l10 = h01 / h00
    l20 = h02 / h00
    d1 = h11 - l10 * h01
    d1 = jnp.where(d1 > 1e-6, d1, 1e30)
    e1 = h12 - l20 * h01
    l21 = e1 / d1
    d2 = h22 - l20 * h02 - l21 * e1
    d2 = jnp.where(d2 > 1e-6, d2, 1e30)
    y0 = g0
    y1_ = g1 - l10 * y0
    y2_ = g2 - l20 * y0 - l21 * y1_
    c2 = y2_ / d2
    c1 = y1_ / d1 - l21 * c2
    c0 = y0 / h00 - l10 * c1 - l20 * c2
    c0, c1, c2 = c0 * s0, c1 * s1, c2 * s2

    c0, c1, c2 = c0[:1], c1[:1], c2[:1]
    outs = []
    for k in range(PIECES):
        slabs = pl.ds(k * (NX // PIECES), NX // PIECES)
        tt[slabs] = c0 * v0[slabs] + c1 * v1[slabs] + c2 * v2[slabs]
        outs.append(
            pltpu.make_async_copy(tt.at[slabs], pressure.at[slabs], out_sem.at[k, 0])
        )
        outs[-1].start()
        for i in range(3):
            res[i, slabs] = adv[i, slabs] - (
                c0 * grad[0, i, slabs] + c1 * grad[1, i, slabs] + c2 * grad[2, i, slabs]
            )
        outs.append(
            pltpu.make_async_copy(
                res.at[:, slabs], projected.at[:, slabs], out_sem.at[k, 1]
            )
        )
        outs[-1].start()
    wait_all(red2, red_send.at[1])
    for copy in outs:
        copy.wait()


def hand_on(projected_in, pressure_in, projected, pressure, proj, pres, load_sem, sem):
    loads, outs = [], []
    for k in range(PIECES):
        slabs = pl.ds(k * (NX // PIECES), NX // PIECES)
        for i, (source, held, target) in enumerate(
            [
                (projected_in.at[:, slabs], proj.at[:, slabs], projected.at[:, slabs]),
                (pressure_in.at[slabs], pres.at[slabs], pressure.at[slabs]),
            ]
        ):
            loads.append(pltpu.make_async_copy(source, held, load_sem.at[k, i]))
            outs.append(pltpu.make_async_copy(held, target, sem.at[k, i]))
    for copy in loads:
        copy.start()
    for load, out in zip(loads, outs):
        load.wait()
        out.start()
    for copy in outs:
        copy.wait()


def per_device(base_flow, adjoint_velocity, penalty):
    field = (NX, NY, NZ)
    v = lambda *shape: pltpu.VMEM(shape, F32)
    consts = [jnp.asarray(t) for t in tables()]
    any_spec = pl.BlockSpec(memory_space=pltpu.HBM)
    sends = 60
    shapes = (
        jax.ShapeDtypeStruct((3,) + field, F32),
        jax.ShapeDtypeStruct(field, F32),
    )
    results = pl.pallas_call(
        kernel,
        out_shape=shapes,
        in_specs=[any_spec] * 6,
        out_specs=(any_spec,) * 2,
        scratch_shapes=[
            v(3, *field),
            v(3, *field),
            v(*field),
            pltpu.VMEM(consts[0].shape, jnp.bfloat16),
            pltpu.VMEM(consts[1].shape, jnp.bfloat16),
            v(*consts[2].shape),
            v(4, *field),
            v(4, *field),
            v(3, *field),
            v(*field),
            v(3, *field),
            v(*field),
            v(3, 3, *field),
            v(*field),
            v(NY, NZ),
            v(2, NY, NZ),
            v(2, NY, NZ),
            v(16, ROWS),
            v(2, 3, 8, ROWS),
            v(2, 4, 8, NZ),
            v(2, 4, 8, NZ),
            v(2, 4, NY, NZ),
            v(2, NY + 16, NZ),
            v(2, 4, NY, NZ),
            v(2, NY + 16, NZ),
            v(2, 2, NY, NZ),
            v(2, 4, NY, NZ),
            v(2, 4, NY, NZ),
            v(3, 2, NY, NZ),
            v(3, 2, NY, NZ),
            v(3, 2, 8, NZ),
            v(3, 2, 8, NZ),
            v(3, 16, ROWS),
            v(3, 16, ROWS),
            v(2, 3, NY, NZ),
            v(2, 3, NY, NZ),
            v(2, 3, 8, NZ),
            v(2, 3, 8, NZ),
            v(16, ROWS),
            v(16, ROWS),
            v(8, NZ),
            v(16, 8, NZ),
            v(8, NZ),
            v(16, 8, NZ),
            v(3, *field),
            pltpu.SemaphoreType.DMA((7,)),
            pltpu.SemaphoreType.DMA((sends + 10,)),
            pltpu.SemaphoreType.DMA((sends + 10,)),
            pltpu.SemaphoreType.DMA((2,)),
            pltpu.SemaphoreType.DMA((2,)),
            pltpu.SemaphoreType.DMA((PIECES, 2)),
        ],
        compiler_params=pltpu.CompilerParams(
            collective_id=0, has_side_effects=True, vmem_limit_bytes=63 * 1024 * 1024
        ),
        name="adjoint",
    )(base_flow, adjoint_velocity, penalty, *consts)
    return pl.pallas_call(
        hand_on,
        out_shape=shapes,
        in_specs=[any_spec] * 2,
        out_specs=(any_spec,) * 2,
        scratch_shapes=[
            v(3, *field),
            v(*field),
            pltpu.SemaphoreType.DMA((PIECES, 2)),
            pltpu.SemaphoreType.DMA((PIECES, 2)),
        ],
        compiler_params=pltpu.CompilerParams(vmem_limit_bytes=63 * 1024 * 1024),
        name="hand_on",
    )(*results)


def solution(mesh):
    spec3 = P(None, "gx", "gy", "gz")
    spec1 = P("gx", "gy", "gz")
    return jax.shard_map(
        per_device,
        mesh=mesh,
        in_specs=(spec3, spec3, spec1),
        out_specs=(spec3, spec1),
        check_vma=False,
    )
```
